32 devices in a mesh: grp: 2 (over x), feed: 16 (over z, y, core).
Axes of the slice: x: 2, y: 2, z: 4, core: 2. Of those that a mesh axis runs over, the one named last changes fastest.
Arguments:
- samples: bfloat16 [512, 102, 8192], P('feed', 'grp'), parts along dimension 1, may hold values from -24 to 24
- fir_taps: float32 [4, 8192], replicated, may hold values from -3 to 3
- owner_map: int32 [256, 1], replicated, may hold values from 0 to 15; in each aligned block of 256 rows (0 to 255, 256 to 511, ...) at most 24 rows name the same one
- dropped_channels: int32 [64], P('grp'), parts along dimension 0, may hold values from 0 to 255
Outputs:
- visibilities: bfloat16 [768, 2, 512, 512], P(('grp', 'feed')), parts along dimension 0
The draws below stay inside these ranges and needn't reach their ends.
There are 2 independent parts, one for each index of `grp`. The reference program is written for one: setup_inputs(seed, part) draws one part's arguments, and reference() takes and returns one part's arrays. A program takes and returns all parts, laid end to end along the dimension named above; an argument that names none is the same for every part. Nothing has to cross between parts.
Inputs may be any that keep to these rules, and one draw needn't show every extreme that they name: `owner_map`: no more than 24 channels share an owner, and some owner has exactly 24.
All inputs are finite; a program needn't handle non-finite values.
Results may differ from the reference program's by a relative error of at most 0.001.
Values sent between devices are 32-bit elements; how exact they have to be, the bound alone decides.
No kernel may reach another device: no remote copies, remote signals or barrier semaphores. Data moves between devices by JAX's collectives and lax.ppermute only.
A program may use at most 384 MiB of HBM per device.

```python
import math
import jax
import jax.numpy as jnp
import numpy as np
from jax import lax

NIN = 512
NFFT = 8192
BAND = 256
BAND_START = 1536
TAPS = 4
SPEC = 48
DROP = 32
FRAMES = 51
CAP = 24
N_FEED = 16


def draw_samples(key, part):
    key = jax.random.fold_in(key, 11)
    noise_key, level_key = jax.random.split(key)
    position = jnp.arange(NIN, dtype=jnp.float32) / max(NIN - 1, 1)
    roughness = jnp.exp(jax.random.uniform(level_key, (NIN,), minval=-0.35, maxval=0.35))
    level = 10.0 ** (0.5 * position) * roughness
    noise = jax.random.normal(noise_key, (NIN, FRAMES, NFFT))
    values = jnp.clip(noise * level[:, None, None], -24.0, 24.0)
    return values.astype(jnp.bfloat16)


def plant(entries, stream_key, low, high):
    longest = entries.shape.index(max(entries.shape))
    spots = []
    for shift in (0, 1):
        where = [jax.random.randint(jax.random.fold_in(stream_key, axis), (), 0, length) for axis, length in enumerate(entries.shape)]
        where[longest] = (where[longest] + shift) % entries.shape[longest]
        spots.append(tuple(where))
    return entries.at[spots[0]].set(low).at[spots[1]].set(high)


def routed_block(rng, own, number, rows, count, top, bound, slope):
    ranking = jax.random.permutation(rng, count)
    packed, usual = shares(count, rows * top, bound, slope, True), shares(count, rows * top, bound, slope, False)
    places = jnp.arange(count)

    def named(sizes, turn):
        used = int((sizes > 0).sum())
        fixed = max(1, used // 4)
        passed = fixed + (places - fixed + turn * (used - fixed)) % max(1, count - fixed)
        return jnp.zeros((count,), jnp.int32).at[ranking[jnp.where(places < fixed, places, passed)]].set(jnp.asarray(sizes, jnp.int32))

    sizes = jnp.where(number % 4 == 0, named(packed, number // 4), named(usual, number - number // 4 - 1))
    mixed = jax.random.permutation(jax.random.fold_in(own, 3), count)
    source_of, sink = mixed[0:count // 2 * 2:2], mixed[1:count // 2 * 2:2]
    margin = jnp.minimum(sizes[source_of] - 1, bound - sizes[sink]) // 2
    margin = jnp.where((source_of == ranking[0]) | (sink == ranking[0]) | (sizes[sink] == 0), 0, jnp.maximum(margin, 0))
    passed = jax.random.randint(jax.random.fold_in(own, 4), (count // 2,), 0, 1 << 20) % (margin + 1)
    sizes = sizes.at[source_of].add(-passed).at[sink].add(passed)
    items = jnp.searchsorted(jnp.cumsum(sizes), jnp.arange(rows * top), side="right").astype(jnp.int32)
    table = items.reshape(top, rows).T
    table = table[jax.random.permutation(jax.random.fold_in(own, 1), rows)]
    turn = jax.random.randint(jax.random.fold_in(own, 2), (rows, 1), 0, top)
    return jnp.take_along_axis(table, (jnp.arange(top)[None, :] + turn) % top, axis=1)


def shares(count, total, limit, lean, full):
    portions = [(1 << 20) // math.isqrt(rank ** lean) + 1 for rank in range(1, count + 1)]
    largest = limit if full else min(limit, max(-(-total // count), total * portions[0] // sum(portions)))
    least = 1 if total - largest >= count - 1 else 0
    given, surplus = [largest] + [least] * (count - 1), total - largest - least * (count - 1)
    while surplus > 0:
        candidates = [i for i in range(1, count) if given[i] < largest] or [i for i in range(1, count) if given[i] < limit]
        whole, budget = sum([portions[i] for i in candidates]), surplus
        for i in candidates:
            more = min(limit - given[i], max(1, budget * portions[i] // whole), surplus)
            given[i] = given[i] + more
            surplus = surplus - more
    return np.array(given)


def normal_values(own_key, extent, scale, most, kind=jnp.bfloat16):
    return jnp.clip(scale * jax.random.normal(own_key, extent, jnp.float32), -most, most).astype(kind)


def setup_inputs(seed: int = 0, part: int = 0) -> dict:
    key_list = jax.random.split(jax.random.key(seed), 5)
    own_keys = jax.random.split(jax.random.fold_in(key_list[4], part), 5)
    samples = draw_samples(jax.random.fold_in(jax.random.fold_in(key_list[4], part), 71), part)
    fir_taps = normal_values(key_list[1], (TAPS, NFFT), 0.5, 3.0, jnp.float32)
    owner_map_keys = jax.random.split(jax.random.fold_in(key_list[2], 1), BAND // BAND)
    owner_map_turns = jax.random.permutation(jax.random.fold_in(key_list[2], 3), BAND // BAND)
    owner_map = jax.vmap(lambda own, number: routed_block(jax.random.fold_in(key_list[2], 2), own, number, BAND, N_FEED, 1, CAP, 2))(owner_map_keys, owner_map_turns).reshape((BAND, 1))
    dropped_channels = plant(jax.random.randint(own_keys[3], (DROP,), 0, BAND), jax.random.fold_in(own_keys[3], 1), 0, BAND - 1).astype(jnp.int32)
    return {"samples": samples, "fir_taps": fir_taps, "owner_map": owner_map, "dropped_channels": dropped_channels}


def slot_tables(owner_map, dropped_channels, capacity, slot_total):
    owners = owner_map[:, 0]
    channels = jnp.arange(owners.shape[0], dtype=jnp.int32)
    same_owner = (owners[:, None] == owners[None, :]) & (channels[None, :] < channels[:, None])
    rank_in = lax.optimization_barrier(jnp.sum(same_owner.astype(jnp.int32), axis=1))
    slot_of = owners * capacity + rank_in
    flagged = jnp.any(dropped_channels[:, None] == channels[None, :], axis=0)
    channel_live = jnp.logical_not(flagged)
    targets = jnp.arange(slot_total, dtype=jnp.int32)
    slot_hit = (slot_of[:, None] == targets[None, :]) & channel_live[:, None]
    chan_of = lax.optimization_barrier(jnp.sum(slot_hit.astype(jnp.int32) * channels[:, None], axis=0)).astype(jnp.int32)
    slot_used = jnp.any(slot_hit, axis=0)
    return (chan_of, slot_used, channel_live)

def window(block, fir_taps):
    taps = fir_taps.shape[0]
    spec_count = block.shape[1] - taps + 1
    summed = jnp.zeros((block.shape[0], spec_count, block.shape[2]), jnp.float32)
    for tap_index in range(taps):
        summed = summed + fir_taps[tap_index][None, None, :] * block[:, tap_index:tap_index + spec_count, :].astype(jnp.float32)
    return summed

def reference(samples, fir_taps, owner_map, dropped_channels):
    capacity = BAND // N_FEED + BAND // (2 * N_FEED)
    slot_total = N_FEED * capacity
    dft_scale = 1.0 / math.sqrt(NFFT)

    def transform(block):
        windowed = window(block, fir_taps)
        spectrum = jnp.fft.rfft(windowed, axis=-1)[:, :, BAND_START:BAND_START + BAND]
        return jnp.stack([jnp.real(spectrum) * dft_scale, jnp.imag(spectrum) * dft_scale], axis=2)
    blocks = samples.reshape(NIN // 64, 64, FRAMES, NFFT)
    spectra = lax.map(transform, blocks).reshape(NIN, SPEC, 2, BAND)
    chan_of, slot_used, channel_live = slot_tables(owner_map, dropped_channels, capacity, slot_total)
    live_mask = channel_live.astype(jnp.float32)
    power = jnp.sum(spectra * spectra * live_mask[None, None, None, :])
    kept = jnp.sum(live_mask)
    mean_power = power / (NIN * SPEC * kept)
    factor = 1.0 / (SPEC * mean_power)
    chosen = jnp.take(spectra, chan_of, axis=3) * slot_used.astype(jnp.float32)[None, None, None, :]
    stacked = jnp.transpose(chosen, (3, 2, 1, 0)).reshape(slot_total, 2 * SPEC, NIN)

    def one_slot(columns):
        real_rows = columns[:SPEC]
        imag_rows = columns[SPEC:]
        rotated = jnp.concatenate([imag_rows, -real_rows], axis=0)
        real_vis = jnp.dot(columns.T, columns, precision=lax.Precision.HIGHEST, preferred_element_type=jnp.float32)
        imag_vis = jnp.dot(rotated.T, columns, precision=lax.Precision.HIGHEST, preferred_element_type=jnp.float32)
        return (jnp.stack([real_vis, imag_vis], axis=0) * factor).astype(jnp.bfloat16)
    return lax.map(one_slot, stacked)
```

```python
import functools
import math

import jax
import jax.numpy as jnp
import ml_dtypes
import numpy as np
from jax import lax
from jax.experimental import pallas as pl
from jax.experimental.pallas import tpu as pltpu
from jax.sharding import PartitionSpec as P

NIN = 512
NFFT = 8192
HALF = NFFT // 2
BAND = 256
BAND_START = 1536
SPEC = 48
GROUP = 16
NB = 256
LANES = 128
MIB = 1 << 20


def dft_table(length, first, width):
    row_ids = lax.broadcasted_iota(jnp.int32, (length, width), 0)
    chan_ids = first + lax.broadcasted_iota(jnp.int32, (length, width), 1)
    phase_int = row_ids * chan_ids % length
    angles = phase_int.astype(jnp.float32) * (2.0 * math.pi / length)
    return jnp.concatenate([jnp.cos(angles), -jnp.sin(angles)], axis=1)


def folded_table():
    n = np.arange(HALF, dtype=np.int64)
    tables = []
    for parity in range(2):
        chans = BAND_START + 2 * np.arange(BAND // 2, dtype=np.int64) + parity
        angles = (chans[:, None] * n[None, :] % NFFT) * (2.0 * math.pi / NFFT)
        full = np.concatenate([np.cos(angles), -np.sin(angles)], axis=0) / math.sqrt(NFFT)
        high = full.astype(np.float32).astype(ml_dtypes.bfloat16)
        low = (full - high.astype(np.float64)).astype(np.float32).astype(ml_dtypes.bfloat16)
        tables += [high, low]
    return np.stack(tables)


def slot_tables(owner_map, dropped_channels, capacity, slot_total):
    owners = owner_map[:, 0]
    channels = jnp.arange(owners.shape[0], dtype=jnp.int32)
    same_owner = (owners[:, None] == owners[None, :]) & (channels[None, :] < channels[:, None])
    rank_in = jnp.sum(same_owner.astype(jnp.int32), axis=1)
    slot_of = owners * capacity + rank_in
    flagged = jnp.any(dropped_channels[:, None] == channels[None, :], axis=0)
    channel_live = jnp.logical_not(flagged)
    targets = jnp.arange(slot_total, dtype=jnp.int32)
    slot_hit = (slot_of[:, None] == targets[None, :]) & channel_live[:, None]
    chan_of = jnp.sum(slot_hit.astype(jnp.int32) * channels[:, None], axis=0)
    slot_used = jnp.any(slot_hit, axis=0)
    return (chan_of, slot_used, channel_live)


def window(block, fir_taps):
    taps = fir_taps.shape[0]
    spec_count = block.shape[1] - taps + 1
    summed = jnp.zeros((block.shape[0], spec_count, block.shape[2]), jnp.float32)
    for tap_index in range(taps):
        summed = summed + fir_taps[tap_index][None, None, :] * block[
            :, tap_index : tap_index + spec_count, :
        ].astype(jnp.float32)
    return summed


def pair_products(left, right):
    return jnp.einsum(
        "qis,qjs->qij",
        left,
        right,
        precision=lax.Precision.HIGHEST,
        preferred_element_type=jnp.float32,
    )


def correlate(received):
    columns = received[0]
    real_rows = columns[:, :, :SPEC]
    imag_rows = columns[:, :, SPEC:]
    rotated = jnp.concatenate([imag_rows, -real_rows], axis=2)
    real_vis = pair_products(columns, columns)
    imag_vis = pair_products(rotated, columns)
    return jnp.stack([real_vis, imag_vis], axis=1)


def local_plain(samples, fir_taps, owner_map, dropped_channels):
    devices = lax.axis_size("feed")
    capacity = BAND // devices + BAND // (2 * devices)
    slot_total = devices * capacity
    in_local = samples.shape[0]
    dft_scale = 1.0 / math.sqrt(NFFT)
    chan_of, slot_used, channel_live = slot_tables(
        owner_map, dropped_channels, capacity, slot_total
    )
    live_mask = channel_live.astype(jnp.float32)
    kept = jnp.sum(live_mask)
    windowed = window(samples, fir_taps).reshape(in_local * SPEC, NFFT)
    table = dft_table(NFFT, BAND_START, BAND)
    spectra = (
        jnp.dot(
            windowed, table, precision=lax.Precision.HIGHEST, preferred_element_type=jnp.float32
        )
        * dft_scale
    )
    spectra = spectra.reshape(in_local, SPEC, 2, BAND)
    chosen = jnp.take(spectra, chan_of, axis=3) * slot_used.astype(jnp.float32)[None, None, None, :]
    outgoing = jnp.transpose(chosen, (3, 0, 2, 1)).reshape(devices, capacity, in_local, 2 * SPEC)
    raw_vis = correlate(lax.all_to_all(outgoing, "feed", split_axis=0, concat_axis=2, tiled=True))
    local_power = jnp.sum(jnp.trace(raw_vis[:, 0], axis1=1, axis2=2))
    power = lax.psum(local_power, "feed")
    mean_power = power / (NIN * SPEC * kept)
    factor = 1.0 / (SPEC * mean_power)
    return (raw_vis * factor).astype(jnp.bfloat16)


def split(value):
    high = value.astype(jnp.bfloat16)
    return high, (value - high.astype(jnp.float32)).astype(jnp.bfloat16)


def contract_last(left, right):
    return lax.dot_general(
        left, right, (((1,), (1,)), ((), ())), preferred_element_type=jnp.float32
    )


def spectra_kernel(parts, carry_in, capacity, taps, in_local, *refs):
    slot_ref, live_ref, taps_a, taps_b, main_a, halo_a, main_b, halo_b, table = refs[:9]
    refs = refs[9:]
    before, refs = refs[:carry_in], refs[carry_in:]
    outs, refs = refs[: len(parts)], refs[len(parts) :]
    power_out, frames, even_h, even_l, odd_h, odd_l, acc, flat = refs
    step = pl.program_id(0)
    tiles = NB // LANES

    for half, (main, halo) in enumerate(((main_a, halo_a), (main_b, halo_b))):
        for tile in range(tiles):
            lanes = slice(tile * LANES, (tile + 1) * LANES)
            for i in range(in_local):
                frames[half, tile, pl.ds(i, GROUP, stride=in_local), :] = main[i, :, lanes].astype(
                    jnp.float32
                )
                tail = halo[i, :, lanes].astype(jnp.float32)[:8]
                frames[half, tile, pl.ds(GROUP * in_local + i, 8, stride=in_local), :] = tail

    for tile in range(tiles):
        lanes = slice(tile * LANES, (tile + 1) * LANES)
        coef_a = [taps_a[t : t + 1, lanes] for t in range(taps)]
        coef_b = [taps_b[t : t + 1, lanes] for t in range(taps)]
        for first in range(0, in_local, 16):

            def load(half, f):
                return frames[half, tile, pl.ds(f * in_local + first, 16), :]

            held_a = [load(0, f) for f in range(taps - 1)]
            held_b = [load(1, f) for f in range(taps - 1)]
            for s in range(GROUP):
                held_a.append(load(0, s + taps - 1))
                held_b.append(load(1, s + taps - 1))
                low_half = sum(coef_a[t] * held_a[t] for t in range(1, taps)) + coef_a[0] * held_a[0]
                high_half = sum(coef_b[t] * held_b[t] for t in range(1, taps)) + coef_b[0] * held_b[0]
                rows = slice(s * in_local + first, s * in_local + first + 16)
                even_h[rows, lanes], even_l[rows, lanes] = split(low_half + high_half)
                odd_h[rows, lanes], odd_l[rows, lanes] = split(low_half - high_half)
                held_a, held_b = held_a[1:], held_b[1:]

    for parity, (high, low) in enumerate(((even_h, even_l), (odd_h, odd_l))):
        total = contract_last(table[2 * parity], high[...])
        total += contract_last(table[2 * parity + 1], high[...])
        total += contract_last(table[2 * parity], low[...])
        rows = slice(parity * BAND, (parity + 1) * BAND)

        @pl.when(step == 0)
        def _():
            acc[rows, :] = total

        @pl.when(step > 0)
        def _():
            acc[rows, :] += total

    @pl.when(step == pl.num_programs(0) - 1)
    def _():
        width = GROUP * in_local // LANES
        for parity in range(2):
            for part in range(2):
                for block in range(BAND // 16):
                    for g in range(width):
                        start = parity * BAND + part * (BAND // 2) + block * 8
                        value = acc[start : start + 8, g * LANES : (g + 1) * LANES]
                        row = block * 128 + parity * 8 + part * width + g
                        flat[pl.ds(row, 8, stride=16), :] = value

        def place(c, total):
            value = flat[pl.ds(pl.multiple_of(c * 8, 8), 8), :]
            slot = slot_ref[c]
            dest, rank = lax.div(slot, capacity), lax.rem(slot, capacity)
            for out, (low, high, extra) in zip(outs, parts):

                @pl.when((rank >= low) & (rank < high))
                def _(out=out, low=low):
                    out[dest, rank - low] = value

            weight = live_ref[c].astype(jnp.float32)
            return total + weight * (value * value)

        total = lax.fori_loop(0, BAND, place, jnp.zeros((8, LANES), jnp.float32), unroll=8)
        for ref in before:
            total = total + ref[...]
        power_out[...] = total
        for out, (low, high, extra) in zip(outs, parts):
            if extra:
                for d in range(out.shape[0]):
                    out[d, high - low] = total


def spectra_call(group, parts, before, table, slot_of, live, fir_taps, samples, devices, capacity):
    in_local, _, _ = samples.shape
    taps = fir_taps.shape[0]
    steps = HALF // NB
    far = HALF // NB

    def frames_spec(offset, block):
        return pl.BlockSpec((in_local, GROUP, NB), lambda j, *_: (0, block, j + offset))

    def taps_spec(offset):
        return pl.BlockSpec((taps, NB), lambda j, *_: (0, j + offset))

    rows = GROUP * in_local
    width = 2 * rows // LANES
    shapes = [
        jax.ShapeDtypeStruct((devices, high - low + extra, width, LANES), jnp.float32)
        for low, high, extra in parts
    ]
    shapes.append(jax.ShapeDtypeStruct((8, LANES), jnp.float32))
    grid_spec = pltpu.PrefetchScalarGridSpec(
        num_scalar_prefetch=2,
        grid=(steps,),
        in_specs=[
            taps_spec(0),
            taps_spec(far),
            frames_spec(0, group),
            frames_spec(0, group + 1),
            frames_spec(far, group),
            frames_spec(far, group + 1),
            pl.BlockSpec((4, BAND, NB), lambda j, *_: (0, 0, j)),
        ]
        + [pl.BlockSpec((8, LANES), lambda j, *_: (0, 0))] * len(before),
        out_specs=[pl.BlockSpec(s.shape, lambda j, *_, n=len(s.shape): (0,) * n) for s in shapes],
        scratch_shapes=[
            pltpu.VMEM((2, NB // LANES, (GROUP + 8) * in_local, LANES), jnp.float32),
            pltpu.VMEM((rows, NB), jnp.bfloat16),
            pltpu.VMEM((rows, NB), jnp.bfloat16),
            pltpu.VMEM((rows, NB), jnp.bfloat16),
            pltpu.VMEM((rows, NB), jnp.bfloat16),
            pltpu.VMEM((2 * BAND, rows), jnp.float32),
            pltpu.VMEM((BAND * 8, LANES), jnp.float32),
        ],
    )
    return pl.pallas_call(
        functools.partial(spectra_kernel, parts, len(before), capacity, taps, in_local),
        out_shape=shapes,
        grid_spec=grid_spec,
        compiler_params=pltpu.CompilerParams(vmem_limit_bytes=40 * MIB),
        cost_estimate=pl.CostEstimate(
            flops=3 * 2 * rows * HALF * 2 * BAND, bytes_accessed=30 * MIB, transcendentals=0
        ),
        name="spectra",
    )(
        slot_of,
        live,
        fir_taps,
        fir_taps,
        samples,
        samples,
        samples,
        samples,
        table,
        *before,
    )


def exchange_lanes(values, in_local):
    count = len(values)
    lane = lax.broadcasted_iota(jnp.int32, values[0].shape, 1) // in_local
    values = list(values)
    distance = count // 2
    while distance:
        upper = (lane & distance) != 0
        shift = distance * in_local
        for a in range(count):
            if a & distance:
                continue
            x, y = values[a], values[a + distance]
            values[a] = jnp.where(upper, pltpu.roll(y, shift, 1), x)
            values[a + distance] = jnp.where(upper, y, pltpu.roll(x, LANES - shift, 1))
        distance //= 2
    return values


def correlate_kernel(counts, in_local, *refs):
    used_ref, factor_ref = refs[:2]
    groups = refs[2 : 2 + counts]
    out, left_real, left_imag, right_a, right_b = refs[-5:]
    slot = pl.program_id(0)
    used = used_ref[slot] != 0
    per_tile = LANES // in_local
    sources = groups[0].shape[0]
    row_tiles = per_tile * counts

    @pl.when(used)
    def _():
        factor = factor_ref[0]
        upper = lax.broadcasted_iota(jnp.int32, (8, LANES), 0) >= 4
        for block in range(sources // per_tile):
            lanes = slice(block * LANES, (block + 1) * LANES)
            tiles = [None] * row_tiles
            for g, ref in enumerate(groups):
                mixed = [ref[block * per_tile + a, 0] for a in range(per_tile)]
                for q, value in enumerate(exchange_lanes(mixed, in_local)):
                    tiles[q * counts + g] = value
            turned = [jnp.where(upper, -1.0, 1.0) * pltpu.roll(t, 4, 0) for t in tiles]
            pad = [jnp.zeros((LANES - 8 * row_tiles, LANES), jnp.float32)]
            columns = jnp.concatenate(tiles + pad, axis=0)
            rotated = jnp.concatenate(turned + pad, axis=0)
            high, low = split(columns)
            right_a[:LANES, lanes] = high
            right_a[LANES:, lanes] = high
            right_b[:, lanes] = low
            high, low = split(columns.T)
            left_real[lanes, :LANES] = high
            left_real[lanes, LANES:] = low
            high, low = split(rotated.T)
            left_imag[lanes, :LANES] = high
            left_imag[lanes, LANES:] = low
        for part, left in enumerate((left_real, left_imag)):
            for block in range(sources // per_tile):
                rows = slice(block * LANES, (block + 1) * LANES)
                total = jnp.dot(left[rows, :], right_a[...], preferred_element_type=jnp.float32)
                total += jnp.dot(
                    left[rows, :LANES], right_b[...], preferred_element_type=jnp.float32
                )
                out[0, part, rows, :] = (total * factor).astype(jnp.bfloat16)

    @pl.when(jnp.logical_not(used))
    def _():
        out[...] = jnp.zeros_like(out)


def correlate_call(received, low, high, capacity, used, factor, total, in_local):
    arrays = [r for r, _ in received]
    sources = arrays[0].shape[0]
    nin = sources * in_local
    width = arrays[0].shape[2]
    aliases = {}
    extra, extra_specs = [], []
    if total is not None:
        extra, extra_specs = [total], [pl.BlockSpec(memory_space=pl.ANY)]
        aliases = {2 + len(arrays): 0}
    in_specs = [
        pl.BlockSpec(memory_space=pltpu.SMEM),
        pl.BlockSpec(memory_space=pltpu.SMEM),
    ] + [
        pl.BlockSpec((sources, 1, width, LANES), lambda s, d=low - first: (0, s + d, 0, 0))
        for _, first in received
    ]
    return pl.pallas_call(
        functools.partial(correlate_kernel, len(arrays), in_local),
        out_shape=jax.ShapeDtypeStruct((capacity, 2, nin, nin), jnp.bfloat16),
        grid=(high - low,),
        in_specs=in_specs + extra_specs,
        out_specs=pl.BlockSpec((1, 2, nin, nin), lambda s: (s + low, 0, 0, 0)),
        scratch_shapes=[
            pltpu.VMEM((nin, 2 * LANES), jnp.bfloat16),
            pltpu.VMEM((nin, 2 * LANES), jnp.bfloat16),
            pltpu.VMEM((2 * LANES, nin), jnp.bfloat16),
            pltpu.VMEM((LANES, nin), jnp.bfloat16),
        ],
        input_output_aliases=aliases,
        compiler_params=pltpu.CompilerParams(vmem_limit_bytes=40 * MIB),
        cost_estimate=pl.CostEstimate(
            flops=(high - low) * 8 * nin * nin * 256,
            bytes_accessed=(high - low) * (4 * nin * nin + 8 * nin * SPEC),
            transcendentals=0,
        ),
        name="correlate",
    )(used[low:high], factor, *arrays, *extra)


def local_blocks(samples, fir_taps, owner_map, dropped_channels):
    devices = lax.axis_size("feed")
    capacity = BAND // devices + BAND // (2 * devices)
    in_local = samples.shape[0]
    owners = owner_map[:, 0]
    channels = jnp.arange(BAND, dtype=jnp.int32)
    same_owner = (owners[:, None] == owners[None, :]) & (channels[None, :] < channels[:, None])
    slot_of = owners * capacity + jnp.sum(same_owner.astype(jnp.int32), axis=1)
    live = jnp.logical_not(jnp.any(dropped_channels[None, :] == channels[:, None], axis=1))
    kept = jnp.sum(live.astype(jnp.float32))
    mine = lax.axis_index("feed") * capacity + jnp.arange(capacity, dtype=jnp.int32)
    used = jnp.any((slot_of[None, :] == mine[:, None]) & live[None, :], axis=1).astype(jnp.int32)

    table = jnp.asarray(folded_table())
    groups = SPEC // GROUP
    middle = capacity // 2
    received, powers = [], []
    for group in range(groups):
        if group < groups - 1:
            parts = ((0, capacity, 0),)
        else:
            parts = ((0, middle, 1), (middle, capacity, 0))
        *blocks, power = spectra_call(
            group,
            parts,
            powers[-1:],
            table,
            slot_of,
            live.astype(jnp.int32),
            fir_taps,
            samples,
            devices,
            capacity,
        )
        powers.append(power)
        received.append(
            [
                lax.all_to_all(block, "feed", split_axis=0, concat_axis=0, tiled=True)
                for block in blocks
            ]
        )
    power = jnp.sum(received[-1][0][:, middle])
    mean_power = power / (NIN * SPEC * kept)
    factor = jnp.reshape(1.0 / (SPEC * mean_power), (1,))
    full = [(blocks[0], 0) for blocks in received[:-1]]
    first = correlate_call(
        full + [(received[-1][0], 0)], 0, middle, capacity, used, factor, None, in_local
    )
    return correlate_call(
        full + [(received[-1][1], middle)], middle, capacity, capacity, used, factor, first, in_local
    )


def solution(mesh):
    in_local = NIN // mesh.shape["feed"]
    blocks = in_local * 4 == LANES
    return jax.shard_map(
        local_blocks if blocks else local_plain,
        mesh=mesh,
        in_specs=(P("feed", "grp", None), P(), P(), P("grp")),
        out_specs=P(("grp", "feed"), None, None, None),
        check_vma=False,
    )
```

```python
import functools
import math

import jax
import jax.numpy as jnp
import ml_dtypes
import numpy as np
from jax import lax
from jax.experimental import pallas as pl
from jax.experimental.pallas import tpu as pltpu
from jax.sharding import PartitionSpec as P

NIN = 512
NFFT = 8192
HALF = NFFT // 2
BAND = 256
BAND_START = 1536
SPEC = 48
GROUP = 16
NB = 256
LANES = 128
MIB = 1 << 20


def dft_table(length, first, width):
    row_ids = lax.broadcasted_iota(jnp.int32, (length, width), 0)
    chan_ids = first + lax.broadcasted_iota(jnp.int32, (length, width), 1)
    phase_int = row_ids * chan_ids % length
    angles = phase_int.astype(jnp.float32) * (2.0 * math.pi / length)
    return jnp.concatenate([jnp.cos(angles), -jnp.sin(angles)], axis=1)


def folded_table():
    n = np.arange(HALF, dtype=np.int64)
    tables = []
    for parity in range(2):
        chans = BAND_START + 2 * np.arange(BAND // 2, dtype=np.int64) + parity
        angles = (chans[:, None] * n[None, :] % NFFT) * (2.0 * math.pi / NFFT)
        full = np.concatenate([np.cos(angles), -np.sin(angles)], axis=0) / math.sqrt(NFFT)
        high = full.astype(np.float32).astype(ml_dtypes.bfloat16)
        low = (full - high.astype(np.float64)).astype(np.float32).astype(ml_dtypes.bfloat16)
        tables += [high, low]
    return np.stack(tables)


def slot_tables(owner_map, dropped_channels, capacity, slot_total):
    owners = owner_map[:, 0]
    channels = jnp.arange(owners.shape[0], dtype=jnp.int32)
    same_owner = (owners[:, None] == owners[None, :]) & (channels[None, :] < channels[:, None])
    rank_in = jnp.sum(same_owner.astype(jnp.int32), axis=1)
    slot_of = owners * capacity + rank_in
    flagged = jnp.any(dropped_channels[:, None] == channels[None, :], axis=0)
    channel_live = jnp.logical_not(flagged)
    targets = jnp.arange(slot_total, dtype=jnp.int32)
    slot_hit = (slot_of[:, None] == targets[None, :]) & channel_live[:, None]
    chan_of = jnp.sum(slot_hit.astype(jnp.int32) * channels[:, None], axis=0)
    slot_used = jnp.any(slot_hit, axis=0)
    return (chan_of, slot_used, channel_live)


def window(block, fir_taps):
    taps = fir_taps.shape[0]
    spec_count = block.shape[1] - taps + 1
    summed = jnp.zeros((block.shape[0], spec_count, block.shape[2]), jnp.float32)
    for tap_index in range(taps):
        summed = summed + fir_taps[tap_index][None, None, :] * block[
            :, tap_index : tap_index + spec_count, :
        ].astype(jnp.float32)
    return summed


def pair_products(left, right):
    return jnp.einsum(
        "qis,qjs->qij",
        left,
        right,
        precision=lax.Precision.HIGHEST,
        preferred_element_type=jnp.float32,
    )


def correlate(received):
    columns = received[0]
    real_rows = columns[:, :, :SPEC]
    imag_rows = columns[:, :, SPEC:]
    rotated = jnp.concatenate([imag_rows, -real_rows], axis=2)
    real_vis = pair_products(columns, columns)
    imag_vis = pair_products(rotated, columns)
    return jnp.stack([real_vis, imag_vis], axis=1)


def local_plain(samples, fir_taps, owner_map, dropped_channels):
    devices = lax.axis_size("feed")
    capacity = BAND // devices + BAND // (2 * devices)
    slot_total = devices * capacity
    in_local = samples.shape[0]
    dft_scale = 1.0 / math.sqrt(NFFT)
    chan_of, slot_used, channel_live = slot_tables(
        owner_map, dropped_channels, capacity, slot_total
    )
    live_mask = channel_live.astype(jnp.float32)
    kept = jnp.sum(live_mask)
    windowed = window(samples, fir_taps).reshape(in_local * SPEC, NFFT)
    table = dft_table(NFFT, BAND_START, BAND)
    spectra = (
        jnp.dot(
            windowed, table, precision=lax.Precision.HIGHEST, preferred_element_type=jnp.float32
        )
        * dft_scale
    )
    spectra = spectra.reshape(in_local, SPEC, 2, BAND)
    chosen = jnp.take(spectra, chan_of, axis=3) * slot_used.astype(jnp.float32)[None, None, None, :]
    outgoing = jnp.transpose(chosen, (3, 0, 2, 1)).reshape(devices, capacity, in_local, 2 * SPEC)
    raw_vis = correlate(lax.all_to_all(outgoing, "feed", split_axis=0, concat_axis=2, tiled=True))
    local_power = jnp.sum(jnp.trace(raw_vis[:, 0], axis1=1, axis2=2))
    power = lax.psum(local_power, "feed")
    mean_power = power / (NIN * SPEC * kept)
    factor = 1.0 / (SPEC * mean_power)
    return (raw_vis * factor).astype(jnp.bfloat16)


def split(value):
    high = value.astype(jnp.bfloat16)
    return high, (value - high.astype(jnp.float32)).astype(jnp.bfloat16)


def contract_last(left, right):
    return lax.dot_general(
        left, right, (((1,), (1,)), ((), ())), preferred_element_type=jnp.float32
    )


def spectra_kernel(parts, carry_in, capacity, taps, in_local, *refs):
    slot_ref, live_ref, taps_a, taps_b, frames_a, frames_b, table = refs[:7]
    refs = refs[7:]
    before, refs = refs[:carry_in], refs[carry_in:]
    outs, refs = refs[: len(parts)], refs[len(parts) :]
    power_out, even_h, even_l, odd_h, odd_l, acc, flat = refs
    step = pl.program_id(0)
    tiles = NB // LANES

    for tile in range(tiles):
        lanes = slice(tile * LANES, (tile + 1) * LANES)
        coef_a = [taps_a[t : t + 1, lanes] for t in range(taps)]
        coef_b = [taps_b[t : t + 1, lanes] for t in range(taps)]
        for first in range(0, in_local, 16):

            def load(half, f):
                ref = (frames_a, frames_b)[half]
                return ref[f, first : first + 16, lanes].astype(jnp.float32)

            held_a = [load(0, f) for f in range(taps - 1)]
            held_b = [load(1, f) for f in range(taps - 1)]
            for s in range(GROUP):
                held_a.append(load(0, s + taps - 1))
                held_b.append(load(1, s + taps - 1))
                low_half = sum(coef_a[t] * held_a[t] for t in range(1, taps)) + coef_a[0] * held_a[0]
                high_half = sum(coef_b[t] * held_b[t] for t in range(1, taps)) + coef_b[0] * held_b[0]
                rows = slice(s * in_local + first, s * in_local + first + 16)
                even_h[rows, lanes], even_l[rows, lanes] = split(low_half + high_half)
                odd_h[rows, lanes], odd_l[rows, lanes] = split(low_half - high_half)
                held_a, held_b = held_a[1:], held_b[1:]

    for parity, (high, low) in enumerate(((even_h, even_l), (odd_h, odd_l))):
        total = contract_last(table[2 * parity], high[...])
        total += contract_last(table[2 * parity + 1], high[...])
        total += contract_last(table[2 * parity], low[...])
        rows = slice(parity * BAND, (parity + 1) * BAND)

        @pl.when(step == 0)
        def _():
            acc[rows, :] = total

        @pl.when(step > 0)
        def _():
            acc[rows, :] += total

    @pl.when(step == pl.num_programs(0) - 1)
    def _():
        width = GROUP * in_local // LANES
        for parity in range(2):
            for part in range(2):
                for block in range(BAND // 16):
                    for g in range(width):
                        start = parity * BAND + part * (BAND // 2) + block * 8
                        value = acc[start : start + 8, g * LANES : (g + 1) * LANES]
                        row = block * 128 + parity * 8 + part * width + g
                        flat[pl.ds(row, 8, stride=16), :] = value

        def place(c, total):
            value = flat[pl.ds(pl.multiple_of(c * 8, 8), 8), :]
            slot = slot_ref[c]
            dest, rank = lax.div(slot, capacity), lax.rem(slot, capacity)
            for out, (low, high, extra) in zip(outs, parts):

                @pl.when((rank >= low) & (rank < high))
                def _(out=out, low=low):
                    out[dest, rank - low] = value

            weight = live_ref[c].astype(jnp.float32)
            return total + weight * (value * value)

        total = lax.fori_loop(0, BAND, place, jnp.zeros((8, LANES), jnp.float32), unroll=8)
        for ref in before:
            total = total + ref[...]
        power_out[...] = total
        for out, (low, high, extra) in zip(outs, parts):
            if extra:
                for d in range(out.shape[0]):
                    out[d, high - low] = total


def spectra_call(group, parts, before, table, slot_of, live, fir_taps, samples, devices, capacity):
    _, in_local, _ = samples.shape
    taps = fir_taps.shape[0]
    steps = HALF // NB
    far = HALF // NB

    def frames_spec(offset):
        count = GROUP + taps - 1
        return pl.BlockSpec(
            (pl.Element(count), pl.Element(in_local), pl.Element(NB)),
            lambda j, *_: (group * GROUP, 0, pl.multiple_of((j + offset) * NB, NB)),
        )

    def taps_spec(offset):
        return pl.BlockSpec((taps, NB), lambda j, *_: (0, j + offset))

    rows = GROUP * in_local
    width = 2 * rows // LANES
    shapes = [
        jax.ShapeDtypeStruct((devices, high - low + extra, width, LANES), jnp.float32)
        for low, high, extra in parts
    ]
    shapes.append(jax.ShapeDtypeStruct((8, LANES), jnp.float32))
    grid_spec = pltpu.PrefetchScalarGridSpec(
        num_scalar_prefetch=2,
        grid=(steps,),
        in_specs=[
            taps_spec(0),
            taps_spec(far),
            frames_spec(0),
            frames_spec(far),
            pl.BlockSpec((4, BAND, NB), lambda j, *_: (0, 0, j)),
        ]
        + [pl.BlockSpec((8, LANES), lambda j, *_: (0, 0))] * len(before),
        out_specs=[pl.BlockSpec(s.shape, lambda j, *_, n=len(s.shape): (0,) * n) for s in shapes],
        scratch_shapes=[
            pltpu.VMEM((rows, NB), jnp.bfloat16),
            pltpu.VMEM((rows, NB), jnp.bfloat16),
            pltpu.VMEM((rows, NB), jnp.bfloat16),
            pltpu.VMEM((rows, NB), jnp.bfloat16),
            pltpu.VMEM((2 * BAND, rows), jnp.float32),
            pltpu.VMEM((BAND * 8, LANES), jnp.float32),
        ],
    )
    return pl.pallas_call(
        functools.partial(spectra_kernel, parts, len(before), capacity, taps, in_local),
        out_shape=shapes,
        grid_spec=grid_spec,
        compiler_params=pltpu.CompilerParams(vmem_limit_bytes=60 * MIB),
        cost_estimate=pl.CostEstimate(
            flops=3 * 2 * rows * HALF * 2 * BAND, bytes_accessed=30 * MIB, transcendentals=0
        ),
        name="spectra",
    )(
        slot_of,
        live,
        fir_taps,
        fir_taps,
        samples,
        samples,
        table,
        *before,
    )


def exchange_lanes(values, in_local):
    count = len(values)
    lane = lax.broadcasted_iota(jnp.int32, values[0].shape, 1) // in_local
    values = list(values)
    distance = count // 2
    while distance:
        upper = (lane & distance) != 0
        shift = distance * in_local
        for a in range(count):
            if a & distance:
                continue
            x, y = values[a], values[a + distance]
            values[a] = jnp.where(upper, pltpu.roll(y, shift, 1), x)
            values[a + distance] = jnp.where(upper, y, pltpu.roll(x, LANES - shift, 1))
        distance //= 2
    return values


def correlate_kernel(counts, in_local, *refs):
    used_ref, factor_ref = refs[:2]
    groups = refs[2 : 2 + counts]
    out, left_real, left_imag, right_a, right_b = refs[-5:]
    slot = pl.program_id(0)
    used = used_ref[slot] != 0
    per_tile = LANES // in_local
    sources = groups[0].shape[0]
    row_tiles = per_tile * counts

    @pl.when(used)
    def _():
        factor = factor_ref[0]
        upper = lax.broadcasted_iota(jnp.int32, (8, LANES), 0) >= 4
        for block in range(sources // per_tile):
            lanes = slice(block * LANES, (block + 1) * LANES)
            tiles = [None] * row_tiles
            for g, ref in enumerate(groups):
                mixed = [ref[block * per_tile + a, 0] for a in range(per_tile)]
                for q, value in enumerate(exchange_lanes(mixed, in_local)):
                    tiles[q * counts + g] = value
            turned = [jnp.where(upper, -1.0, 1.0) * pltpu.roll(t, 4, 0) for t in tiles]
            pad = [jnp.zeros((LANES - 8 * row_tiles, LANES), jnp.float32)]
            columns = jnp.concatenate(tiles + pad, axis=0)
            rotated = jnp.concatenate(turned + pad, axis=0)
            high, low = split(columns)
            right_a[:LANES, lanes] = high
            right_a[LANES:, lanes] = high
            right_b[:, lanes] = low
            high, low = split(columns.T)
            left_real[lanes, :LANES] = high
            left_real[lanes, LANES:] = low
            high, low = split(rotated.T)
            left_imag[lanes, :LANES] = high
            left_imag[lanes, LANES:] = low
        for part, left in enumerate((left_real, left_imag)):
            for block in range(sources // per_tile):
                rows = slice(block * LANES, (block + 1) * LANES)
                total = jnp.dot(left[rows, :], right_a[...], preferred_element_type=jnp.float32)
                total += jnp.dot(
                    left[rows, :LANES], right_b[...], preferred_element_type=jnp.float32
                )
                out[0, part, rows, :] = (total * factor).astype(jnp.bfloat16)

    @pl.when(jnp.logical_not(used))
    def _():
        out[...] = jnp.zeros_like(out)


def correlate_call(received, low, high, capacity, used, factor, total, in_local):
    arrays = [r for r, _ in received]
    sources = arrays[0].shape[0]
    nin = sources * in_local
    width = arrays[0].shape[2]
    aliases = {}
    extra, extra_specs = [], []
    if total is not None:
        extra, extra_specs = [total], [pl.BlockSpec(memory_space=pl.ANY)]
        aliases = {2 + len(arrays): 0}
    in_specs = [
        pl.BlockSpec(memory_space=pltpu.SMEM),
        pl.BlockSpec(memory_space=pltpu.SMEM),
    ] + [
        pl.BlockSpec((sources, 1, width, LANES), lambda s, d=low - first: (0, s + d, 0, 0))
        for _, first in received
    ]
    return pl.pallas_call(
        functools.partial(correlate_kernel, len(arrays), in_local),
        out_shape=jax.ShapeDtypeStruct((capacity, 2, nin, nin), jnp.bfloat16),
        grid=(high - low,),
        in_specs=in_specs + extra_specs,
        out_specs=pl.BlockSpec((1, 2, nin, nin), lambda s: (s + low, 0, 0, 0)),
        scratch_shapes=[
            pltpu.VMEM((nin, 2 * LANES), jnp.bfloat16),
            pltpu.VMEM((nin, 2 * LANES), jnp.bfloat16),
            pltpu.VMEM((2 * LANES, nin), jnp.bfloat16),
            pltpu.VMEM((LANES, nin), jnp.bfloat16),
        ],
        input_output_aliases=aliases,
        compiler_params=pltpu.CompilerParams(vmem_limit_bytes=60 * MIB),
        cost_estimate=pl.CostEstimate(
            flops=(high - low) * 8 * nin * nin * 256,
            bytes_accessed=(high - low) * (4 * nin * nin + 8 * nin * SPEC),
            transcendentals=0,
        ),
        name="correlate",
    )(used[low:high], factor, *arrays, *extra)


def local_blocks(samples, fir_taps, owner_map, dropped_channels):
    devices = lax.axis_size("feed")
    capacity = BAND // devices + BAND // (2 * devices)
    in_local = samples.shape[0]
    samples = jnp.transpose(samples, (1, 0, 2))
    owners = owner_map[:, 0]
    channels = jnp.arange(BAND, dtype=jnp.int32)
    same_owner = (owners[:, None] == owners[None, :]) & (channels[None, :] < channels[:, None])
    slot_of = owners * capacity + jnp.sum(same_owner.astype(jnp.int32), axis=1)
    live = jnp.logical_not(jnp.any(dropped_channels[None, :] == channels[:, None], axis=1))
    kept = jnp.sum(live.astype(jnp.float32))
    mine = lax.axis_index("feed") * capacity + jnp.arange(capacity, dtype=jnp.int32)
    used = jnp.any((slot_of[None, :] == mine[:, None]) & live[None, :], axis=1).astype(jnp.int32)

    table = jnp.asarray(folded_table())
    groups = SPEC // GROUP
    middle = capacity // 2
    received, powers = [], []
    for group in range(groups):
        if group < groups - 1:
            parts = ((0, capacity, 0),)
        else:
            parts = ((0, middle, 1), (middle, capacity, 0))
        *blocks, power = spectra_call(
            group,
            parts,
            powers[-1:],
            table,
            slot_of,
            live.astype(jnp.int32),
            fir_taps,
            samples,
            devices,
            capacity,
        )
        powers.append(power)
        received.append(
            [
                lax.all_to_all(block, "feed", split_axis=0, concat_axis=0, tiled=True)
                for block in blocks
            ]
        )
    power = jnp.sum(received[-1][0][:, middle])
    mean_power = power / (NIN * SPEC * kept)
    factor = jnp.reshape(1.0 / (SPEC * mean_power), (1,))
    full = [(blocks[0], 0) for blocks in received[:-1]]
    first = correlate_call(
        full + [(received[-1][0], 0)], 0, middle, capacity, used, factor, None, in_local
    )
    return correlate_call(
        full + [(received[-1][1], middle)], middle, capacity, capacity, used, factor, first, in_local
    )


def solution(mesh):
    in_local = NIN // mesh.shape["feed"]
    blocks = in_local * 4 == LANES
    return jax.shard_map(
        local_blocks if blocks else local_plain,
        mesh=mesh,
        in_specs=(P("feed", "grp", None), P(), P(), P("grp")),
        out_specs=P(("grp", "feed"), None, None, None),
        check_vma=False,
    )
```

```python
import functools
import math

import jax
import jax.numpy as jnp
import ml_dtypes
import numpy as np
from jax import lax
from jax.experimental import pallas as pl
from jax.experimental.pallas import tpu as pltpu
from jax.sharding import PartitionSpec as P

NIN = 512
NFFT = 8192
HALF = NFFT // 2
BAND = 256
BAND_START = 1536
SPEC = 48
FIRST = 16
KB = 256
LANES = 128
MIB = 1 << 20


def dft_table(length, first, width):
    row_ids = lax.broadcasted_iota(jnp.int32, (length, width), 0)
    chan_ids = first + lax.broadcasted_iota(jnp.int32, (length, width), 1)
    phase_int = row_ids * chan_ids % length
    angles = phase_int.astype(jnp.float32) * (2.0 * math.pi / length)
    return jnp.concatenate([jnp.cos(angles), -jnp.sin(angles)], axis=1)


def folded_table():
    n = np.arange(HALF, dtype=np.int64)
    tables = []
    for parity in range(2):
        chans = BAND_START + 2 * np.arange(BAND // 2, dtype=np.int64) + parity
        angles = (n[:, None] * chans[None, :] % NFFT) * (2.0 * math.pi / NFFT)
        full = np.concatenate([np.cos(angles), -np.sin(angles)], axis=1) / math.sqrt(NFFT)
        high = full.astype(np.float32).astype(ml_dtypes.bfloat16)
        low = (full - high.astype(np.float64)).astype(np.float32).astype(ml_dtypes.bfloat16)
        tables.append(np.stack([high, low]))
    return np.stack(tables)


def slot_tables(owner_map, dropped_channels, capacity, slot_total):
    owners = owner_map[:, 0]
    channels = jnp.arange(owners.shape[0], dtype=jnp.int32)
    same_owner = (owners[:, None] == owners[None, :]) & (channels[None, :] < channels[:, None])
    rank_in = jnp.sum(same_owner.astype(jnp.int32), axis=1)
    slot_of = owners * capacity + rank_in
    flagged = jnp.any(dropped_channels[:, None] == channels[None, :], axis=0)
    channel_live = jnp.logical_not(flagged)
    targets = jnp.arange(slot_total, dtype=jnp.int32)
    slot_hit = (slot_of[:, None] == targets[None, :]) & channel_live[:, None]
    chan_of = jnp.sum(slot_hit.astype(jnp.int32) * channels[:, None], axis=0)
    slot_used = jnp.any(slot_hit, axis=0)
    return (chan_of, slot_used, channel_live)


def window(block, fir_taps):
    taps = fir_taps.shape[0]
    spec_count = block.shape[1] - taps + 1
    summed = jnp.zeros((block.shape[0], spec_count, block.shape[2]), jnp.float32)
    for tap_index in range(taps):
        summed = summed + fir_taps[tap_index][None, None, :] * block[
            :, tap_index : tap_index + spec_count, :
        ].astype(jnp.float32)
    return summed


def pair_products(left, right):
    return jnp.einsum(
        "qis,qjs->qij",
        left,
        right,
        precision=lax.Precision.HIGHEST,
        preferred_element_type=jnp.float32,
    )


def correlate(received):
    columns = received[0]
    real_rows = columns[:, :, :SPEC]
    imag_rows = columns[:, :, SPEC:]
    rotated = jnp.concatenate([imag_rows, -real_rows], axis=2)
    real_vis = pair_products(columns, columns)
    imag_vis = pair_products(rotated, columns)
    return jnp.stack([real_vis, imag_vis], axis=1)


def local_plain(samples, fir_taps, owner_map, dropped_channels):
    devices = lax.axis_size("feed")
    capacity = BAND // devices + BAND // (2 * devices)
    slot_total = devices * capacity
    in_local = samples.shape[0]
    dft_scale = 1.0 / math.sqrt(NFFT)
    chan_of, slot_used, channel_live = slot_tables(
        owner_map, dropped_channels, capacity, slot_total
    )
    live_mask = channel_live.astype(jnp.float32)
    kept = jnp.sum(live_mask)
    windowed = window(samples, fir_taps).reshape(in_local * SPEC, NFFT)
    table = dft_table(NFFT, BAND_START, BAND)
    spectra = (
        jnp.dot(
            windowed, table, precision=lax.Precision.HIGHEST, preferred_element_type=jnp.float32
        )
        * dft_scale
    )
    spectra = spectra.reshape(in_local, SPEC, 2, BAND)
    chosen = jnp.take(spectra, chan_of, axis=3) * slot_used.astype(jnp.float32)[None, None, None, :]
    outgoing = jnp.transpose(chosen, (3, 0, 2, 1)).reshape(devices, capacity, in_local, 2 * SPEC)
    raw_vis = correlate(lax.all_to_all(outgoing, "feed", split_axis=0, concat_axis=2, tiled=True))
    local_power = jnp.sum(jnp.trace(raw_vis[:, 0], axis1=1, axis2=2))
    power = lax.psum(local_power, "feed")
    mean_power = power / (NIN * SPEC * kept)
    factor = 1.0 / (SPEC * mean_power)
    return (raw_vis * factor).astype(jnp.bfloat16)


def split(value):
    high = value.astype(jnp.bfloat16)
    return high, (value - high.astype(jnp.float32)).astype(jnp.bfloat16)


def spectra_kernel(count, parts, carry_in, taps, in_local, *refs):
    row_ref, live_ref, taps_a, taps_b, frames_a, frames_b, table_a, table_b, table_last = refs[:9]
    refs = refs[9:]
    before, refs = refs[:carry_in], refs[carry_in:]
    outs, refs = refs[: len(parts)], refs[len(parts) :]
    power_out, even_0, odd_0, even_1, odd_1, acc, flat = refs
    step = pl.program_id(0)
    rows = count * in_local

    def windowed(block, even, odd):
        for tile in range(KB // LANES):
            own = slice(tile * LANES, (tile + 1) * LANES)
            lanes = slice(block * KB + tile * LANES, block * KB + (tile + 1) * LANES)
            coef_a = [taps_a[t : t + 1, lanes] for t in range(taps)]
            coef_b = [taps_b[t : t + 1, lanes] for t in range(taps)]
            for first in range(0, in_local, 16):

                def load(ref, f):
                    return ref[f, first : first + 16, lanes].astype(jnp.float32)

                held_a = [load(frames_a, f) for f in range(taps - 1)]
                held_b = [load(frames_b, f) for f in range(taps - 1)]
                for s in range(count):
                    held_a.append(load(frames_a, s + taps - 1))
                    held_b.append(load(frames_b, s + taps - 1))
                    near = sum(c * x for c, x in zip(coef_a[1:], held_a[1:])) + coef_a[0] * held_a[0]
                    far = sum(c * x for c, x in zip(coef_b[1:], held_b[1:])) + coef_b[0] * held_b[0]
                    at = slice(s * in_local + first, s * in_local + first + 16)
                    for ref, value in ((even, near + far), (odd, near - far)):
                        high, low = split(value)
                        ref[at, tile * LANES : (tile + 1) * LANES] = high
                        ref[at, KB + tile * LANES : KB + (tile + 1) * LANES] = low
                    held_a, held_b = held_a[1:], held_b[1:]

    def multiply(table, even, odd):
        for parity, ref in enumerate((even, odd)):
            cols = slice(parity * BAND, (parity + 1) * BAND)
            right = jnp.concatenate([table[parity, 0], table[parity, 0], table[parity, 1]], axis=0)
            for start in range(0, rows, 256):
                at = slice(start, start + 256)
                left = jnp.concatenate([ref[at, :], ref[at, :KB]], axis=1)
                acc[at, cols] += jnp.dot(left, right, preferred_element_type=jnp.float32)

    @pl.when(step == 0)
    def _():
        even_1[...] = jnp.zeros_like(even_1)
        odd_1[...] = jnp.zeros_like(odd_1)
        acc[...] = jnp.zeros_like(acc)

    multiply(table_b, even_1, odd_1)
    windowed(0, even_0, odd_0)
    multiply(table_a, even_0, odd_0)
    windowed(1, even_1, odd_1)

    @pl.when(step == pl.num_programs(0) - 1)
    def _():
        multiply(table_last, even_1, odd_1)
        width = rows // LANES
        for parity in range(2):
            for part in range(2):
                cols = slice(parity * BAND + part * LANES, parity * BAND + (part + 1) * LANES)
                for g in range(width):
                    turned = acc[g * LANES : (g + 1) * LANES, cols].T
                    row = (parity * 2 + part) * width + g
                    flat[pl.ds(row, LANES, stride=4 * width), :] = turned
        size = 2 * width

        def place(c, total):
            value = flat[pl.ds(pl.multiple_of(c * size, size), size), :]
            for p, out in enumerate(outs):
                row = row_ref[p, c]

                @pl.when(row >= 0)
                def _(out=out, row=row):
                    out[row] = value

            square = sum(value[start : start + 8] ** 2 for start in range(0, size, 8))
            return total + live_ref[c].astype(jnp.float32) * square

        total = lax.fori_loop(0, BAND, place, jnp.zeros((8, LANES), jnp.float32), unroll=8)
        for ref in before:
            total = total + ref[...]
        power_out[...] = total
        for out, (low, high, extra) in zip(outs, parts):
            if extra:
                for d in range(out.shape[0] // (high - low + extra)):
                    out[(d + 1) * (high - low + extra) - 1, :8] = total


def spectra_call(first, count, parts, before, table, place, live, fir_taps, samples, devices):
    _, in_local, _ = samples.shape
    taps = fir_taps.shape[0]
    step_size = 2 * KB
    steps = HALF // step_size
    owners, ranks = place
    rows_of = [
        jnp.where((ranks >= low) & (ranks < high), owners * (high - low + extra) + ranks - low, -1)
        for low, high, extra in parts
    ]

    def frames_spec(offset):
        return pl.BlockSpec(
            (pl.Element(count + taps - 1), pl.Element(in_local), pl.Element(step_size)),
            lambda j, *_: (first, 0, pl.multiple_of((j + offset) * step_size, step_size)),
        )

    def taps_spec(offset):
        return pl.BlockSpec((taps, step_size), lambda j, *_: (0, j + offset))

    def table_spec(index):
        return pl.BlockSpec((2, 2, KB, BAND), lambda j, *_: (0, 0, index(j), 0))

    rows = count * in_local
    width = 2 * rows // LANES
    shapes = [
        jax.ShapeDtypeStruct((devices * (high - low + extra), width, LANES), jnp.float32)
        for low, high, extra in parts
    ]
    shapes.append(jax.ShapeDtypeStruct((8, LANES), jnp.float32))
    grid_spec = pltpu.PrefetchScalarGridSpec(
        num_scalar_prefetch=2,
        grid=(steps,),
        in_specs=[
            taps_spec(0),
            taps_spec(steps),
            frames_spec(0),
            frames_spec(steps),
            table_spec(lambda j: 2 * j),
            table_spec(lambda j: jnp.maximum(2 * j - 1, 0)),
            table_spec(lambda j: 2 * steps - 1),
        ]
        + [pl.BlockSpec((8, LANES), lambda j, *_: (0, 0))] * len(before),
        out_specs=[pl.BlockSpec(s.shape, lambda j, *_, n=len(s.shape): (0,) * n) for s in shapes],
        scratch_shapes=[pltpu.VMEM((rows, 2 * KB), jnp.bfloat16)] * 4
        + [
            pltpu.VMEM((rows, 2 * BAND), jnp.float32),
            pltpu.VMEM((BAND * width, LANES), jnp.float32),
        ],
    )
    *blocks, power = pl.pallas_call(
        functools.partial(spectra_kernel, count, parts, len(before), taps, in_local),
        out_shape=shapes,
        grid_spec=grid_spec,
        compiler_params=pltpu.CompilerParams(vmem_limit_bytes=60 * MIB),
        cost_estimate=pl.CostEstimate(
            flops=3 * 2 * rows * HALF * 2 * BAND, bytes_accessed=30 * MIB, transcendentals=0
        ),
        name="spectra",
    )(
        jnp.stack(rows_of),
        live,
        fir_taps,
        fir_taps,
        samples,
        samples,
        table,
        table,
        table,
        *before,
    )
    return [block.reshape(devices, -1, width, LANES) for block in blocks], power


def exchange_lanes(values, in_local):
    count = len(values)
    lane = lax.broadcasted_iota(jnp.int32, values[0].shape, 1) // in_local
    values = list(values)
    distance = count // 2
    while distance:
        upper = (lane & distance) != 0
        shift = distance * in_local
        for a in range(count):
            if a & distance:
                continue
            x, y = values[a], values[a + distance]
            values[a] = jnp.where(upper, pltpu.roll(y, shift, 1), x)
            values[a + distance] = jnp.where(upper, y, pltpu.roll(x, LANES - shift, 1))
        distance //= 2
    return values


def correlate_kernel(counts, slots, in_local, *refs):
    factor_ref, used_ref = refs[:2]
    groups = refs[2 : 2 + counts]
    out = refs[-1 - 2 * slots]
    scratch = refs[-2 * slots :]
    per_tile = LANES // in_local
    sources = groups[0].shape[0]
    factor = factor_ref[0]
    upper = lax.broadcasted_iota(jnp.int32, (8, LANES), 0) >= 4

    def prepare(slot, left, right):
        for block in range(sources // per_tile):
            lanes = slice(block * LANES, (block + 1) * LANES)
            straight, turned = [], []
            for ref in groups:
                width = ref.shape[2]
                tiles = []
                for start in range(0, width, 8):
                    mixed = [
                        ref[block * per_tile + a, slot, start : start + 8] for a in range(per_tile)
                    ]
                    tiles.append(exchange_lanes(mixed, in_local))
                for q in range(per_tile):
                    column = [t[q] for t in tiles]
                    straight += column
                    if len(column) == 1:
                        swapped = pltpu.roll(column[0], 4, 0)
                        turned.append(jnp.where(upper, -swapped, swapped))
                    else:
                        half = len(column) // 2
                        turned += column[half:] + [-t for t in column[:half]]
            pad = [jnp.zeros((LANES - 8 * len(straight), LANES), jnp.float32)]
            columns = jnp.concatenate(straight + pad, axis=0)
            rotated = jnp.concatenate(turned + pad, axis=0)
            high, low = split(columns)
            right[:LANES, lanes] = high
            right[LANES : 2 * LANES, lanes] = high
            right[2 * LANES :, lanes] = low
            for part, value in enumerate((columns, rotated)):
                high, low = split(value.T)
                at = slice((part * sources // per_tile + block) * LANES, (part * sources // per_tile + block + 1) * LANES)
                left[at, :LANES] = high
                left[at, LANES : 2 * LANES] = low
                left[at, 2 * LANES :] = high

    def multiply(slot, left, right):
        used = used_ref[pl.program_id(0) * slots + slot] != 0
        nin = sources * in_local
        for part in range(2):
            for start in range(0, nin, 256):
                total = jnp.dot(
                    left[part * nin + start : part * nin + start + 256, :],
                    right[...],
                    preferred_element_type=jnp.float32,
                )
                total = jnp.where(used, total * factor, 0.0)
                out[slot, part, start : start + 256, :] = total.astype(jnp.bfloat16)

    for slot in range(slots):
        prepare(slot, scratch[2 * slot], scratch[2 * slot + 1])
        if slot:
            multiply(slot - 1, scratch[2 * slot - 2], scratch[2 * slot - 1])
    multiply(slots - 1, scratch[2 * slots - 2], scratch[2 * slots - 1])


def correlate_call(received, low, high, capacity, used, factor, total, in_local, slots):
    arrays = [r for r, _ in received]
    sources = arrays[0].shape[0]
    nin = sources * in_local
    aliases = {}
    extra, extra_specs = [], []
    if total is not None:
        extra, extra_specs = [total], [pl.BlockSpec(memory_space=pl.ANY)]
        aliases = {2 + len(arrays): 0}
    in_specs = [
        pl.BlockSpec(memory_space=pltpu.SMEM),
        pl.BlockSpec(memory_space=pltpu.SMEM),
    ] + [
        pl.BlockSpec(
            (sources, slots, r.shape[2], LANES),
            lambda s, d=(low - first) // slots: (0, s + d, 0, 0),
        )
        for r, first in received
    ]
    return pl.pallas_call(
        functools.partial(correlate_kernel, len(arrays), slots, in_local),
        out_shape=jax.ShapeDtypeStruct((capacity, 2, nin, nin), jnp.bfloat16),
        grid=((high - low) // slots,),
        in_specs=in_specs + extra_specs,
        out_specs=pl.BlockSpec((slots, 2, nin, nin), lambda s: (s + low // slots, 0, 0, 0)),
        scratch_shapes=[
            pltpu.VMEM((2 * nin, 3 * LANES), jnp.bfloat16),
            pltpu.VMEM((3 * LANES, nin), jnp.bfloat16),
        ]
        * slots,
        input_output_aliases=aliases,
        compiler_params=pltpu.CompilerParams(vmem_limit_bytes=60 * MIB),
        cost_estimate=pl.CostEstimate(
            flops=(high - low) * 8 * nin * nin * 256,
            bytes_accessed=(high - low) * (4 * nin * nin + 8 * nin * SPEC),
            transcendentals=0,
        ),
        name="correlate",
    )(factor, used[low:high], *arrays, *extra)


def exchange(block):
    return lax.all_to_all(block, "feed", split_axis=0, concat_axis=0, tiled=True)


def local_blocks(samples, fir_taps, owner_map, dropped_channels):
    devices = lax.axis_size("feed")
    capacity = BAND // devices + BAND // (2 * devices)
    in_local = samples.shape[0]
    frames = jnp.transpose(samples, (1, 0, 2))
    owners = owner_map[:, 0]
    channels = jnp.arange(BAND, dtype=jnp.int32)
    same_owner = (owners[:, None] == owners[None, :]) & (channels[None, :] < channels[:, None])
    ranks = jnp.sum(same_owner.astype(jnp.int32), axis=1)
    live = jnp.logical_not(jnp.any(dropped_channels[None, :] == channels[:, None], axis=1))
    kept = jnp.sum(live.astype(jnp.float32))
    mine = (owners == lax.axis_index("feed")) & live
    slots = jnp.arange(capacity, dtype=jnp.int32)
    used = jnp.any((ranks[None, :] == slots[:, None]) & mine[None, :], axis=1).astype(jnp.int32)

    table = jnp.asarray(folded_table())
    middle = capacity * 3 // 4
    live_flags = live.astype(jnp.int32)
    call = functools.partial(
        spectra_call,
        table=table,
        place=(owners, ranks),
        live=live_flags,
        fir_taps=fir_taps,
        samples=frames,
        devices=devices,
    )
    (block_a,), power = call(0, FIRST, ((0, capacity, 0),), [])
    received_a = exchange(block_a)
    (block_b, block_c), _ = call(
        FIRST, SPEC - FIRST, ((0, middle, 1), (middle, capacity, 0)), [power]
    )
    block_b, received_a = lax.optimization_barrier((block_b, received_a))
    received_b = exchange(block_b)
    block_c, received_b = lax.optimization_barrier((block_c, received_b))
    received_c = exchange(block_c)

    power = jnp.sum(received_b[:, middle, :8])
    mean_power = power / (NIN * SPEC * kept)
    factor = jnp.reshape(1.0 / (SPEC * mean_power), (1,))
    run = functools.partial(
        correlate_call, capacity=capacity, used=used, factor=factor, in_local=in_local, slots=2
    )
    first = run([(received_a, 0), (received_b, 0)], 0, middle, total=None)
    return run([(received_a, 0), (received_c, middle)], middle, capacity, total=first)


def solution(mesh):
    in_local = NIN // mesh.shape["feed"]
    blocks = in_local * 4 == LANES
    return jax.shard_map(
        local_blocks if blocks else local_plain,
        mesh=mesh,
        in_specs=(P("feed", "grp", None), P(), P(), P("grp")),
        out_specs=P(("grp", "feed"), None, None, None),
        check_vma=False,
    )
```

```python
import functools
import math

import jax
import jax.numpy as jnp
import ml_dtypes
import numpy as np
from jax import lax
from jax.experimental import pallas as pl
from jax.experimental.pallas import tpu as pltpu
from jax.sharding import PartitionSpec as P

NIN = 512
NFFT = 8192
HALF = NFFT // 2
BAND = 256
BAND_START = 1536
SPEC = 48
FIRST = 16
KB = 256
LANES = 128
MIB = 1 << 20


def dft_table(length, first, width):
    row_ids = lax.broadcasted_iota(jnp.int32, (length, width), 0)
    chan_ids = first + lax.broadcasted_iota(jnp.int32, (length, width), 1)
    phase_int = row_ids * chan_ids % length
    angles = phase_int.astype(jnp.float32) * (2.0 * math.pi / length)
    return jnp.concatenate([jnp.cos(angles), -jnp.sin(angles)], axis=1)


def folded_table():
    n = np.arange(HALF, dtype=np.int64)
    tables = []
    for parity in range(2):
        chans = BAND_START + 2 * np.arange(BAND // 2, dtype=np.int64) + parity
        angles = (n[:, None] * chans[None, :] % NFFT) * (2.0 * math.pi / NFFT)
        full = np.concatenate([np.cos(angles), -np.sin(angles)], axis=1) / math.sqrt(NFFT)
        high = full.astype(np.float32).astype(ml_dtypes.bfloat16)
        low = (full - high.astype(np.float64)).astype(np.float32).astype(ml_dtypes.bfloat16)
        tables.append(np.stack([high, low]))
    return np.stack(tables)


def slot_tables(owner_map, dropped_channels, capacity, slot_total):
    owners = owner_map[:, 0]
    channels = jnp.arange(owners.shape[0], dtype=jnp.int32)
    same_owner = (owners[:, None] == owners[None, :]) & (channels[None, :] < channels[:, None])
    rank_in = jnp.sum(same_owner.astype(jnp.int32), axis=1)
    slot_of = owners * capacity + rank_in
    flagged = jnp.any(dropped_channels[:, None] == channels[None, :], axis=0)
    channel_live = jnp.logical_not(flagged)
    targets = jnp.arange(slot_total, dtype=jnp.int32)
    slot_hit = (slot_of[:, None] == targets[None, :]) & channel_live[:, None]
    chan_of = jnp.sum(slot_hit.astype(jnp.int32) * channels[:, None], axis=0)
    slot_used = jnp.any(slot_hit, axis=0)
    return (chan_of, slot_used, channel_live)


def window(block, fir_taps):
    taps = fir_taps.shape[0]
    spec_count = block.shape[1] - taps + 1
    summed = jnp.zeros((block.shape[0], spec_count, block.shape[2]), jnp.float32)
    for tap_index in range(taps):
        summed = summed + fir_taps[tap_index][None, None, :] * block[
            :, tap_index : tap_index + spec_count, :
        ].astype(jnp.float32)
    return summed


def pair_products(left, right):
    return jnp.einsum(
        "qis,qjs->qij",
        left,
        right,
        precision=lax.Precision.HIGHEST,
        preferred_element_type=jnp.float32,
    )


def correlate(received):
    columns = received[0]
    real_rows = columns[:, :, :SPEC]
    imag_rows = columns[:, :, SPEC:]
    rotated = jnp.concatenate([imag_rows, -real_rows], axis=2)
    real_vis = pair_products(columns, columns)
    imag_vis = pair_products(rotated, columns)
    return jnp.stack([real_vis, imag_vis], axis=1)


def local_plain(samples, fir_taps, owner_map, dropped_channels):
    devices = lax.axis_size("feed")
    capacity = BAND // devices + BAND // (2 * devices)
    slot_total = devices * capacity
    in_local = samples.shape[0]
    dft_scale = 1.0 / math.sqrt(NFFT)
    chan_of, slot_used, channel_live = slot_tables(
        owner_map, dropped_channels, capacity, slot_total
    )
    live_mask = channel_live.astype(jnp.float32)
    kept = jnp.sum(live_mask)
    windowed = window(samples, fir_taps).reshape(in_local * SPEC, NFFT)
    table = dft_table(NFFT, BAND_START, BAND)
    spectra = (
        jnp.dot(
            windowed, table, precision=lax.Precision.HIGHEST, preferred_element_type=jnp.float32
        )
        * dft_scale
    )
    spectra = spectra.reshape(in_local, SPEC, 2, BAND)
    chosen = jnp.take(spectra, chan_of, axis=3) * slot_used.astype(jnp.float32)[None, None, None, :]
    outgoing = jnp.transpose(chosen, (3, 0, 2, 1)).reshape(devices, capacity, in_local, 2 * SPEC)
    raw_vis = correlate(lax.all_to_all(outgoing, "feed", split_axis=0, concat_axis=2, tiled=True))
    local_power = jnp.sum(jnp.trace(raw_vis[:, 0], axis1=1, axis2=2))
    power = lax.psum(local_power, "feed")
    mean_power = power / (NIN * SPEC * kept)
    factor = 1.0 / (SPEC * mean_power)
    return (raw_vis * factor).astype(jnp.bfloat16)


def split(value):
    high = value.astype(jnp.bfloat16)
    return high, (value - high.astype(jnp.float32)).astype(jnp.bfloat16)


def spectra_kernel(count, last, devices, message, taps, in_local, *refs):
    row_ref, taps_a, taps_b, frames_a, frames_b, table_a, table_b, table_last = refs[:8]
    if last:
        before, out = refs[8:10]
    else:
        out, power_out = refs[8:10]
    even_0, odd_0, even_1, odd_1, acc, flat = refs[10:]
    step = pl.program_id(0)
    rows = count * in_local

    def windowed(block, even, odd):
        for tile in range(KB // LANES):
            own = slice(tile * LANES, (tile + 1) * LANES)
            lanes = slice(block * KB + tile * LANES, block * KB + (tile + 1) * LANES)
            coef_a = [taps_a[t : t + 1, lanes] for t in range(taps)]
            coef_b = [taps_b[t : t + 1, lanes] for t in range(taps)]
            for first in range(0, in_local, 16):

                def load(ref, f):
                    return ref[f, first : first + 16, lanes].astype(jnp.float32)

                held_a = [load(frames_a, f) for f in range(taps - 1)]
                held_b = [load(frames_b, f) for f in range(taps - 1)]
                for s in range(count):
                    held_a.append(load(frames_a, s + taps - 1))
                    held_b.append(load(frames_b, s + taps - 1))
                    near = sum(c * x for c, x in zip(coef_a[1:], held_a[1:])) + coef_a[0] * held_a[0]
                    far = sum(c * x for c, x in zip(coef_b[1:], held_b[1:])) + coef_b[0] * held_b[0]
                    at = slice(s * in_local + first, s * in_local + first + 16)
                    for ref, value in ((even, near + far), (odd, near - far)):
                        high, low = split(value)
                        ref[at, tile * LANES : (tile + 1) * LANES] = high
                        ref[at, KB + tile * LANES : KB + (tile + 1) * LANES] = low
                    held_a, held_b = held_a[1:], held_b[1:]

    def multiply(table, even, odd):
        for parity, ref in enumerate((even, odd)):
            cols = slice(parity * BAND, (parity + 1) * BAND)
            right = jnp.concatenate([table[parity, 0], table[parity, 0], table[parity, 1]], axis=0)
            for start in range(0, rows, 512):
                at = slice(start, start + 512)
                left = jnp.concatenate([ref[at, :], ref[at, :KB]], axis=1)
                acc[at, cols] += jnp.dot(left, right, preferred_element_type=jnp.float32)

    @pl.when(step == 0)
    def _():
        even_1[...] = jnp.zeros_like(even_1)
        odd_1[...] = jnp.zeros_like(odd_1)
        acc[...] = jnp.zeros_like(acc)

    multiply(table_b, even_1, odd_1)
    windowed(0, even_0, odd_0)
    multiply(table_a, even_0, odd_0)
    windowed(1, even_1, odd_1)

    @pl.when(step == pl.num_programs(0) - 1)
    def _():
        multiply(table_last, even_1, odd_1)
        width = rows // LANES
        for parity in range(2):
            for part in range(2):
                cols = slice(parity * BAND + part * LANES, parity * BAND + (part + 1) * LANES)
                for g in range(width):
                    turned = acc[g * LANES : (g + 1) * LANES, cols].T
                    row = (parity * 2 + part) * width + g
                    flat[pl.ds(row, LANES, stride=4 * width), :] = turned
        size = 2 * width

        def place(c, total):
            value = flat[pl.ds(pl.multiple_of(c * size, size), size), :]
            row = row_ref[c]

            @pl.when(row >= 0)
            def _():
                out[pl.ds(pl.multiple_of(row * 8, 8), size), :] = value

            square = sum(value[start : start + 8] ** 2 for start in range(0, size, 8))
            return total + (row >= 0).astype(jnp.float32) * square

        total = lax.fori_loop(0, BAND, place, jnp.zeros((8, LANES), jnp.float32), unroll=8)
        if last:
            total = total + before[...]
            for d in range(devices):
                out[(d + 1) * message - 8 : (d + 1) * message, :] = total
        else:
            power_out[...] = total


def spectra_call(first, count, before, table, owners, ranks, dead, fir_taps, samples, devices):
    _, in_local, _ = samples.shape
    taps = fir_taps.shape[0]
    step_size = 2 * KB
    steps = HALF // step_size
    last = before is not None
    rows = count * in_local
    width = 2 * rows // LANES
    capacity = BAND // devices + BAND // (2 * devices)
    message = capacity * width + 8 * last
    row_of = jnp.where(dead, -1, owners * (message // 8) + ranks * (width // 8))

    def frames_spec(offset):
        return pl.BlockSpec(
            (pl.Element(count + taps - 1), pl.Element(in_local), pl.Element(step_size)),
            lambda j, *_: (first, 0, pl.multiple_of((j + offset) * step_size, step_size)),
        )

    def taps_spec(offset):
        return pl.BlockSpec((taps, step_size), lambda j, *_: (0, j + offset))

    def table_spec(index):
        return pl.BlockSpec((2, 2, KB, BAND), lambda j, *_: (0, 0, index(j), 0))

    block = jax.ShapeDtypeStruct((devices * message, LANES), jnp.float32)
    power = jax.ShapeDtypeStruct((8, LANES), jnp.float32)
    whole = [pl.BlockSpec(block.shape, lambda j, *_: (0, 0))]
    single = [pl.BlockSpec(power.shape, lambda j, *_: (0, 0))]
    grid_spec = pltpu.PrefetchScalarGridSpec(
        num_scalar_prefetch=1,
        grid=(steps,),
        in_specs=[
            taps_spec(0),
            taps_spec(steps),
            frames_spec(0),
            frames_spec(steps),
            table_spec(lambda j: 2 * j),
            table_spec(lambda j: jnp.maximum(2 * j - 1, 0)),
            table_spec(lambda j: 2 * steps - 1),
        ]
        + (single if last else []),
        out_specs=whole + ([] if last else single),
        scratch_shapes=[pltpu.VMEM((rows, 2 * KB), jnp.bfloat16)] * 4
        + [
            pltpu.VMEM((rows, 2 * BAND), jnp.float32),
            pltpu.VMEM((BAND * width, LANES), jnp.float32),
        ],
    )
    sent, *rest = pl.pallas_call(
        functools.partial(spectra_kernel, count, last, devices, message, taps, in_local),
        out_shape=[block] + ([] if last else [power]),
        grid_spec=grid_spec,
        compiler_params=pltpu.CompilerParams(vmem_limit_bytes=60 * MIB),
        cost_estimate=pl.CostEstimate(
            flops=3 * 2 * rows * HALF * 2 * BAND, bytes_accessed=30 * MIB, transcendentals=0
        ),
        name="spectra",
    )(
        row_of,
        fir_taps,
        fir_taps,
        samples,
        samples,
        table,
        table,
        table,
        *([before] if last else []),
    )
    return [sent.reshape(devices, message, LANES)] + rest


def exchange_lanes(values, in_local):
    count = len(values)
    lane = lax.broadcasted_iota(jnp.int32, values[0].shape, 1) // in_local
    values = list(values)
    distance = count // 2
    while distance:
        upper = (lane & distance) != 0
        shift = distance * in_local
        for a in range(count):
            if a & distance:
                continue
            x, y = values[a], values[a + distance]
            values[a] = jnp.where(upper, pltpu.roll(y, shift, 1), x)
            values[a + distance] = jnp.where(upper, y, pltpu.roll(x, LANES - shift, 1))
        distance //= 2
    return values


def correlate_kernel(widths, slots, in_local, factor_ref, used_ref, *refs):
    groups = refs[: len(widths)]
    out = refs[len(widths)]
    scratch = refs[len(widths) + 1 :]
    per_tile = LANES // in_local
    sources = groups[0].shape[0]
    factor = factor_ref[0]
    upper = lax.broadcasted_iota(jnp.int32, (8, LANES), 0) >= 4

    def prepare(slot, left, right):
        for block in range(sources // per_tile):
            lanes = slice(block * LANES, (block + 1) * LANES)
            straight, turned = [], []
            for ref, width in zip(groups, widths):
                tiles = []
                for start in range(slot * width, (slot + 1) * width, 8):
                    mixed = [
                        ref[block * per_tile + a, start : start + 8] for a in range(per_tile)
                    ]
                    tiles.append(exchange_lanes(mixed, in_local))
                for q in range(per_tile):
                    column = [t[q] for t in tiles]
                    straight += column
                    if len(column) == 1:
                        swapped = pltpu.roll(column[0], 4, 0)
                        turned.append(jnp.where(upper, -swapped, swapped))
                    else:
                        half = len(column) // 2
                        turned += column[half:] + [-t for t in column[:half]]
            pad = [jnp.zeros((LANES - 8 * len(straight), LANES), jnp.float32)]
            columns = jnp.concatenate(straight + pad, axis=0)
            rotated = jnp.concatenate(turned + pad, axis=0)
            high, low = split(columns)
            right[:LANES, lanes] = high
            right[LANES : 2 * LANES, lanes] = high
            right[2 * LANES :, lanes] = low
            for part, value in enumerate((columns, rotated)):
                high, low = split(value.T)
                at = slice((part * sources // per_tile + block) * LANES, (part * sources // per_tile + block + 1) * LANES)
                left[at, :LANES] = high
                left[at, LANES : 2 * LANES] = low
                left[at, 2 * LANES :] = high

    def multiply(slot, left, right):
        used = used_ref[pl.program_id(0) * slots + slot] != 0
        nin = sources * in_local
        for part in range(2):
            total = jnp.dot(
                left[part * nin : (part + 1) * nin, :],
                right[...],
                preferred_element_type=jnp.float32,
            )
            total = jnp.where(used, total * factor, 0.0)
            out[slot, part] = total.astype(jnp.bfloat16)

    for slot in range(slots):
        prepare(slot, scratch[2 * slot], scratch[2 * slot + 1])
        if slot:
            multiply(slot - 1, scratch[2 * slot - 2], scratch[2 * slot - 1])
    multiply(slots - 1, scratch[2 * slots - 2], scratch[2 * slots - 1])


def correlate_call(received, widths, capacity, used, factor, in_local, slots):
    sources = received[0].shape[0]
    nin = sources * in_local
    in_specs = [
        pl.BlockSpec(memory_space=pltpu.SMEM),
        pl.BlockSpec(memory_space=pltpu.SMEM),
    ] + [pl.BlockSpec((sources, slots * width, LANES), lambda s: (0, s, 0)) for width in widths]
    return pl.pallas_call(
        functools.partial(correlate_kernel, widths, slots, in_local),
        out_shape=jax.ShapeDtypeStruct((capacity, 2, nin, nin), jnp.bfloat16),
        grid=(capacity // slots,),
        in_specs=in_specs,
        out_specs=pl.BlockSpec((slots, 2, nin, nin), lambda s: (s, 0, 0, 0)),
        scratch_shapes=[
            pltpu.VMEM((2 * nin, 3 * LANES), jnp.bfloat16),
            pltpu.VMEM((3 * LANES, nin), jnp.bfloat16),
        ]
        * slots,
        compiler_params=pltpu.CompilerParams(vmem_limit_bytes=60 * MIB),
        cost_estimate=pl.CostEstimate(
            flops=capacity * 8 * nin * nin * 256,
            bytes_accessed=capacity * (4 * nin * nin + 8 * nin * SPEC),
            transcendentals=0,
        ),
        name="correlate",
    )(factor, used, *received)


def exchange(block):
    return lax.all_to_all(block, "feed", split_axis=0, concat_axis=0, tiled=True)


def channel_tables(owners, dropped_channels):
    channels = jnp.arange(BAND, dtype=jnp.int32)[:, None]
    names = jnp.concatenate([owners, dropped_channels])[None, :]
    entry = jnp.arange(names.shape[1], dtype=jnp.int32)[None, :]
    earlier = (entry < channels) & (names == owners[:, None])
    flagged = (entry >= BAND) & (names == channels)
    total = jnp.sum(jnp.where(flagged, BAND, earlier.astype(jnp.int32)), axis=1)
    return total % BAND, total >= BAND


def local_blocks(samples, fir_taps, owner_map, dropped_channels):
    devices = lax.axis_size("feed")
    capacity = BAND // devices + BAND // (2 * devices)
    in_local = samples.shape[0]
    owners = owner_map[:, 0]
    ranks, dead = channel_tables(owners, dropped_channels)
    call = functools.partial(
        spectra_call,
        table=jnp.asarray(folded_table()),
        owners=owners,
        ranks=ranks,
        dead=dead,
        fir_taps=fir_taps,
        samples=jnp.transpose(samples, (1, 0, 2)),
        devices=devices,
    )
    block_a, power = call(0, FIRST, None)
    received_a = exchange(block_a)
    (block_b,) = call(FIRST, SPEC - FIRST, power)
    block_b, received_a = lax.optimization_barrier((block_b, received_a))
    received_b = exchange(block_b)

    kept = jnp.sum(jnp.logical_not(dead).astype(jnp.float32))
    mine = (owners == lax.axis_index("feed")) & jnp.logical_not(dead)
    slots = jnp.arange(capacity, dtype=jnp.int32)
    used = jnp.any((ranks[None, :] == slots[:, None]) & mine[None, :], axis=1).astype(jnp.int32)
    mean_power = jnp.sum(received_b[:, -8:]) / (NIN * SPEC * kept)
    factor = jnp.reshape(1.0 / (SPEC * mean_power), (1,))
    widths = [block.shape[1] // capacity for block in (block_a, block_b)]
    return correlate_call(
        [received_a, received_b], widths, capacity, used, factor, in_local, slots=2
    )


def solution(mesh):
    in_local = NIN // mesh.shape["feed"]
    blocks = in_local * 4 == LANES
    return jax.shard_map(
        local_blocks if blocks else local_plain,
        mesh=mesh,
        in_specs=(P("feed", "grp", None), P(), P(), P("grp")),
        out_specs=P(("grp", "feed"), None, None, None),
        check_vma=False,
    )
```

```python
import functools
import math

import jax
import jax.numpy as jnp
import ml_dtypes
import numpy as np
from jax import lax
from jax.experimental import pallas as pl
from jax.experimental.pallas import tpu as pltpu
from jax.sharding import PartitionSpec as P

NIN = 512
NFFT = 8192
HALF = NFFT // 2
BAND = 256
BAND_START = 1536
SPEC = 48
FIRST = 16
KB = 256
LANES = 128
MIB = 1 << 20


def dft_table(length, first, width):
    row_ids = lax.broadcasted_iota(jnp.int32, (length, width), 0)
    chan_ids = first + lax.broadcasted_iota(jnp.int32, (length, width), 1)
    phase_int = row_ids * chan_ids % length
    angles = phase_int.astype(jnp.float32) * (2.0 * math.pi / length)
    return jnp.concatenate([jnp.cos(angles), -jnp.sin(angles)], axis=1)


def folded_table():
    n = np.arange(HALF, dtype=np.int64)
    tables = []
    for parity in range(2):
        chans = BAND_START + 2 * np.arange(BAND // 2, dtype=np.int64) + parity
        angles = (n[:, None] * chans[None, :] % NFFT) * (2.0 * math.pi / NFFT)
        full = np.concatenate([np.cos(angles), -np.sin(angles)], axis=1) / math.sqrt(NFFT)
        high = full.astype(np.float32).astype(ml_dtypes.bfloat16)
        low = (full - high.astype(np.float64)).astype(np.float32).astype(ml_dtypes.bfloat16)
        tables.append(np.stack([high, low]))
    return np.stack(tables)


def slot_tables(owner_map, dropped_channels, capacity, slot_total):
    owners = owner_map[:, 0]
    channels = jnp.arange(owners.shape[0], dtype=jnp.int32)
    same_owner = (owners[:, None] == owners[None, :]) & (channels[None, :] < channels[:, None])
    rank_in = jnp.sum(same_owner.astype(jnp.int32), axis=1)
    slot_of = owners * capacity + rank_in
    flagged = jnp.any(dropped_channels[:, None] == channels[None, :], axis=0)
    channel_live = jnp.logical_not(flagged)
    targets = jnp.arange(slot_total, dtype=jnp.int32)
    slot_hit = (slot_of[:, None] == targets[None, :]) & channel_live[:, None]
    chan_of = jnp.sum(slot_hit.astype(jnp.int32) * channels[:, None], axis=0)
    slot_used = jnp.any(slot_hit, axis=0)
    return (chan_of, slot_used, channel_live)


def window(block, fir_taps):
    taps = fir_taps.shape[0]
    spec_count = block.shape[1] - taps + 1
    summed = jnp.zeros((block.shape[0], spec_count, block.shape[2]), jnp.float32)
    for tap_index in range(taps):
        summed = summed + fir_taps[tap_index][None, None, :] * block[
            :, tap_index : tap_index + spec_count, :
        ].astype(jnp.float32)
    return summed


def pair_products(left, right):
    return jnp.einsum(
        "qis,qjs->qij",
        left,
        right,
        precision=lax.Precision.HIGHEST,
        preferred_element_type=jnp.float32,
    )


def correlate(received):
    columns = received[0]
    real_rows = columns[:, :, :SPEC]
    imag_rows = columns[:, :, SPEC:]
    rotated = jnp.concatenate([imag_rows, -real_rows], axis=2)
    real_vis = pair_products(columns, columns)
    imag_vis = pair_products(rotated, columns)
    return jnp.stack([real_vis, imag_vis], axis=1)


def local_plain(samples, fir_taps, owner_map, dropped_channels):
    devices = lax.axis_size("feed")
    capacity = BAND // devices + BAND // (2 * devices)
    slot_total = devices * capacity
    in_local = samples.shape[0]
    dft_scale = 1.0 / math.sqrt(NFFT)
    chan_of, slot_used, channel_live = slot_tables(
        owner_map, dropped_channels, capacity, slot_total
    )
    live_mask = channel_live.astype(jnp.float32)
    kept = jnp.sum(live_mask)
    windowed = window(samples, fir_taps).reshape(in_local * SPEC, NFFT)
    table = dft_table(NFFT, BAND_START, BAND)
    spectra = (
        jnp.dot(
            windowed, table, precision=lax.Precision.HIGHEST, preferred_element_type=jnp.float32
        )
        * dft_scale
    )
    spectra = spectra.reshape(in_local, SPEC, 2, BAND)
    chosen = jnp.take(spectra, chan_of, axis=3) * slot_used.astype(jnp.float32)[None, None, None, :]
    outgoing = jnp.transpose(chosen, (3, 0, 2, 1)).reshape(devices, capacity, in_local, 2 * SPEC)
    raw_vis = correlate(lax.all_to_all(outgoing, "feed", split_axis=0, concat_axis=2, tiled=True))
    local_power = jnp.sum(jnp.trace(raw_vis[:, 0], axis1=1, axis2=2))
    power = lax.psum(local_power, "feed")
    mean_power = power / (NIN * SPEC * kept)
    factor = 1.0 / (SPEC * mean_power)
    return (raw_vis * factor).astype(jnp.bfloat16)


def split(value):
    high = value.astype(jnp.bfloat16)
    return high, (value - high.astype(jnp.float32)).astype(jnp.bfloat16)


def spectra_kernel(count, last, devices, message, taps, in_local, *refs):
    row_ref, taps_a, taps_b, frames_a, frames_b, table_a, table_b, table_last = refs[:8]
    if last:
        before, out = refs[8:10]
    else:
        out, power_out = refs[8:10]
    even_0, odd_0, even_1, odd_1, acc, flat = refs[10:]
    step = pl.program_id(0)
    rows = count * in_local

    def window_piece(block, tile, begin, even, odd):
            lanes = slice(block * KB + tile * LANES, block * KB + (tile + 1) * LANES)
            coef_a = [taps_a[t : t + 1, lanes] for t in range(taps)]
            coef_b = [taps_b[t : t + 1, lanes] for t in range(taps)]
            for first in range(0, in_local, 16):

                def load(ref, f):
                    return ref[f, first : first + 16, lanes].astype(jnp.float32)

                held_a = [load(frames_a, begin + f) for f in range(taps - 1)]
                held_b = [load(frames_b, begin + f) for f in range(taps - 1)]
                for s in range(begin, begin + 8):
                    held_a.append(load(frames_a, s + taps - 1))
                    held_b.append(load(frames_b, s + taps - 1))
                    near = sum(c * x for c, x in zip(coef_a[1:], held_a[1:])) + coef_a[0] * held_a[0]
                    far = sum(c * x for c, x in zip(coef_b[1:], held_b[1:])) + coef_b[0] * held_b[0]
                    at = slice(s * in_local + first, s * in_local + first + 16)
                    for ref, value in ((even, near + far), (odd, near - far)):
                        high, low = split(value)
                        ref[at, tile * LANES : (tile + 1) * LANES] = high
                        ref[at, KB + tile * LANES : KB + (tile + 1) * LANES] = low
                    held_a, held_b = held_a[1:], held_b[1:]

    def matmul_piece(table, parity, start, ref):
        cols = slice(parity * BAND, (parity + 1) * BAND)
        at = slice(start, start + 256)
        right = jnp.concatenate([table[parity, 0], table[parity, 0], table[parity, 1]], axis=0)
        left = jnp.concatenate([ref[at, :], ref[at, :KB]], axis=1)
        acc[at, cols] += jnp.dot(left, right, preferred_element_type=jnp.float32)

    def matmul_pieces(table, even, odd):
        return [
            functools.partial(matmul_piece, table, parity, start, ref)
            for parity, ref in enumerate((even, odd))
            for start in range(0, rows, 256)
        ]

    def window_pieces(block, even, odd):
        return [
            functools.partial(window_piece, block, tile, begin, even, odd)
            for tile in range(KB // LANES)
            for begin in range(0, count, 8)
        ]

    def alternate(left, right):
        for one, other in zip(left, right, strict=True):
            one()
            other()

    @pl.when(step == 0)
    def _():
        even_1[...] = jnp.zeros_like(even_1)
        odd_1[...] = jnp.zeros_like(odd_1)
        acc[...] = jnp.zeros_like(acc)

    alternate(matmul_pieces(table_b, even_1, odd_1), window_pieces(0, even_0, odd_0))
    alternate(matmul_pieces(table_a, even_0, odd_0), window_pieces(1, even_1, odd_1))

    @pl.when(step == pl.num_programs(0) - 1)
    def _():
        for piece in matmul_pieces(table_last, even_1, odd_1):
            piece()
        width = rows // LANES
        for parity in range(2):
            for part in range(2):
                cols = slice(parity * BAND + part * LANES, parity * BAND + (part + 1) * LANES)
                for g in range(width):
                    turned = acc[g * LANES : (g + 1) * LANES, cols].T
                    row = (parity * 2 + part) * width + g
                    flat[pl.ds(row, LANES, stride=4 * width), :] = turned
        size = 2 * width

        def place(c, total):
            value = flat[pl.ds(pl.multiple_of(c * size, size), size), :]
            row = row_ref[c]

            @pl.when(row >= 0)
            def _():
                out[pl.ds(pl.multiple_of(row * 8, 8), size), :] = value

            square = sum(value[start : start + 8] ** 2 for start in range(0, size, 8))
            return total + (row >= 0).astype(jnp.float32) * square

        total = lax.fori_loop(0, BAND, place, jnp.zeros((8, LANES), jnp.float32), unroll=8)
        if last:
            total = total + before[...]
            for d in range(devices):
                out[(d + 1) * message - 8 : (d + 1) * message, :] = total
        else:
            power_out[...] = total


def spectra_call(first, count, before, table, owners, ranks, dead, fir_taps, samples, devices):
    _, in_local, _ = samples.shape
    taps = fir_taps.shape[0]
    step_size = 2 * KB
    steps = HALF // step_size
    last = before is not None
    rows = count * in_local
    width = 2 * rows // LANES
    capacity = BAND // devices + BAND // (2 * devices)
    message = capacity * width + 8 * last
    row_of = jnp.where(dead, -1, owners * (message // 8) + ranks * (width // 8))

    def frames_spec(offset):
        return pl.BlockSpec(
            (pl.Element(count + taps - 1), pl.Element(in_local), pl.Element(step_size)),
            lambda j, *_: (first, 0, pl.multiple_of((j + offset) * step_size, step_size)),
        )

    def taps_spec(offset):
        return pl.BlockSpec((taps, step_size), lambda j, *_: (0, j + offset))

    def table_spec(index):
        return pl.BlockSpec((2, 2, KB, BAND), lambda j, *_: (0, 0, index(j), 0))

    block = jax.ShapeDtypeStruct((devices * message, LANES), jnp.float32)
    power = jax.ShapeDtypeStruct((8, LANES), jnp.float32)
    whole = [pl.BlockSpec(block.shape, lambda j, *_: (0, 0))]
    single = [pl.BlockSpec(power.shape, lambda j, *_: (0, 0))]
    grid_spec = pltpu.PrefetchScalarGridSpec(
        num_scalar_prefetch=1,
        grid=(steps,),
        in_specs=[
            taps_spec(0),
            taps_spec(steps),
            frames_spec(0),
            frames_spec(steps),
            table_spec(lambda j: 2 * j),
            table_spec(lambda j: jnp.maximum(2 * j - 1, 0)),
            table_spec(lambda j: 2 * steps - 1),
        ]
        + (single if last else []),
        out_specs=whole + ([] if last else single),
        scratch_shapes=[pltpu.VMEM((rows, 2 * KB), jnp.bfloat16)] * 4
        + [
            pltpu.VMEM((rows, 2 * BAND), jnp.float32),
            pltpu.VMEM((BAND * width, LANES), jnp.float32),
        ],
    )
    sent, *rest = pl.pallas_call(
        functools.partial(spectra_kernel, count, last, devices, message, taps, in_local),
        out_shape=[block] + ([] if last else [power]),
        grid_spec=grid_spec,
        compiler_params=pltpu.CompilerParams(vmem_limit_bytes=60 * MIB),
        cost_estimate=pl.CostEstimate(
            flops=3 * 2 * rows * HALF * 2 * BAND, bytes_accessed=30 * MIB, transcendentals=0
        ),
        name="spectra",
    )(
        row_of,
        fir_taps,
        fir_taps,
        samples,
        samples,
        table,
        table,
        table,
        *([before] if last else []),
    )
    return [sent.reshape(devices, message, LANES)] + rest


def exchange_lanes(values, in_local):
    count = len(values)
    lane = lax.broadcasted_iota(jnp.int32, values[0].shape, 1) // in_local
    values = list(values)
    distance = count // 2
    while distance:
        upper = (lane & distance) != 0
        shift = distance * in_local
        for a in range(count):
            if a & distance:
                continue
            x, y = values[a], values[a + distance]
            values[a] = jnp.where(upper, pltpu.roll(y, shift, 1), x)
            values[a + distance] = jnp.where(upper, y, pltpu.roll(x, LANES - shift, 1))
        distance //= 2
    return values


def correlate_kernel(widths, in_local, factor_ref, used_ref, *refs):
    groups = refs[: len(widths)]
    out, left_0, right_0, left_1, right_1, staged, sems = refs[len(widths) :]
    step, last = pl.program_id(0), pl.num_programs(0) - 1
    per_tile = LANES // in_local
    blocks = groups[0].shape[0] // per_tile
    nin = groups[0].shape[0] * in_local
    factor = factor_ref[0]
    upper = lax.broadcasted_iota(jnp.int32, (8, LANES), 0) >= 4

    def prepare(slot, left, right, block):
        used = used_ref[2 * step + slot] != 0
        straight, turned = [], []
        for ref, width in zip(groups, widths):
            tiles = []
            for start in range(slot * width, (slot + 1) * width, 8):
                mixed = [
                    jnp.where(used, ref[block * per_tile + a, start : start + 8], 0.0)
                    for a in range(per_tile)
                ]
                tiles.append(exchange_lanes(mixed, in_local))
            for q in range(per_tile):
                column = [t[q] for t in tiles]
                straight += column
                if len(column) == 1:
                    swapped = pltpu.roll(column[0], 4, 0)
                    turned.append(jnp.where(upper, swapped, -swapped))
                else:
                    half = len(column) // 2
                    turned += [-t for t in column[half:]] + column[:half]
        pad = [jnp.zeros((LANES - 8 * len(straight), LANES), jnp.float32)]
        columns = jnp.concatenate(straight + pad, axis=0)
        for part, value in enumerate((columns, jnp.concatenate(turned + pad, axis=0))):
            high, low = split(value)
            lanes = slice(part * nin + block * LANES, part * nin + (block + 1) * LANES)
            right[:LANES, lanes] = high
            right[LANES : 2 * LANES, lanes] = high
            right[2 * LANES :, lanes] = low
        high, low = split(columns.T)
        at = slice(block * LANES, (block + 1) * LANES)
        left[at, :LANES] = high
        left[at, LANES : 2 * LANES] = low
        left[at, 2 * LANES :] = high

    def multiply(slot, left, right, block):
        size = 2 * nin // blocks
        total = jnp.dot(
            left[...],
            right[:, block * size : (block + 1) * size],
            preferred_element_type=jnp.float32,
        )
        start = block * size % nin
        staged[slot, block * size // nin, :, start : start + size] = (total * factor).astype(
            jnp.bfloat16
        )

    def copy(slot, index):
        return pltpu.make_async_copy(staged.at[slot], out.at[index], sems.at[slot])

    @pl.when(step >= 2)
    def _():
        copy(1, 2 * step - 3).wait()

    for block in range(blocks):
        multiply(1, left_1, right_1, block)
        prepare(0, left_0, right_0, block)

    @pl.when(step >= 1)
    def _():
        copy(1, 2 * step - 1).start()
        copy(0, 2 * step - 2).wait()

    for block in range(blocks):
        multiply(0, left_0, right_0, block)
        prepare(1, left_1, right_1, block)

    copy(0, 2 * step).start()

    @pl.when(step == last)
    def _():
        copy(1, 2 * step - 1).wait()
        for block in range(blocks):
            multiply(1, left_1, right_1, block)
        copy(1, 2 * step + 1).start()
        copy(0, 2 * step).wait()
        copy(1, 2 * step + 1).wait()


def correlate_call(received, widths, capacity, used, factor, in_local):
    sources = received[0].shape[0]
    nin = sources * in_local
    in_specs = [
        pl.BlockSpec(memory_space=pltpu.SMEM),
        pl.BlockSpec(memory_space=pltpu.SMEM),
    ] + [pl.BlockSpec((sources, 2 * width, LANES), lambda s: (0, s, 0)) for width in widths]
    return pl.pallas_call(
        functools.partial(correlate_kernel, widths, in_local),
        out_shape=jax.ShapeDtypeStruct((capacity, 2, nin, nin), jnp.bfloat16),
        grid=(capacity // 2,),
        in_specs=in_specs,
        out_specs=pl.BlockSpec(memory_space=pl.ANY),
        scratch_shapes=[
            pltpu.VMEM((nin, 3 * LANES), jnp.bfloat16),
            pltpu.VMEM((3 * LANES, 2 * nin), jnp.bfloat16),
        ]
        * 2
        + [pltpu.VMEM((2, 2, nin, nin), jnp.bfloat16), pltpu.SemaphoreType.DMA((2,))],
        compiler_params=pltpu.CompilerParams(vmem_limit_bytes=60 * MIB),
        cost_estimate=pl.CostEstimate(
            flops=capacity * 8 * nin * nin * 256,
            bytes_accessed=capacity * (4 * nin * nin + 8 * nin * SPEC),
            transcendentals=0,
        ),
        name="correlate",
    )(factor, used, *received)


def exchange(block):
    return lax.all_to_all(block, "feed", split_axis=0, concat_axis=0, tiled=True)


def channel_tables(owners, dropped_channels):
    channels = jnp.arange(BAND, dtype=jnp.int32)[:, None]
    names = jnp.concatenate([owners, dropped_channels])[None, :]
    entry = jnp.arange(names.shape[1], dtype=jnp.int32)[None, :]
    earlier = (entry < channels) & (names == owners[:, None])
    flagged = (entry >= BAND) & (names == channels)
    total = jnp.sum(jnp.where(flagged, BAND, earlier.astype(jnp.int32)), axis=1)
    return total % BAND, total >= BAND


def local_blocks(samples, fir_taps, owner_map, dropped_channels):
    devices = lax.axis_size("feed")
    capacity = BAND // devices + BAND // (2 * devices)
    in_local = samples.shape[0]
    owners = owner_map[:, 0]
    ranks, dead = channel_tables(owners, dropped_channels)
    call = functools.partial(
        spectra_call,
        table=jnp.asarray(folded_table()),
        owners=owners,
        ranks=ranks,
        dead=dead,
        fir_taps=fir_taps,
        samples=jnp.transpose(samples, (1, 0, 2)),
        devices=devices,
    )
    block_a, power = call(0, FIRST, None)
    received_a = exchange(block_a)
    (block_b,) = call(FIRST, SPEC - FIRST, power)
    block_b, received_a = lax.optimization_barrier((block_b, received_a))
    received_b = exchange(block_b)

    kept = jnp.sum(jnp.logical_not(dead).astype(jnp.float32))
    mine = (owners == lax.axis_index("feed")) & jnp.logical_not(dead)
    slots = jnp.arange(capacity, dtype=jnp.int32)
    used = jnp.any((ranks[None, :] == slots[:, None]) & mine[None, :], axis=1).astype(jnp.int32)
    mean_power = jnp.sum(received_b[:, -8:]) / (NIN * SPEC * kept)
    factor = jnp.reshape(1.0 / (SPEC * mean_power), (1,))
    widths = [block.shape[1] // capacity for block in (block_a, block_b)]
    return correlate_call(
        [received_a, received_b], widths, capacity, used, factor, in_local
    )


def solution(mesh):
    in_local = NIN // mesh.shape["feed"]
    blocks = in_local * 4 == LANES
    return jax.shard_map(
        local_blocks if blocks else local_plain,
        mesh=mesh,
        in_specs=(P("feed", "grp", None), P(), P(), P("grp")),
        out_specs=P(("grp", "feed"), None, None, None),
        check_vma=False,
    )
```

```python
import functools
import math

import jax
import jax.numpy as jnp
import ml_dtypes
import numpy as np
from jax import lax
from jax.experimental import pallas as pl
from jax.experimental.pallas import tpu as pltpu
from jax.sharding import PartitionSpec as P

NIN = 512
NFFT = 8192
HALF = NFFT // 2
BAND = 256
BAND_START = 1536
SPEC = 48
FIRST = 16
KB = 256
LANES = 128
MIB = 1 << 20


def dft_table(length, first, width):
    row_ids = lax.broadcasted_iota(jnp.int32, (length, width), 0)
    chan_ids = first + lax.broadcasted_iota(jnp.int32, (length, width), 1)
    phase_int = row_ids * chan_ids % length
    angles = phase_int.astype(jnp.float32) * (2.0 * math.pi / length)
    return jnp.concatenate([jnp.cos(angles), -jnp.sin(angles)], axis=1)


def folded_table():
    n = np.arange(HALF, dtype=np.int64)
    tables = []
    for parity in range(2):
        chans = BAND_START + 2 * np.arange(BAND // 2, dtype=np.int64) + parity
        angles = (n[:, None] * chans[None, :] % NFFT) * (2.0 * math.pi / NFFT)
        full = np.stack([np.cos(angles), -np.sin(angles)]) / math.sqrt(NFFT)
        high = full.astype(np.float32).astype(ml_dtypes.bfloat16)
        low = (full - high.astype(np.float64)).astype(np.float32).astype(ml_dtypes.bfloat16)
        tables.append(np.stack([high, low]))
    return np.stack(tables)


def slot_tables(owner_map, dropped_channels, capacity, slot_total):
    owners = owner_map[:, 0]
    channels = jnp.arange(owners.shape[0], dtype=jnp.int32)
    same_owner = (owners[:, None] == owners[None, :]) & (channels[None, :] < channels[:, None])
    rank_in = jnp.sum(same_owner.astype(jnp.int32), axis=1)
    slot_of = owners * capacity + rank_in
    flagged = jnp.any(dropped_channels[:, None] == channels[None, :], axis=0)
    channel_live = jnp.logical_not(flagged)
    targets = jnp.arange(slot_total, dtype=jnp.int32)
    slot_hit = (slot_of[:, None] == targets[None, :]) & channel_live[:, None]
    chan_of = jnp.sum(slot_hit.astype(jnp.int32) * channels[:, None], axis=0)
    slot_used = jnp.any(slot_hit, axis=0)
    return (chan_of, slot_used, channel_live)


def window(block, fir_taps):
    taps = fir_taps.shape[0]
    spec_count = block.shape[1] - taps + 1
    summed = jnp.zeros((block.shape[0], spec_count, block.shape[2]), jnp.float32)
    for tap_index in range(taps):
        summed = summed + fir_taps[tap_index][None, None, :] * block[
            :, tap_index : tap_index + spec_count, :
        ].astype(jnp.float32)
    return summed


def pair_products(left, right):
    return jnp.einsum(
        "qis,qjs->qij",
        left,
        right,
        precision=lax.Precision.HIGHEST,
        preferred_element_type=jnp.float32,
    )


def correlate(received):
    columns = received[0]
    real_rows = columns[:, :, :SPEC]
    imag_rows = columns[:, :, SPEC:]
    rotated = jnp.concatenate([imag_rows, -real_rows], axis=2)
    real_vis = pair_products(columns, columns)
    imag_vis = pair_products(rotated, columns)
    return jnp.stack([real_vis, imag_vis], axis=1)


def local_plain(samples, fir_taps, owner_map, dropped_channels):
    devices = lax.axis_size("feed")
    capacity = BAND // devices + BAND // (2 * devices)
    slot_total = devices * capacity
    in_local = samples.shape[0]
    dft_scale = 1.0 / math.sqrt(NFFT)
    chan_of, slot_used, channel_live = slot_tables(
        owner_map, dropped_channels, capacity, slot_total
    )
    live_mask = channel_live.astype(jnp.float32)
    kept = jnp.sum(live_mask)
    windowed = window(samples, fir_taps).reshape(in_local * SPEC, NFFT)
    table = dft_table(NFFT, BAND_START, BAND)
    spectra = (
        jnp.dot(
            windowed, table, precision=lax.Precision.HIGHEST, preferred_element_type=jnp.float32
        )
        * dft_scale
    )
    spectra = spectra.reshape(in_local, SPEC, 2, BAND)
    chosen = jnp.take(spectra, chan_of, axis=3) * slot_used.astype(jnp.float32)[None, None, None, :]
    outgoing = jnp.transpose(chosen, (3, 0, 2, 1)).reshape(devices, capacity, in_local, 2 * SPEC)
    raw_vis = correlate(lax.all_to_all(outgoing, "feed", split_axis=0, concat_axis=2, tiled=True))
    local_power = jnp.sum(jnp.trace(raw_vis[:, 0], axis1=1, axis2=2))
    power = lax.psum(local_power, "feed")
    mean_power = power / (NIN * SPEC * kept)
    factor = 1.0 / (SPEC * mean_power)
    return (raw_vis * factor).astype(jnp.bfloat16)


def split(value):
    high = value.astype(jnp.bfloat16)
    return high, (value - high.astype(jnp.float32)).astype(jnp.bfloat16)


def spectra_kernel(count, last, devices, message, taps, in_local, *refs):
    row_ref, taps_a, taps_b, frames_a, frames_b, table_a, table_b, table_last = refs[:8]
    if last:
        before, out = refs[8:10]
    else:
        out, power_out = refs[8:10]
    even_0, odd_0, even_1, odd_1, acc, flat = refs[10:]
    step = pl.program_id(0)
    rows = count * in_local

    def window_piece(block, tile, begin, even, odd):
            lanes = slice(block * KB + tile * LANES, block * KB + (tile + 1) * LANES)
            coef_a = [taps_a[t : t + 1, lanes] for t in range(taps)]
            coef_b = [taps_b[t : t + 1, lanes] for t in range(taps)]
            for first in range(0, in_local, 16):

                def load(ref, f):
                    return ref[f, first : first + 16, lanes].astype(jnp.float32)

                held_a = [load(frames_a, begin + f) for f in range(taps - 1)]
                held_b = [load(frames_b, begin + f) for f in range(taps - 1)]
                for s in range(begin, begin + 8):
                    held_a.append(load(frames_a, s + taps - 1))
                    held_b.append(load(frames_b, s + taps - 1))
                    near = sum(c * x for c, x in zip(coef_a[1:], held_a[1:])) + coef_a[0] * held_a[0]
                    far = sum(c * x for c, x in zip(coef_b[1:], held_b[1:])) + coef_b[0] * held_b[0]
                    at = slice(s * in_local + first, s * in_local + first + 16)
                    for ref, value in ((even, near + far), (odd, near - far)):
                        ref[0, tile, at, :], ref[1, tile, at, :] = split(value)
                    held_a, held_b = held_a[1:], held_b[1:]

    def matmul_piece(table, parity, start, ref):
        cols = slice(parity * BAND, (parity + 1) * BAND)
        at = slice(start, start + 256)
        tall = [
            jnp.concatenate([table[parity, part, 0], table[parity, part, 1]], axis=1)
            for part in range(2)
        ]
        right = jnp.concatenate([tall[0], tall[0], tall[1]], axis=0)
        wide = [ref[part, tile, at, :] for part in (0, 1, 0) for tile in range(KB // LANES)]
        left = jnp.concatenate(wide, axis=1)
        acc[at, cols] += jnp.dot(left, right, preferred_element_type=jnp.float32)

    def matmul_pieces(table, even, odd):
        return [
            functools.partial(matmul_piece, table, parity, start, ref)
            for parity, ref in enumerate((even, odd))
            for start in range(0, rows, 256)
        ]

    def window_pieces(block, even, odd):
        return [
            functools.partial(window_piece, block, tile, begin, even, odd)
            for tile in range(KB // LANES)
            for begin in range(0, count, 8)
        ]

    def alternate(left, right):
        for one, other in zip(left, right, strict=True):
            one()
            other()

    @pl.when(step == 0)
    def _():
        even_1[...] = jnp.zeros_like(even_1)
        odd_1[...] = jnp.zeros_like(odd_1)
        acc[...] = jnp.zeros_like(acc)

    alternate(matmul_pieces(table_b, even_1, odd_1), window_pieces(0, even_0, odd_0))
    alternate(matmul_pieces(table_a, even_0, odd_0), window_pieces(1, even_1, odd_1))

    @pl.when(step == pl.num_programs(0) - 1)
    def _():
        for piece in matmul_pieces(table_last, even_1, odd_1):
            piece()
        width = rows // LANES
        for parity in range(2):
            for part in range(2):
                cols = slice(parity * BAND + part * LANES, parity * BAND + (part + 1) * LANES)
                for g in range(width):
                    turned = acc[g * LANES : (g + 1) * LANES, cols].T
                    row = (parity * 2 + part) * width + g
                    flat[pl.ds(row, LANES, stride=4 * width), :] = turned
        size = 2 * width

        def place(c, total):
            value = flat[pl.ds(pl.multiple_of(c * size, size), size), :]
            row = row_ref[c]

            @pl.when(row >= 0)
            def _():
                out[pl.ds(pl.multiple_of(row * 8, 8), size), :] = value

            square = sum(value[start : start + 8] ** 2 for start in range(0, size, 8))
            return total + (row >= 0).astype(jnp.float32) * square

        total = lax.fori_loop(0, BAND, place, jnp.zeros((8, LANES), jnp.float32), unroll=8)
        if last:
            total = total + before[...]
            for d in range(devices):
                out[(d + 1) * message - 8 : (d + 1) * message, :] = total
        else:
            power_out[...] = total


def spectra_call(first, count, before, table, owners, ranks, dead, fir_taps, samples, devices):
    _, in_local, _ = samples.shape
    taps = fir_taps.shape[0]
    step_size = 2 * KB
    steps = HALF // step_size
    last = before is not None
    rows = count * in_local
    width = 2 * rows // LANES
    capacity = BAND // devices + BAND // (2 * devices)
    message = capacity * width + 8 * last
    row_of = jnp.where(dead, -1, owners * (message // 8) + ranks * (width // 8))

    def frames_spec(offset):
        return pl.BlockSpec(
            (pl.Element(count + taps - 1), pl.Element(in_local), pl.Element(step_size)),
            lambda j, *_: (first, 0, pl.multiple_of((j + offset) * step_size, step_size)),
        )

    def taps_spec(offset):
        return pl.BlockSpec((taps, step_size), lambda j, *_: (0, j + offset))

    def table_spec(index):
        return pl.BlockSpec((2, 2, 2, KB, LANES), lambda j, *_: (0, 0, 0, index(j), 0))

    block = jax.ShapeDtypeStruct((devices * message, LANES), jnp.float32)
    power = jax.ShapeDtypeStruct((8, LANES), jnp.float32)
    whole = [pl.BlockSpec(block.shape, lambda j, *_: (0, 0))]
    single = [pl.BlockSpec(power.shape, lambda j, *_: (0, 0))]
    grid_spec = pltpu.PrefetchScalarGridSpec(
        num_scalar_prefetch=1,
        grid=(steps,),
        in_specs=[
            taps_spec(0),
            taps_spec(steps),
            frames_spec(0),
            frames_spec(steps),
            table_spec(lambda j: 2 * j),
            table_spec(lambda j: jnp.maximum(2 * j - 1, 0)),
            table_spec(lambda j: 2 * steps - 1),
        ]
        + (single if last else []),
        out_specs=whole + ([] if last else single),
        scratch_shapes=[pltpu.VMEM((2, KB // LANES, rows, LANES), jnp.bfloat16)] * 4
        + [
            pltpu.VMEM((rows, 2 * BAND), jnp.float32),
            pltpu.VMEM((BAND * width, LANES), jnp.float32),
        ],
    )
    sent, *rest = pl.pallas_call(
        functools.partial(spectra_kernel, count, last, devices, message, taps, in_local),
        out_shape=[block] + ([] if last else [power]),
        grid_spec=grid_spec,
        compiler_params=pltpu.CompilerParams(vmem_limit_bytes=60 * MIB),
        cost_estimate=pl.CostEstimate(
            flops=3 * 2 * rows * HALF * 2 * BAND, bytes_accessed=30 * MIB, transcendentals=0
        ),
        name="spectra",
    )(
        row_of,
        fir_taps,
        fir_taps,
        samples,
        samples,
        table,
        table,
        table,
        *([before] if last else []),
    )
    return [sent.reshape(devices, message, LANES)] + rest


def exchange_lanes(values, in_local):
    count = len(values)
    lane = lax.broadcasted_iota(jnp.int32, values[0].shape, 1) // in_local
    values = list(values)
    distance = count // 2
    while distance:
        upper = (lane & distance) != 0
        shift = distance * in_local
        for a in range(count):
            if a & distance:
                continue
            x, y = values[a], values[a + distance]
            values[a] = jnp.where(upper, pltpu.roll(y, shift, 1), x)
            values[a + distance] = jnp.where(upper, y, pltpu.roll(x, LANES - shift, 1))
        distance //= 2
    return values


def correlate_kernel(widths, in_local, factor_ref, used_ref, *refs):
    groups = refs[: len(widths)]
    out, left_0, right_0, left_1, right_1, staged, sems = refs[len(widths) :]
    step, last = pl.program_id(0), pl.num_programs(0) - 1
    per_tile = LANES // in_local
    blocks = groups[0].shape[0] // per_tile
    nin = groups[0].shape[0] * in_local
    factor = factor_ref[0]
    upper = lax.broadcasted_iota(jnp.int32, (8, LANES), 0) >= 4

    def prepare(slot, left, right, block):
        used = used_ref[2 * step + slot] != 0
        straight, turned = [], []
        for ref, width in zip(groups, widths):
            tiles = []
            for start in range(slot * width, (slot + 1) * width, 8):
                mixed = [
                    jnp.where(used, ref[block * per_tile + a, start : start + 8], 0.0)
                    for a in range(per_tile)
                ]
                tiles.append(exchange_lanes(mixed, in_local))
            for q in range(per_tile):
                column = [t[q] for t in tiles]
                straight += column
                if len(column) == 1:
                    swapped = pltpu.roll(column[0], 4, 0)
                    turned.append(jnp.where(upper, swapped, -swapped))
                else:
                    half = len(column) // 2
                    turned += [-t for t in column[half:]] + column[:half]
        pad = [jnp.zeros((LANES - 8 * len(straight), LANES), jnp.float32)]
        columns = jnp.concatenate(straight + pad, axis=0)
        for part, value in enumerate((columns, jnp.concatenate(turned + pad, axis=0))):
            right[0, part * blocks + block], right[1, part * blocks + block] = split(value)
        at = slice(block * LANES, (block + 1) * LANES)
        left[0, at, :], left[1, at, :] = split(columns.T)

    def multiply(slot, left, right, part):
        wide = [
            jnp.concatenate([right[k, part * blocks + b] for b in range(blocks)], axis=1)
            for k in range(2)
        ]
        total = jnp.dot(
            jnp.concatenate([left[0], left[1], left[0]], axis=1),
            jnp.concatenate([wide[0], wide[0], wide[1]], axis=0),
            preferred_element_type=jnp.float32,
        )
        staged[slot, part] = (total * factor).astype(jnp.bfloat16)

    def copy(slot, index):
        return pltpu.make_async_copy(staged.at[slot], out.at[index], sems.at[slot])

    @pl.when(step >= 2)
    def _():
        copy(1, 2 * step - 3).wait()

    for part in range(2):
        multiply(1, left_1, right_1, part)
        for block in range(part * blocks // 2, (part + 1) * blocks // 2):
            prepare(0, left_0, right_0, block)

    @pl.when(step >= 1)
    def _():
        copy(1, 2 * step - 1).start()
        copy(0, 2 * step - 2).wait()

    for part in range(2):
        multiply(0, left_0, right_0, part)
        for block in range(part * blocks // 2, (part + 1) * blocks // 2):
            prepare(1, left_1, right_1, block)

    copy(0, 2 * step).start()

    @pl.when(step == last)
    def _():
        copy(1, 2 * step - 1).wait()
        for part in range(2):
            multiply(1, left_1, right_1, part)
        copy(1, 2 * step + 1).start()
        copy(0, 2 * step).wait()
        copy(1, 2 * step + 1).wait()


def correlate_call(received, widths, capacity, used, factor, in_local):
    sources = received[0].shape[0]
    nin = sources * in_local
    in_specs = [
        pl.BlockSpec(memory_space=pltpu.SMEM),
        pl.BlockSpec(memory_space=pltpu.SMEM),
    ] + [pl.BlockSpec((sources, 2 * width, LANES), lambda s: (0, s, 0)) for width in widths]
    return pl.pallas_call(
        functools.partial(correlate_kernel, widths, in_local),
        out_shape=jax.ShapeDtypeStruct((capacity, 2, nin, nin), jnp.bfloat16),
        grid=(capacity // 2,),
        in_specs=in_specs,
        out_specs=pl.BlockSpec(memory_space=pl.ANY),
        scratch_shapes=[
            pltpu.VMEM((2, nin, LANES), jnp.bfloat16),
            pltpu.VMEM((2, 2 * nin // LANES, LANES, LANES), jnp.bfloat16),
        ]
        * 2
        + [pltpu.VMEM((2, 2, nin, nin), jnp.bfloat16), pltpu.SemaphoreType.DMA((2,))],
        compiler_params=pltpu.CompilerParams(vmem_limit_bytes=60 * MIB),
        cost_estimate=pl.CostEstimate(
            flops=capacity * 8 * nin * nin * 256,
            bytes_accessed=capacity * (4 * nin * nin + 8 * nin * SPEC),
            transcendentals=0,
        ),
        name="correlate",
    )(factor, used, *received)


def exchange(block):
    return lax.all_to_all(block, "feed", split_axis=0, concat_axis=0, tiled=True)


def channel_tables(owners, dropped_channels):
    channels = jnp.arange(BAND, dtype=jnp.int32)[:, None]
    names = jnp.concatenate([owners, dropped_channels])[None, :]
    entry = jnp.arange(names.shape[1], dtype=jnp.int32)[None, :]
    earlier = (entry < channels) & (names == owners[:, None])
    flagged = (entry >= BAND) & (names == channels)
    total = jnp.sum(jnp.where(flagged, BAND, earlier.astype(jnp.int32)), axis=1)
    return total % BAND, total >= BAND


def local_blocks(samples, fir_taps, owner_map, dropped_channels):
    devices = lax.axis_size("feed")
    capacity = BAND // devices + BAND // (2 * devices)
    in_local = samples.shape[0]
    owners = owner_map[:, 0]
    ranks, dead = channel_tables(owners, dropped_channels)
    call = functools.partial(
        spectra_call,
        table=jnp.asarray(folded_table()),
        owners=owners,
        ranks=ranks,
        dead=dead,
        fir_taps=fir_taps,
        samples=jnp.transpose(samples, (1, 0, 2)),
        devices=devices,
    )
    block_a, power = call(0, FIRST, None)
    received_a = exchange(block_a)
    (block_b,) = call(FIRST, SPEC - FIRST, power)
    block_b, received_a = lax.optimization_barrier((block_b, received_a))
    received_b = exchange(block_b)

    kept = jnp.sum(jnp.logical_not(dead).astype(jnp.float32))
    mine = (owners == lax.axis_index("feed")) & jnp.logical_not(dead)
    slots = jnp.arange(capacity, dtype=jnp.int32)
    used = jnp.any((ranks[None, :] == slots[:, None]) & mine[None, :], axis=1).astype(jnp.int32)
    mean_power = jnp.sum(received_b[:, -8:]) / (NIN * SPEC * kept)
    factor = jnp.reshape(1.0 / (SPEC * mean_power), (1,))
    widths = [block.shape[1] // capacity for block in (block_a, block_b)]
    return correlate_call(
        [received_a, received_b], widths, capacity, used, factor, in_local
    )


def solution(mesh):
    in_local = NIN // mesh.shape["feed"]
    blocks = in_local * 4 == LANES
    return jax.shard_map(
        local_blocks if blocks else local_plain,
        mesh=mesh,
        in_specs=(P("feed", "grp", None), P(), P(), P("grp")),
        out_specs=P(("grp", "feed"), None, None, None),
        check_vma=False,
    )
```

```python
import functools
import math

import jax
import jax.numpy as jnp
import ml_dtypes
import numpy as np
from jax import lax
from jax.experimental import pallas as pl
from jax.experimental.pallas import tpu as pltpu
from jax.sharding import PartitionSpec as P

NIN = 512
NFFT = 8192
HALF = NFFT // 2
BAND = 256
BAND_START = 1536
SPEC = 48
FIRST = 16
KB = 256
LANES = 128
STAGES = 4
MIB = 1 << 20


def dft_table(length, first, width):
    row_ids = lax.broadcasted_iota(jnp.int32, (length, width), 0)
    chan_ids = first + lax.broadcasted_iota(jnp.int32, (length, width), 1)
    phase_int = row_ids * chan_ids % length
    angles = phase_int.astype(jnp.float32) * (2.0 * math.pi / length)
    return jnp.concatenate([jnp.cos(angles), -jnp.sin(angles)], axis=1)


def folded_table():
    n = np.arange(HALF, dtype=np.int64)
    tables = []
    for parity in range(2):
        chans = BAND_START + 2 * np.arange(BAND // 2, dtype=np.int64) + parity
        angles = (n[:, None] * chans[None, :] % NFFT) * (2.0 * math.pi / NFFT)
        full = np.stack([np.cos(angles), -np.sin(angles)]) / math.sqrt(NFFT)
        high = full.astype(np.float32).astype(ml_dtypes.bfloat16)
        low = (full - high.astype(np.float64)).astype(np.float32).astype(ml_dtypes.bfloat16)
        tables.append(np.stack([high, low]))
    return np.stack(tables)


def slot_tables(owner_map, dropped_channels, capacity, slot_total):
    owners = owner_map[:, 0]
    channels = jnp.arange(owners.shape[0], dtype=jnp.int32)
    same_owner = (owners[:, None] == owners[None, :]) & (channels[None, :] < channels[:, None])
    rank_in = jnp.sum(same_owner.astype(jnp.int32), axis=1)
    slot_of = owners * capacity + rank_in
    flagged = jnp.any(dropped_channels[:, None] == channels[None, :], axis=0)
    channel_live = jnp.logical_not(flagged)
    targets = jnp.arange(slot_total, dtype=jnp.int32)
    slot_hit = (slot_of[:, None] == targets[None, :]) & channel_live[:, None]
    chan_of = jnp.sum(slot_hit.astype(jnp.int32) * channels[:, None], axis=0)
    slot_used = jnp.any(slot_hit, axis=0)
    return (chan_of, slot_used, channel_live)


def window(block, fir_taps):
    taps = fir_taps.shape[0]
    spec_count = block.shape[1] - taps + 1
    summed = jnp.zeros((block.shape[0], spec_count, block.shape[2]), jnp.float32)
    for tap_index in range(taps):
        summed = summed + fir_taps[tap_index][None, None, :] * block[
            :, tap_index : tap_index + spec_count, :
        ].astype(jnp.float32)
    return summed


def pair_products(left, right):
    return jnp.einsum(
        "qis,qjs->qij",
        left,
        right,
        precision=lax.Precision.HIGHEST,
        preferred_element_type=jnp.float32,
    )


def correlate(received):
    columns = received[0]
    real_rows = columns[:, :, :SPEC]
    imag_rows = columns[:, :, SPEC:]
    rotated = jnp.concatenate([imag_rows, -real_rows], axis=2)
    real_vis = pair_products(columns, columns)
    imag_vis = pair_products(rotated, columns)
    return jnp.stack([real_vis, imag_vis], axis=1)


def local_plain(samples, fir_taps, owner_map, dropped_channels):
    devices = lax.axis_size("feed")
    capacity = BAND // devices + BAND // (2 * devices)
    slot_total = devices * capacity
    in_local = samples.shape[0]
    dft_scale = 1.0 / math.sqrt(NFFT)
    chan_of, slot_used, channel_live = slot_tables(
        owner_map, dropped_channels, capacity, slot_total
    )
    live_mask = channel_live.astype(jnp.float32)
    kept = jnp.sum(live_mask)
    windowed = window(samples, fir_taps).reshape(in_local * SPEC, NFFT)
    table = dft_table(NFFT, BAND_START, BAND)
    spectra = (
        jnp.dot(
            windowed, table, precision=lax.Precision.HIGHEST, preferred_element_type=jnp.float32
        )
        * dft_scale
    )
    spectra = spectra.reshape(in_local, SPEC, 2, BAND)
    chosen = jnp.take(spectra, chan_of, axis=3) * slot_used.astype(jnp.float32)[None, None, None, :]
    outgoing = jnp.transpose(chosen, (3, 0, 2, 1)).reshape(devices, capacity, in_local, 2 * SPEC)
    raw_vis = correlate(lax.all_to_all(outgoing, "feed", split_axis=0, concat_axis=2, tiled=True))
    local_power = jnp.sum(jnp.trace(raw_vis[:, 0], axis1=1, axis2=2))
    power = lax.psum(local_power, "feed")
    mean_power = power / (NIN * SPEC * kept)
    factor = 1.0 / (SPEC * mean_power)
    return (raw_vis * factor).astype(jnp.bfloat16)


def split(value):
    high = value.astype(jnp.bfloat16)
    return high, (value - high.astype(jnp.float32)).astype(jnp.bfloat16)


def spectra_kernel(count, last, devices, blocks, taps, in_local, *refs):
    row_ref, taps_a, taps_b, frames_a, frames_b, table_a, table_b, table_last = refs[:8]
    refs = refs[8:]
    if last:
        before, refs = refs[0], refs[1:]
    outs, refs = refs[:blocks], refs[blocks:]
    if not last:
        power_out, refs = refs[0], refs[1:]
    even_0, odd_0, even_1, odd_1, acc, flat = refs
    step = pl.program_id(0)
    rows = count * in_local

    def window_piece(block, first, begin, even, odd):
        lanes = slice(block * KB, (block + 1) * KB)
        coef_a = [taps_a[t : t + 1, lanes] for t in range(taps)]
        coef_b = [taps_b[t : t + 1, lanes] for t in range(taps)]

        def load(ref, f):
            return ref[f, first : first + 8, lanes].astype(jnp.float32)

        held_a = [load(frames_a, begin + f) for f in range(taps - 1)]
        held_b = [load(frames_b, begin + f) for f in range(taps - 1)]
        for s in range(begin, begin + 8, 2):
            pair = []
            for f in (s, s + 1):
                held_a.append(load(frames_a, f + taps - 1))
                held_b.append(load(frames_b, f + taps - 1))
                near = sum(c * x for c, x in zip(coef_a[1:], held_a[1:])) + coef_a[0] * held_a[0]
                far = sum(c * x for c, x in zip(coef_b[1:], held_b[1:])) + coef_b[0] * held_b[0]
                pair.append((near + far, near - far))
                held_a, held_b = held_a[1:], held_b[1:]
            start = row_of(s, first)
            for ref, values in zip((even, odd), zip(*pair)):
                for tile in range(KB // LANES):
                    own = slice(tile * LANES, (tile + 1) * LANES)
                    value = jnp.concatenate([v[:, own] for v in values], axis=0)
                    ref[0, tile, start : start + 16, :], ref[1, tile, start : start + 16, :] = split(
                        value
                    )

    def row_of(s, i):
        return s // 2 * 2 * in_local + i // 8 * 16 + s % 2 * 8

    def matmul_piece(table, parity, start, ref):
        cols = slice(parity * BAND, (parity + 1) * BAND)
        at = slice(start, start + 256)
        tall = [
            jnp.concatenate([table[parity, part, 0], table[parity, part, 1]], axis=1)
            for part in range(2)
        ]
        right = jnp.concatenate([tall[0], tall[0], tall[1]], axis=0)
        wide = [ref[part, tile, at, :] for part in (0, 1, 0) for tile in range(KB // LANES)]
        left = jnp.concatenate(wide, axis=1)
        acc[at, cols] += jnp.dot(left, right, preferred_element_type=jnp.float32)

    def matmul_pieces(table, even, odd):
        return [
            functools.partial(matmul_piece, table, parity, start, ref)
            for parity, ref in enumerate((even, odd))
            for start in range(0, rows, 256)
        ]

    def window_pieces(block, even, odd):
        return [
            functools.partial(window_piece, block, first, begin, even, odd)
            for first in range(0, in_local, 8)
            for begin in range(0, count, 8)
        ]

    def alternate(left, right):
        share = len(right) // len(left)
        for k, piece in enumerate(left):
            piece()
            for other in right[k * share : (k + 1) * share]:
                other()

    @pl.when(step == 0)
    def _():
        even_1[...] = jnp.zeros_like(even_1)
        odd_1[...] = jnp.zeros_like(odd_1)
        acc[...] = jnp.zeros_like(acc)

    alternate(matmul_pieces(table_b, even_1, odd_1), window_pieces(0, even_0, odd_0))
    alternate(matmul_pieces(table_a, even_0, odd_0), window_pieces(1, even_1, odd_1))

    @pl.when(step == pl.num_programs(0) - 1)
    def _():
        for piece in matmul_pieces(table_last, even_1, odd_1):
            piece()
        width = rows // LANES
        for parity in range(2):
            for part in range(2):
                cols = slice(parity * BAND + part * LANES, parity * BAND + (part + 1) * LANES)
                for g in range(width):
                    starts = [
                        row_of(s, i)
                        for s in range(g * LANES // in_local, (g + 1) * LANES // in_local)
                        for i in range(0, in_local, 8)
                    ]
                    turned = jnp.concatenate([acc[r : r + 8, cols] for r in starts], axis=0).T
                    row = (parity * 2 + part) * width + g
                    flat[pl.ds(row, LANES, stride=4 * width), :] = turned
        size = 2 * width

        def place(c, total):
            value = flat[pl.ds(pl.multiple_of(c * size, size), size), :]
            live = jnp.int32(-1)
            for p, out in enumerate(outs):
                row = row_ref[p, c]
                live = jnp.maximum(live, row)

                @pl.when(row >= 0)
                def _(out=out, row=row):
                    out[pl.ds(pl.multiple_of(row * 8, 8), size), :] = value

            square = sum(value[start : start + 8] ** 2 for start in range(0, size, 8))
            return total + (live >= 0).astype(jnp.float32) * square

        total = lax.fori_loop(0, BAND, place, jnp.zeros((8, LANES), jnp.float32), unroll=8)
        if last:
            total = total + before[...]
            message = outs[0].shape[0] // devices
            for d in range(devices):
                outs[0][(d + 1) * message - 8 : (d + 1) * message, :] = total
        else:
            power_out[...] = total


def spectra_call(first, count, parts, before, table, owners, ranks, dead, fir_taps, samples, devices):
    _, in_local, _ = samples.shape
    taps = fir_taps.shape[0]
    step_size = 2 * KB
    steps = HALF // step_size
    last = before is not None
    rows = count * in_local
    width = 2 * rows // LANES
    messages = [
        (high - low) * width + 8 * (last and p == 0) for p, (low, high) in enumerate(parts)
    ]
    rows_of = [
        jnp.where(
            dead | (ranks < low) | (ranks >= high),
            -1,
            owners * (message // 8) + (ranks - low) * (width // 8),
        )
        for (low, high), message in zip(parts, messages)
    ]

    def frames_spec(offset):
        return pl.BlockSpec(
            (pl.Element(count + taps - 1), pl.Element(in_local), pl.Element(step_size)),
            lambda j, *_: (first, 0, pl.multiple_of((j + offset) * step_size, step_size)),
        )

    def taps_spec(offset):
        return pl.BlockSpec((taps, step_size), lambda j, *_: (0, j + offset))

    def table_spec(index):
        return pl.BlockSpec((2, 2, 2, KB, LANES), lambda j, *_: (0, 0, 0, index(j), 0))

    blocks = [jax.ShapeDtypeStruct((devices * m, LANES), jnp.float32) for m in messages]
    power = jax.ShapeDtypeStruct((8, LANES), jnp.float32)
    whole = [pl.BlockSpec(block.shape, lambda j, *_: (0, 0)) for block in blocks]
    single = [pl.BlockSpec(power.shape, lambda j, *_: (0, 0))]
    grid_spec = pltpu.PrefetchScalarGridSpec(
        num_scalar_prefetch=1,
        grid=(steps,),
        in_specs=[
            taps_spec(0),
            taps_spec(steps),
            frames_spec(0),
            frames_spec(steps),
            table_spec(lambda j: 2 * j),
            table_spec(lambda j: jnp.maximum(2 * j - 1, 0)),
            table_spec(lambda j: 2 * steps - 1),
        ]
        + (single if last else []),
        out_specs=whole + ([] if last else single),
        scratch_shapes=[pltpu.VMEM((2, KB // LANES, rows, LANES), jnp.bfloat16)] * 4
        + [
            pltpu.VMEM((rows, 2 * BAND), jnp.float32),
            pltpu.VMEM((BAND * width, LANES), jnp.float32),
        ],
    )
    results = pl.pallas_call(
        functools.partial(spectra_kernel, count, last, devices, len(parts), taps, in_local),
        out_shape=blocks + ([] if last else [power]),
        grid_spec=grid_spec,
        compiler_params=pltpu.CompilerParams(vmem_limit_bytes=60 * MIB),
        cost_estimate=pl.CostEstimate(
            flops=3 * 2 * rows * HALF * 2 * BAND, bytes_accessed=30 * MIB, transcendentals=0
        ),
        name="spectra",
    )(
        jnp.stack(rows_of),
        fir_taps,
        fir_taps,
        samples,
        samples,
        table,
        table,
        table,
        *([before] if last else []),
    )
    sent = [r.reshape(devices, m, LANES) for r, m in zip(results, messages)]
    return sent + list(results[len(parts) :])


def exchange_lanes(values, in_local):
    count = len(values)
    lane = lax.broadcasted_iota(jnp.int32, values[0].shape, 1) // in_local
    values = list(values)
    distance = count // 2
    while distance:
        upper = (lane & distance) != 0
        shift = distance * in_local
        for a in range(count):
            if a & distance:
                continue
            x, y = values[a], values[a + distance]
            values[a] = jnp.where(upper, pltpu.roll(y, shift, 1), x)
            values[a + distance] = jnp.where(upper, y, pltpu.roll(x, LANES - shift, 1))
        distance //= 2
    return values


def correlate_kernel(widths, low, count, in_local, factor_ref, used_ref, *refs):
    groups = refs[: len(widths)]
    out, left_0, right_0, left_1, right_1, staged, sems = refs[-7:]
    step, last = pl.program_id(0), count // 2 - 1
    per_tile = LANES // in_local
    blocks = groups[0].shape[0] // per_tile
    nin = groups[0].shape[0] * in_local
    factor = factor_ref[0]
    upper = lax.broadcasted_iota(jnp.int32, (8, LANES), 0) >= 4

    def prepare(slot, left, right, block):
        used = used_ref[2 * step + slot] != 0
        straight, turned = [], []
        for ref, width in zip(groups, widths):
            tiles = []
            for start in range(slot * width, (slot + 1) * width, 8):
                mixed = [
                    jnp.where(used, ref[block * per_tile + a, start : start + 8], 0.0)
                    for a in range(per_tile)
                ]
                tiles.append(exchange_lanes(mixed, in_local))
            for q in range(per_tile):
                column = [t[q] for t in tiles]
                straight += column
                if len(column) == 1:
                    swapped = pltpu.roll(column[0], 4, 0)
                    turned.append(jnp.where(upper, swapped, -swapped))
                else:
                    half = len(column) // 2
                    turned += [-t for t in column[half:]] + column[:half]
        pad = [jnp.zeros((LANES - 8 * len(straight), LANES), jnp.float32)]
        columns = jnp.concatenate(straight + pad, axis=0)
        for part, value in enumerate((columns, jnp.concatenate(turned + pad, axis=0))):
            right[0, part * blocks + block], right[1, part * blocks + block] = split(value)
        at = slice(block * LANES, (block + 1) * LANES)
        left[0, at, :], left[1, at, :] = split(columns.T)

    def multiply(index, left, right, part):
        wide = [
            jnp.concatenate([right[k, part * blocks + b] for b in range(blocks)], axis=1)
            for k in range(2)
        ]
        total = jnp.dot(
            jnp.concatenate([left[0], left[1], left[0]], axis=1),
            jnp.concatenate([wide[0], wide[0], wide[1]], axis=0),
            preferred_element_type=jnp.float32,
        )
        staged[lax.rem(index + STAGES, STAGES), part] = (total * factor).astype(jnp.bfloat16)

    def copies(index):
        buffer = lax.rem(index, STAGES)
        return [
            pltpu.make_async_copy(
                staged.at[buffer, part, pl.ds(half * nin // 2, nin // 2)],
                out.at[low + index, part, pl.ds(half * nin // 2, nin // 2)],
                sems.at[buffer, 2 * part + half],
            )
            for part in range(2)
            for half in range(2)
        ]

    def start(index):
        for copy in copies(index):
            copy.start()

    def wait(index):
        for copy in copies(index):
            copy.wait()

    odd, even = 2 * step - 1, 2 * step

    @pl.when(odd >= STAGES)
    def _():
        wait(odd - STAGES)

    for part in range(2):
        multiply(odd, left_1, right_1, part)
        for block in range(part * blocks // 2, (part + 1) * blocks // 2):
            prepare(0, left_0, right_0, block)

    @pl.when(step >= 1)
    def _():
        start(odd)

    @pl.when(even >= STAGES)
    def _():
        wait(even - STAGES)

    for part in range(2):
        multiply(even, left_0, right_0, part)
        for block in range(part * blocks // 2, (part + 1) * blocks // 2):
            prepare(1, left_1, right_1, block)

    start(even)

    @pl.when(step == last)
    def _():
        if count > STAGES:
            wait(jnp.int32(count - 1 - STAGES))
        for part in range(2):
            multiply(even + 1, left_1, right_1, part)
        start(even + 1)
        for index in range(count - min(STAGES, count), count):
            wait(jnp.int32(index))


def correlate_call(received, widths, low, high, capacity, used, factor, before, in_local):
    arrays = [r for r, _ in received]
    nin = arrays[0].shape[0] * in_local
    count = high - low
    in_specs = [
        pl.BlockSpec(memory_space=pltpu.SMEM),
        pl.BlockSpec(memory_space=pltpu.SMEM),
    ] + [
        pl.BlockSpec(
            (r.shape[0], 2 * width, LANES), lambda s, d=(low - first) // 2: (0, s + d, 0)
        )
        for (r, first), width in zip(received, widths)
    ]
    aliases = {}
    if before is not None:
        in_specs.append(pl.BlockSpec(memory_space=pl.ANY))
        aliases = {2 + len(arrays): 0}
        arrays.append(before)
    return pl.pallas_call(
        functools.partial(correlate_kernel, widths, low, count, in_local),
        out_shape=jax.ShapeDtypeStruct((capacity, 2, nin, nin), jnp.bfloat16),
        grid=(count // 2,),
        in_specs=in_specs,
        out_specs=pl.BlockSpec(memory_space=pl.ANY),
        scratch_shapes=[
            pltpu.VMEM((2, nin, LANES), jnp.bfloat16),
            pltpu.VMEM((2, 2 * nin // LANES, LANES, LANES), jnp.bfloat16),
        ]
        * 2
        + [
            pltpu.VMEM((STAGES, 2, nin, nin), jnp.bfloat16),
            pltpu.SemaphoreType.DMA((STAGES, 4)),
        ],
        input_output_aliases=aliases,
        compiler_params=pltpu.CompilerParams(vmem_limit_bytes=60 * MIB),
        cost_estimate=pl.CostEstimate(
            flops=count * 8 * nin * nin * 256,
            bytes_accessed=count * (4 * nin * nin + 8 * nin * SPEC),
            transcendentals=0,
        ),
        name="correlate",
    )(factor, used[low:high], *arrays)


def exchange(block):
    return lax.all_to_all(block, "feed", split_axis=0, concat_axis=0, tiled=True)


def channel_tables(owners, dropped_channels):
    channels = jnp.arange(BAND, dtype=jnp.int32)[:, None]
    names = jnp.concatenate([owners, dropped_channels])[None, :]
    entry = jnp.arange(names.shape[1], dtype=jnp.int32)[None, :]
    earlier = (entry < channels) & (names == owners[:, None])
    flagged = (entry >= BAND) & (names == channels)
    total = jnp.sum(jnp.where(flagged, BAND, earlier.astype(jnp.int32)), axis=1)
    return total % BAND, total >= BAND


def local_blocks(samples, fir_taps, owner_map, dropped_channels):
    devices = lax.axis_size("feed")
    capacity = BAND // devices + BAND // (2 * devices)
    in_local = samples.shape[0]
    owners = owner_map[:, 0]
    ranks, dead = channel_tables(owners, dropped_channels)
    call = functools.partial(
        spectra_call,
        table=jnp.asarray(folded_table()),
        owners=owners,
        ranks=ranks,
        dead=dead,
        fir_taps=fir_taps,
        samples=jnp.transpose(samples, (1, 0, 2)),
        devices=devices,
    )
    middle = capacity - 4
    block_a, power = call(0, FIRST, [(0, capacity)], None)
    received_a = exchange(block_a)
    block_b, block_c = call(FIRST, SPEC - FIRST, [(0, middle), (middle, capacity)], power)
    block_b, received_a = lax.optimization_barrier((block_b, received_a))
    received_b = exchange(block_b)
    block_c, received_b = lax.optimization_barrier((block_c, received_b))
    received_c = exchange(block_c)

    kept = jnp.sum(jnp.logical_not(dead).astype(jnp.float32))
    mine = (owners == lax.axis_index("feed")) & jnp.logical_not(dead)
    slots = jnp.arange(capacity, dtype=jnp.int32)
    used = jnp.any((ranks[None, :] == slots[:, None]) & mine[None, :], axis=1).astype(jnp.int32)
    mean_power = jnp.sum(received_b[:, -8:]) / (NIN * SPEC * kept)
    factor = jnp.reshape(1.0 / (SPEC * mean_power), (1,))
    run = functools.partial(
        correlate_call,
        widths=[2 * n * in_local // LANES for n in (FIRST, SPEC - FIRST)],
        capacity=capacity,
        used=used,
        factor=factor,
        in_local=in_local,
    )
    first = run([(received_a, 0), (received_b, 0)], low=0, high=middle, before=None)
    return run(
        [(received_a, 0), (received_c, middle)], low=middle, high=capacity, before=first
    )


def solution(mesh):
    in_local = NIN // mesh.shape["feed"]
    blocks = in_local * 4 == LANES
    return jax.shard_map(
        local_blocks if blocks else local_plain,
        mesh=mesh,
        in_specs=(P("feed", "grp", None), P(), P(), P("grp")),
        out_specs=P(("grp", "feed"), None, None, None),
        check_vma=False,
    )
```

```python
import functools
import math

import jax
import jax.numpy as jnp
import ml_dtypes
import numpy as np
from jax import lax
from jax.experimental import pallas as pl
from jax.experimental.pallas import tpu as pltpu
from jax.sharding import PartitionSpec as P

NIN = 512
NFFT = 8192
HALF = NFFT // 2
BAND = 256
BAND_START = 1536
SPEC = 48
FIRST = 16
KB = 256
LANES = 128
STAGES = 4
MIB = 1 << 20


def dft_table(length, first, width):
    row_ids = lax.broadcasted_iota(jnp.int32, (length, width), 0)
    chan_ids = first + lax.broadcasted_iota(jnp.int32, (length, width), 1)
    phase_int = row_ids * chan_ids % length
    angles = phase_int.astype(jnp.float32) * (2.0 * math.pi / length)
    return jnp.concatenate([jnp.cos(angles), -jnp.sin(angles)], axis=1)


def folded_table():
    n = np.arange(HALF, dtype=np.int64)
    tables = []
    for parity in range(2):
        chans = BAND_START + 2 * np.arange(BAND // 2, dtype=np.int64) + parity
        angles = (n[:, None] * chans[None, :] % NFFT) * (2.0 * math.pi / NFFT)
        full = np.stack([np.cos(angles), -np.sin(angles)]) / math.sqrt(NFFT)
        high = full.astype(np.float32).astype(ml_dtypes.bfloat16)
        low = (full - high.astype(np.float64)).astype(np.float32).astype(ml_dtypes.bfloat16)
        tables.append(np.stack([high, low]))
    return np.stack(tables)


def slot_tables(owner_map, dropped_channels, capacity, slot_total):
    owners = owner_map[:, 0]
    channels = jnp.arange(owners.shape[0], dtype=jnp.int32)
    same_owner = (owners[:, None] == owners[None, :]) & (channels[None, :] < channels[:, None])
    rank_in = jnp.sum(same_owner.astype(jnp.int32), axis=1)
    slot_of = owners * capacity + rank_in
    flagged = jnp.any(dropped_channels[:, None] == channels[None, :], axis=0)
    channel_live = jnp.logical_not(flagged)
    targets = jnp.arange(slot_total, dtype=jnp.int32)
    slot_hit = (slot_of[:, None] == targets[None, :]) & channel_live[:, None]
    chan_of = jnp.sum(slot_hit.astype(jnp.int32) * channels[:, None], axis=0)
    slot_used = jnp.any(slot_hit, axis=0)
    return (chan_of, slot_used, channel_live)


def window(block, fir_taps):
    taps = fir_taps.shape[0]
    spec_count = block.shape[1] - taps + 1
    summed = jnp.zeros((block.shape[0], spec_count, block.shape[2]), jnp.float32)
    for tap_index in range(taps):
        summed = summed + fir_taps[tap_index][None, None, :] * block[
            :, tap_index : tap_index + spec_count, :
        ].astype(jnp.float32)
    return summed


def pair_products(left, right):
    return jnp.einsum(
        "qis,qjs->qij",
        left,
        right,
        precision=lax.Precision.HIGHEST,
        preferred_element_type=jnp.float32,
    )


def correlate(received):
    columns = received[0]
    real_rows = columns[:, :, :SPEC]
    imag_rows = columns[:, :, SPEC:]
    rotated = jnp.concatenate([imag_rows, -real_rows], axis=2)
    real_vis = pair_products(columns, columns)
    imag_vis = pair_products(rotated, columns)
    return jnp.stack([real_vis, imag_vis], axis=1)


def local_plain(samples, fir_taps, owner_map, dropped_channels):
    devices = lax.axis_size("feed")
    capacity = BAND // devices + BAND // (2 * devices)
    slot_total = devices * capacity
    in_local = samples.shape[0]
    dft_scale = 1.0 / math.sqrt(NFFT)
    chan_of, slot_used, channel_live = slot_tables(
        owner_map, dropped_channels, capacity, slot_total
    )
    live_mask = channel_live.astype(jnp.float32)
    kept = jnp.sum(live_mask)
    windowed = window(samples, fir_taps).reshape(in_local * SPEC, NFFT)
    table = dft_table(NFFT, BAND_START, BAND)
    spectra = (
        jnp.dot(
            windowed, table, precision=lax.Precision.HIGHEST, preferred_element_type=jnp.float32
        )
        * dft_scale
    )
    spectra = spectra.reshape(in_local, SPEC, 2, BAND)
    chosen = jnp.take(spectra, chan_of, axis=3) * slot_used.astype(jnp.float32)[None, None, None, :]
    outgoing = jnp.transpose(chosen, (3, 0, 2, 1)).reshape(devices, capacity, in_local, 2 * SPEC)
    raw_vis = correlate(lax.all_to_all(outgoing, "feed", split_axis=0, concat_axis=2, tiled=True))
    local_power = jnp.sum(jnp.trace(raw_vis[:, 0], axis1=1, axis2=2))
    power = lax.psum(local_power, "feed")
    mean_power = power / (NIN * SPEC * kept)
    factor = 1.0 / (SPEC * mean_power)
    return (raw_vis * factor).astype(jnp.bfloat16)


def weighted(coefs, values):
    terms = [c * v for c, v in zip(coefs, values)]
    while len(terms) > 1:
        terms = [sum(terms[k + 1 : k + 2], terms[k]) for k in range(0, len(terms), 2)]
    return terms[0]


def split(value):
    high = value.astype(jnp.bfloat16)
    return high, (value - high.astype(jnp.float32)).astype(jnp.bfloat16)


def spectra_kernel(count, last, devices, message, blocks, taps, in_local, *refs):
    row_ref, taps_a, taps_b, frames_a, frames_b, table_a, table_b, table_last = refs[:8]
    refs = refs[8:]
    if last:
        before, refs = refs[0], refs[1:]
    outs, refs = refs[:blocks], refs[blocks:]
    if not last:
        power_out, refs = refs[0], refs[1:]
    even_0, odd_0, even_1, odd_1, acc, flat, staged, sems = refs
    step = pl.program_id(0)
    rows = count * in_local

    def window_piece(block, tile, begin, even, odd):
        lanes = slice(block * KB + tile * LANES, block * KB + (tile + 1) * LANES)
        coef_a = [jnp.broadcast_to(taps_a[t : t + 1, lanes], (16, LANES)) for t in range(taps)]
        coef_b = [jnp.broadcast_to(taps_b[t : t + 1, lanes], (16, LANES)) for t in range(taps)]
        for first in range(0, in_local, 16):

            def load(ref, f):
                return ref[f, first : first + 16, lanes].astype(jnp.float32)

            held_a = [load(frames_a, begin + f) for f in range(taps - 1)]
            held_b = [load(frames_b, begin + f) for f in range(taps - 1)]
            for s in range(begin, begin + 8):
                held_a.append(load(frames_a, s + taps - 1))
                held_b.append(load(frames_b, s + taps - 1))
                near = weighted(coef_a, held_a)
                far = weighted(coef_b, held_b)
                at = slice(s * in_local + first, s * in_local + first + 16)
                for ref, value in ((even, near + far), (odd, near - far)):
                    ref[0, tile, at, :], ref[1, tile, at, :] = split(value)
                held_a, held_b = held_a[1:], held_b[1:]

    def matmul_piece(table, parity, start, ref):
        cols = slice(parity * BAND, (parity + 1) * BAND)
        at = slice(start, start + 512)
        tall = [
            jnp.concatenate([table[parity, part, 0], table[parity, part, 1]], axis=1)
            for part in range(2)
        ]
        right = jnp.concatenate([tall[0], tall[0], tall[1]], axis=0)
        wide = [ref[part, tile, at, :] for part in (0, 1, 0) for tile in range(KB // LANES)]
        left = jnp.concatenate(wide, axis=1)
        acc[at, cols] += jnp.dot(left, right, preferred_element_type=jnp.float32)

    def matmul_pieces(table, even, odd):
        return [
            functools.partial(matmul_piece, table, parity, start, ref)
            for parity, ref in enumerate((even, odd))
            for start in range(0, rows, 512)
        ]

    def window_pieces(block, even, odd):
        return [
            functools.partial(window_piece, block, tile, begin, even, odd)
            for tile in range(KB // LANES)
            for begin in range(0, count, 8)
        ]

    def alternate(left, right):
        share = len(right) // len(left)
        for k, piece in enumerate(left):
            piece()
            for other in right[k * share : (k + 1) * share]:
                other()

    @pl.when(step == 0)
    def _():
        even_1[...] = jnp.zeros_like(even_1)
        odd_1[...] = jnp.zeros_like(odd_1)
        acc[...] = jnp.zeros_like(acc)

    alternate(matmul_pieces(table_b, even_1, odd_1), window_pieces(0, even_0, odd_0))
    alternate(matmul_pieces(table_a, even_0, odd_0), window_pieces(1, even_1, odd_1))

    @pl.when(step == pl.num_programs(0) - 1)
    def _():
        for piece in matmul_pieces(table_last, even_1, odd_1):
            piece()
        width = rows // LANES
        for parity in range(2):
            for part in range(2):
                cols = slice(parity * BAND + part * LANES, parity * BAND + (part + 1) * LANES)
                for g in range(width):
                    turned = acc[g * LANES : (g + 1) * LANES, cols].T
                    row = (parity * 2 + part) * width + g
                    flat[pl.ds(row, LANES, stride=4 * width), :] = turned
        size = 2 * width

        def place(c, total):
            value = flat[pl.ds(pl.multiple_of(c * size, size), size), :]
            row = row_ref[c]

            @pl.when(row >= 0)
            def _():
                staged[pl.ds(pl.multiple_of(row * 8, 8), size), :] = value

            square = value[:8] * value[:8]
            for start in range(8, size, 8):
                square += value[start : start + 8] * value[start : start + 8]
            return total + (row >= 0).astype(jnp.float32) * square

        total = lax.fori_loop(0, BAND, place, jnp.zeros((8, LANES), jnp.float32), unroll=8)
        if last:
            total = total + before[...]
            for d in range(devices):
                staged[(d + 1) * message - 8 : (d + 1) * message, :] = total
        else:
            power_out[...] = total
        copies, row = [], 0
        for k, out in enumerate(outs):
            count_rows = out.shape[0]
            copies.append(
                pltpu.make_async_copy(staged.at[pl.ds(row, count_rows)], out, sems.at[k])
            )
            row += count_rows
        for copy in copies:
            copy.start()
        for copy in copies:
            copy.wait()


def spectra_call(first, count, parts, place, before, table, ranks, dead, fir_taps, samples):
    _, in_local, _ = samples.shape
    taps = fir_taps.shape[0]
    step_size = 2 * KB
    steps = HALF // step_size
    last = before is not None
    rows = count * in_local
    width = 2 * rows // LANES
    devices = sum(parts)
    capacity = BAND // devices + BAND // (2 * devices)
    message = capacity * width + 8 * last
    row_of = jnp.where(dead, -1, place * (message // 8) + ranks * (width // 8))

    def frames_spec(offset):
        return pl.BlockSpec(
            (pl.Element(count + taps - 1), pl.Element(in_local), pl.Element(step_size)),
            lambda j, *_: (first, 0, pl.multiple_of((j + offset) * step_size, step_size)),
        )

    def taps_spec(offset):
        return pl.BlockSpec((taps, step_size), lambda j, *_: (0, j + offset))

    def table_spec(index):
        return pl.BlockSpec((2, 2, 2, KB, LANES), lambda j, *_: (0, 0, 0, index(j), 0))

    blocks = [jax.ShapeDtypeStruct((n * message, LANES), jnp.float32) for n in parts]
    power = jax.ShapeDtypeStruct((8, LANES), jnp.float32)
    whole = [pl.BlockSpec(memory_space=pl.ANY)] * len(parts)
    single = [pl.BlockSpec(power.shape, lambda j, *_: (0, 0))]
    grid_spec = pltpu.PrefetchScalarGridSpec(
        num_scalar_prefetch=1,
        grid=(steps,),
        in_specs=[
            taps_spec(0),
            taps_spec(steps),
            frames_spec(0),
            frames_spec(steps),
            table_spec(lambda j: 2 * j),
            table_spec(lambda j: jnp.maximum(2 * j - 1, 0)),
            table_spec(lambda j: 2 * steps - 1),
        ]
        + (single if last else []),
        out_specs=whole + ([] if last else single),
        scratch_shapes=[pltpu.VMEM((2, KB // LANES, rows, LANES), jnp.bfloat16)] * 4
        + [
            pltpu.VMEM((rows, 2 * BAND), jnp.float32),
            pltpu.VMEM((BAND * width, LANES), jnp.float32),
            pltpu.VMEM((devices * message, LANES), jnp.float32),
            pltpu.SemaphoreType.DMA((len(parts),)),
        ],
    )
    results = pl.pallas_call(
        functools.partial(spectra_kernel, count, last, devices, message, len(parts), taps, in_local),
        out_shape=blocks + ([] if last else [power]),
        grid_spec=grid_spec,
        compiler_params=pltpu.CompilerParams(vmem_limit_bytes=60 * MIB),
        cost_estimate=pl.CostEstimate(
            flops=3 * 2 * rows * HALF * 2 * BAND, bytes_accessed=30 * MIB, transcendentals=0
        ),
        name="spectra",
    )(
        row_of,
        fir_taps,
        fir_taps,
        samples,
        samples,
        table,
        table,
        table,
        *([before] if last else []),
    )
    sent = [r.reshape(n, message, LANES) for r, n in zip(results, parts)]
    return sent + list(results[len(parts) :])


def exchange_lanes(values, in_local):
    count = len(values)
    lane = lax.broadcasted_iota(jnp.int32, values[0].shape, 1) // in_local
    values = list(values)
    distance = count // 2
    while distance:
        upper = (lane & distance) != 0
        shift = distance * in_local
        for a in range(count):
            if a & distance:
                continue
            x, y = values[a], values[a + distance]
            values[a] = jnp.where(upper, pltpu.roll(y, shift, 1), x)
            values[a + distance] = jnp.where(upper, y, pltpu.roll(x, LANES - shift, 1))
        distance //= 2
    return values


def correlate_kernel(widths, count, in_local, factor_ref, used_ref, index_ref, *refs):
    near_a, near_b, *far_b = refs[:-8]
    out, left_0, right_0, left_1, right_1, second, staged, sems = refs[-8:]
    step, last = pl.program_id(0), count // 2 - 1
    per_tile = LANES // in_local
    blocks = near_a.shape[0] // per_tile
    nin = near_a.shape[0] * in_local
    factor = factor_ref[0]
    upper = lax.broadcasted_iota(jnp.int32, (8, LANES), 0) >= 4

    def prepare(slot, left, right, block):
        used = used_ref[2 * step + slot] != 0
        straight, turned = [], []
        for group, (ref, width) in enumerate(zip((near_a, second), widths)):
            tiles = []
            for start in range(slot * width, (slot + 1) * width, 8):
                mixed = []
                for source in range(block * per_tile, (block + 1) * per_tile):
                    at = index_ref[source] if group else source
                    mixed.append(jnp.where(used, ref[at, start : start + 8], 0.0))
                tiles.append(exchange_lanes(mixed, in_local))
            for q in range(per_tile):
                column = [t[q] for t in tiles]
                straight += column
                if len(column) == 1:
                    swapped = pltpu.roll(column[0], 4, 0)
                    turned.append(jnp.where(upper, swapped, -swapped))
                else:
                    half = len(column) // 2
                    turned += [-t for t in column[half:]] + column[:half]
        pad = [jnp.zeros((LANES - 8 * len(straight), LANES), jnp.float32)]
        columns = jnp.concatenate(straight + pad, axis=0)
        for part, value in enumerate((columns, jnp.concatenate(turned + pad, axis=0))):
            right[0, part * blocks + block], right[1, part * blocks + block] = split(value)
        at = slice(block * LANES, (block + 1) * LANES)
        left[0, at, :], left[1, at, :] = split(columns.T)

    def multiply(index, left, right, part):
        wide = [
            jnp.concatenate([right[k, part * blocks + b] for b in range(blocks)], axis=1)
            for k in range(2)
        ]
        total = jnp.dot(
            jnp.concatenate([left[0], left[1], left[0]], axis=1),
            jnp.concatenate([wide[0], wide[0], wide[1]], axis=0),
            preferred_element_type=jnp.float32,
        )
        staged[lax.rem(index + STAGES, STAGES), part] = (total * factor).astype(jnp.bfloat16)

    def copies(index):
        buffer = lax.rem(index, STAGES)
        return [
            pltpu.make_async_copy(
                staged.at[buffer, part, pl.ds(half * nin // 2, nin // 2)],
                out.at[index, part, pl.ds(half * nin // 2, nin // 2)],
                sems.at[buffer, 2 * part + half],
            )
            for part in range(2)
            for half in range(2)
        ]

    def start(index):
        for copy in copies(index):
            copy.start()

    def wait(index):
        for copy in copies(index):
            copy.wait()

    odd, even = 2 * step - 1, 2 * step
    second[: near_b.shape[0]] = near_b[...]
    for k, ref in enumerate(far_b):
        second[near_b.shape[0] + k] = ref[0]

    @pl.when(odd >= STAGES)
    def _():
        wait(odd - STAGES)

    for part in range(2):
        multiply(odd, left_1, right_1, part)
        for block in range(part * blocks // 2, (part + 1) * blocks // 2):
            prepare(0, left_0, right_0, block)

    @pl.when(step >= 1)
    def _():
        start(odd)

    @pl.when(even >= STAGES)
    def _():
        wait(even - STAGES)

    for part in range(2):
        multiply(even, left_0, right_0, part)
        for block in range(part * blocks // 2, (part + 1) * blocks // 2):
            prepare(1, left_1, right_1, block)

    start(even)

    @pl.when(step == last)
    def _():
        if count > STAGES:
            wait(jnp.int32(count - 1 - STAGES))
        for part in range(2):
            multiply(even + 1, left_1, right_1, part)
        start(even + 1)
        for index in range(count - min(STAGES, count), count):
            wait(jnp.int32(index))


def correlate_call(received, widths, capacity, used, factor, index, in_local):
    sources = received[0].shape[0]
    nin = sources * in_local
    count = capacity
    in_specs = [pl.BlockSpec(memory_space=pltpu.SMEM)] * 3 + [
        pl.BlockSpec((r.shape[0], 2 * width, LANES), lambda s: (0, s, 0))
        for r, width in zip(received, widths[:1] + widths[1:] * len(received))
    ]
    return pl.pallas_call(
        functools.partial(correlate_kernel, widths, count, in_local),
        out_shape=jax.ShapeDtypeStruct((capacity, 2, nin, nin), jnp.bfloat16),
        grid=(count // 2,),
        in_specs=in_specs,
        out_specs=pl.BlockSpec(memory_space=pl.ANY),
        scratch_shapes=[
            pltpu.VMEM((2, nin, LANES), jnp.bfloat16),
            pltpu.VMEM((2, 2 * nin // LANES, LANES, LANES), jnp.bfloat16),
        ]
        * 2
        + [
            pltpu.VMEM((sources, 2 * widths[1], LANES), jnp.float32),
            pltpu.VMEM((STAGES, 2, nin, nin), jnp.bfloat16),
            pltpu.SemaphoreType.DMA((STAGES, 4)),
        ],
        compiler_params=pltpu.CompilerParams(vmem_limit_bytes=60 * MIB),
        cost_estimate=pl.CostEstimate(
            flops=count * 8 * nin * nin * 256,
            bytes_accessed=count * (4 * nin * nin + 8 * nin * SPEC),
            transcendentals=0,
        ),
        name="correlate",
    )(factor, used, index, *received)


def exchange(block):
    return lax.all_to_all(block, "feed", split_axis=0, concat_axis=0, tiled=True)


def exchange_halves(near, far, flight):
    devices = 2 * near.shape[0]
    half = near.shape[0]
    groups = [list(range(half)), list(range(half, devices))]
    close = lax.all_to_all(
        near, "feed", split_axis=0, concat_axis=0, axis_index_groups=groups, tiled=True
    )
    arrived = []
    for k, block in enumerate(far):
        if k >= flight:
            block, arrived[k - flight] = lax.optimization_barrier((block, arrived[k - flight]))
        arrived.append(lax.ppermute(block, "feed", [(i, i ^ (half + k)) for i in range(devices)]))
    return [close] + arrived


def channel_tables(owners, dropped_channels):
    channels = jnp.arange(BAND, dtype=jnp.int32)[:, None]
    names = jnp.concatenate([owners, dropped_channels])[None, :]
    entry = jnp.arange(names.shape[1], dtype=jnp.int32)[None, :]
    earlier = (entry < channels) & (names == owners[:, None])
    flagged = (entry >= BAND) & (names == channels)
    total = jnp.sum(jnp.where(flagged, BAND, earlier.astype(jnp.int32)), axis=1)
    return total % BAND, total >= BAND


def local_blocks(samples, fir_taps, owner_map, dropped_channels):
    devices = lax.axis_size("feed")
    capacity = BAND // devices + BAND // (2 * devices)
    in_local = samples.shape[0]
    owners = owner_map[:, 0]
    ranks, dead = channel_tables(owners, dropped_channels)
    call = functools.partial(
        spectra_call,
        table=jnp.asarray(folded_table()),
        ranks=ranks,
        dead=dead,
        fir_taps=fir_taps,
        samples=jnp.transpose(samples, (1, 0, 2)),
    )
    half = devices // 2
    me = lax.axis_index("feed")

    def place(device):
        return jnp.where(device // half == me // half, device % half, half + (device ^ me) % half)

    block_a, power = call(0, FIRST, [devices], owners, None)
    received_a = exchange(block_a)
    near, *far = call(FIRST, SPEC - FIRST, [half] + [1] * half, place(owners), power)
    near, received_a = lax.optimization_barrier((near, received_a))
    received_b = exchange_halves(near, far, 3)

    kept = jnp.sum(jnp.logical_not(dead).astype(jnp.float32))
    mine = (owners == lax.axis_index("feed")) & jnp.logical_not(dead)
    slots = jnp.arange(capacity, dtype=jnp.int32)
    used = jnp.any((ranks[None, :] == slots[:, None]) & mine[None, :], axis=1).astype(jnp.int32)
    powers = jnp.concatenate([block[:, -8:] for block in received_b])
    mean_power = jnp.sum(powers) / (NIN * SPEC * kept)
    factor = jnp.reshape(1.0 / (SPEC * mean_power), (1,))
    widths = [2 * n * in_local // LANES for n in (FIRST, SPEC - FIRST)]
    index = place(jnp.arange(devices, dtype=jnp.int32)).astype(jnp.int32)
    return correlate_call(
        [received_a] + received_b, widths, capacity, used, factor, index, in_local
    )


def solution(mesh):
    in_local = NIN // mesh.shape["feed"]
    blocks = in_local * 4 == LANES
    return jax.shard_map(
        local_blocks if blocks else local_plain,
        mesh=mesh,
        in_specs=(P("feed", "grp", None), P(), P(), P("grp")),
        out_specs=P(("grp", "feed"), None, None, None),
        check_vma=False,
    )
```

```python
import functools
import math

import jax
import jax.numpy as jnp
import ml_dtypes
import numpy as np
from jax import lax
from jax.experimental import pallas as pl
from jax.experimental.pallas import tpu as pltpu
from jax.sharding import PartitionSpec as P

NIN = 512
NFFT = 8192
HALF = NFFT // 2
BAND = 256
BAND_START = 1536
SPEC = 48
FIRST = 16
KB = 256
LANES = 128
STAGES = 4
MIB = 1 << 20


def dft_table(length, first, width):
    row_ids = lax.broadcasted_iota(jnp.int32, (length, width), 0)
    chan_ids = first + lax.broadcasted_iota(jnp.int32, (length, width), 1)
    phase_int = row_ids * chan_ids % length
    angles = phase_int.astype(jnp.float32) * (2.0 * math.pi / length)
    return jnp.concatenate([jnp.cos(angles), -jnp.sin(angles)], axis=1)


def folded_table():
    n = np.arange(HALF, dtype=np.int64)
    tables = []
    for parity in range(2):
        chans = BAND_START + 2 * np.arange(BAND // 2, dtype=np.int64) + parity
        angles = (n[:, None] * chans[None, :] % NFFT) * (2.0 * math.pi / NFFT)
        full = np.stack([np.cos(angles), -np.sin(angles)]) / math.sqrt(NFFT)
        high = full.astype(np.float32).astype(ml_dtypes.bfloat16)
        low = (full - high.astype(np.float64)).astype(np.float32).astype(ml_dtypes.bfloat16)
        tables.append(np.stack([high, low]))
    return np.stack(tables)


def slot_tables(owner_map, dropped_channels, capacity, slot_total):
    owners = owner_map[:, 0]
    channels = jnp.arange(owners.shape[0], dtype=jnp.int32)
    same_owner = (owners[:, None] == owners[None, :]) & (channels[None, :] < channels[:, None])
    rank_in = jnp.sum(same_owner.astype(jnp.int32), axis=1)
    slot_of = owners * capacity + rank_in
    flagged = jnp.any(dropped_channels[:, None] == channels[None, :], axis=0)
    channel_live = jnp.logical_not(flagged)
    targets = jnp.arange(slot_total, dtype=jnp.int32)
    slot_hit = (slot_of[:, None] == targets[None, :]) & channel_live[:, None]
    chan_of = jnp.sum(slot_hit.astype(jnp.int32) * channels[:, None], axis=0)
    slot_used = jnp.any(slot_hit, axis=0)
    return (chan_of, slot_used, channel_live)


def window(block, fir_taps):
    taps = fir_taps.shape[0]
    spec_count = block.shape[1] - taps + 1
    summed = jnp.zeros((block.shape[0], spec_count, block.shape[2]), jnp.float32)
    for tap_index in range(taps):
        summed = summed + fir_taps[tap_index][None, None, :] * block[
            :, tap_index : tap_index + spec_count, :
        ].astype(jnp.float32)
    return summed


def pair_products(left, right):
    return jnp.einsum(
        "qis,qjs->qij",
        left,
        right,
        precision=lax.Precision.HIGHEST,
        preferred_element_type=jnp.float32,
    )


def correlate(received):
    columns = received[0]
    real_rows = columns[:, :, :SPEC]
    imag_rows = columns[:, :, SPEC:]
    rotated = jnp.concatenate([imag_rows, -real_rows], axis=2)
    real_vis = pair_products(columns, columns)
    imag_vis = pair_products(rotated, columns)
    return jnp.stack([real_vis, imag_vis], axis=1)


def local_plain(samples, fir_taps, owner_map, dropped_channels):
    devices = lax.axis_size("feed")
    capacity = BAND // devices + BAND // (2 * devices)
    slot_total = devices * capacity
    in_local = samples.shape[0]
    dft_scale = 1.0 / math.sqrt(NFFT)
    chan_of, slot_used, channel_live = slot_tables(
        owner_map, dropped_channels, capacity, slot_total
    )
    live_mask = channel_live.astype(jnp.float32)
    kept = jnp.sum(live_mask)
    windowed = window(samples, fir_taps).reshape(in_local * SPEC, NFFT)
    table = dft_table(NFFT, BAND_START, BAND)
    spectra = (
        jnp.dot(
            windowed, table, precision=lax.Precision.HIGHEST, preferred_element_type=jnp.float32
        )
        * dft_scale
    )
    spectra = spectra.reshape(in_local, SPEC, 2, BAND)
    chosen = jnp.take(spectra, chan_of, axis=3) * slot_used.astype(jnp.float32)[None, None, None, :]
    outgoing = jnp.transpose(chosen, (3, 0, 2, 1)).reshape(devices, capacity, in_local, 2 * SPEC)
    raw_vis = correlate(lax.all_to_all(outgoing, "feed", split_axis=0, concat_axis=2, tiled=True))
    local_power = jnp.sum(jnp.trace(raw_vis[:, 0], axis1=1, axis2=2))
    power = lax.psum(local_power, "feed")
    mean_power = power / (NIN * SPEC * kept)
    factor = 1.0 / (SPEC * mean_power)
    return (raw_vis * factor).astype(jnp.bfloat16)


def weighted(coefs, values):
    terms = [c * v for c, v in zip(coefs, values)]
    while len(terms) > 1:
        terms = [sum(terms[k + 1 : k + 2], terms[k]) for k in range(0, len(terms), 2)]
    return terms[0]


def split(value):
    high = value.astype(jnp.bfloat16)
    return high, (value - high.astype(jnp.float32)).astype(jnp.bfloat16)


def spectra_kernel(count, last, devices, message, blocks, taps, in_local, *refs):
    row_ref, taps_a, taps_b, frames_a, frames_b, table_a, table_b, table_last = refs[:8]
    refs = refs[8:]
    if last:
        before, refs = refs[0], refs[1:]
    outs, refs = refs[:blocks], refs[blocks:]
    if not last:
        power_out, refs = refs[0], refs[1:]
    even_0, odd_0, even_1, odd_1, acc, flat, staged, sems = refs
    step = pl.program_id(0)
    rows = count * in_local

    def window_piece(block, tile, begin, even, odd):
        lanes = slice(block * KB + tile * LANES, block * KB + (tile + 1) * LANES)
        coef_a = [jnp.broadcast_to(taps_a[t : t + 1, lanes], (16, LANES)) for t in range(taps)]
        coef_b = [jnp.broadcast_to(taps_b[t : t + 1, lanes], (16, LANES)) for t in range(taps)]
        for first in range(0, in_local, 16):

            def load(ref, f):
                return ref[f, first : first + 16, lanes].astype(jnp.float32)

            held_a = [load(frames_a, begin + f) for f in range(taps - 1)]
            held_b = [load(frames_b, begin + f) for f in range(taps - 1)]
            for s in range(begin, begin + 8):
                held_a.append(load(frames_a, s + taps - 1))
                held_b.append(load(frames_b, s + taps - 1))
                near = weighted(coef_a, held_a)
                far = weighted(coef_b, held_b)
                at = slice(s * in_local + first, s * in_local + first + 16)
                for ref, value in ((even, near + far), (odd, near - far)):
                    ref[0, tile, at, :], ref[1, tile, at, :] = split(value)
                held_a, held_b = held_a[1:], held_b[1:]

    def matmul_piece(table, parity, start, ref):
        cols = slice(parity * BAND, (parity + 1) * BAND)
        at = slice(start, start + 512)
        tall = [
            jnp.concatenate([table[parity, part, 0], table[parity, part, 1]], axis=1)
            for part in range(2)
        ]
        right = jnp.concatenate([tall[0], tall[0], tall[1]], axis=0)
        wide = [ref[part, tile, at, :] for part in (0, 1, 0) for tile in range(KB // LANES)]
        left = jnp.concatenate(wide, axis=1)
        acc[at, cols] += jnp.dot(left, right, preferred_element_type=jnp.float32)

    def matmul_pieces(table, even, odd):
        return [
            functools.partial(matmul_piece, table, parity, start, ref)
            for parity, ref in enumerate((even, odd))
            for start in range(0, rows, 512)
        ]

    def window_pieces(block, even, odd):
        return [
            functools.partial(window_piece, block, tile, begin, even, odd)
            for tile in range(KB // LANES)
            for begin in range(0, count, 8)
        ]

    def alternate(left, right):
        share = len(right) // len(left)
        for k, piece in enumerate(left):
            piece()
            for other in right[k * share : (k + 1) * share]:
                other()

    @pl.when(step == 0)
    def _():
        even_1[...] = jnp.zeros_like(even_1)
        odd_1[...] = jnp.zeros_like(odd_1)
        acc[...] = jnp.zeros_like(acc)

    alternate(matmul_pieces(table_b, even_1, odd_1), window_pieces(0, even_0, odd_0))
    alternate(matmul_pieces(table_a, even_0, odd_0), window_pieces(1, even_1, odd_1))

    @pl.when(step == pl.num_programs(0) - 1)
    def _():
        for piece in matmul_pieces(table_last, even_1, odd_1):
            piece()
        width = rows // LANES
        for parity in range(2):
            for part in range(2):
                cols = slice(parity * BAND + part * LANES, parity * BAND + (part + 1) * LANES)
                for g in range(width):
                    turned = acc[g * LANES : (g + 1) * LANES, cols].T
                    row = (parity * 2 + part) * width + g
                    flat[pl.ds(row, LANES, stride=4 * width), :] = turned
        size = 2 * width

        def place(c, total):
            value = flat[pl.ds(pl.multiple_of(c * size, size), size), :]
            row = row_ref[c]

            @pl.when(row >= 0)
            def _():
                staged[pl.ds(pl.multiple_of(row * 8, 8), size), :] = value

            square = value[:8] * value[:8]
            for start in range(8, size, 8):
                square += value[start : start + 8] * value[start : start + 8]
            return total + (row >= 0).astype(jnp.float32) * square

        total = lax.fori_loop(0, BAND, place, jnp.zeros((8, LANES), jnp.float32), unroll=8)
        if last:
            total = total + before[...]
            for d in range(devices):
                staged[(d + 1) * message - 8 : (d + 1) * message, :] = total
        else:
            power_out[...] = total
        copies, row = [], 0
        for k, out in enumerate(outs):
            count_rows = out.shape[0]
            copies.append(
                pltpu.make_async_copy(staged.at[pl.ds(row, count_rows)], out, sems.at[k])
            )
            row += count_rows
        for copy in copies:
            copy.start()
        for copy in copies:
            copy.wait()


def spectra_call(first, count, sizes, row_of, before, table, fir_taps, samples):
    _, in_local, _ = samples.shape
    taps = fir_taps.shape[0]
    step_size = 2 * KB
    steps = HALF // step_size
    last = before is not None
    rows = count * in_local
    width = 2 * rows // LANES
    total_rows = sum(n * r for n, r in sizes)
    message = sizes[0][1]
    devices = sum(n for n, r in sizes if r == message)

    def frames_spec(offset):
        return pl.BlockSpec(
            (pl.Element(count + taps - 1), pl.Element(in_local), pl.Element(step_size)),
            lambda j, *_: (first, 0, pl.multiple_of((j + offset) * step_size, step_size)),
        )

    def taps_spec(offset):
        return pl.BlockSpec((taps, step_size), lambda j, *_: (0, j + offset))

    def table_spec(index):
        return pl.BlockSpec((2, 2, 2, KB, LANES), lambda j, *_: (0, 0, 0, index(j), 0))

    blocks = [jax.ShapeDtypeStruct((n * r, LANES), jnp.float32) for n, r in sizes]
    power = jax.ShapeDtypeStruct((8, LANES), jnp.float32)
    whole = [pl.BlockSpec(memory_space=pl.ANY)] * len(sizes)
    single = [pl.BlockSpec(power.shape, lambda j, *_: (0, 0))]
    grid_spec = pltpu.PrefetchScalarGridSpec(
        num_scalar_prefetch=1,
        grid=(steps,),
        in_specs=[
            taps_spec(0),
            taps_spec(steps),
            frames_spec(0),
            frames_spec(steps),
            table_spec(lambda j: 2 * j),
            table_spec(lambda j: jnp.maximum(2 * j - 1, 0)),
            table_spec(lambda j: 2 * steps - 1),
        ]
        + (single if last else []),
        out_specs=whole + ([] if last else single),
        scratch_shapes=[pltpu.VMEM((2, KB // LANES, rows, LANES), jnp.bfloat16)] * 4
        + [
            pltpu.VMEM((rows, 2 * BAND), jnp.float32),
            pltpu.VMEM((BAND * width, LANES), jnp.float32),
            pltpu.VMEM((total_rows, LANES), jnp.float32),
            pltpu.SemaphoreType.DMA((len(sizes),)),
        ],
    )
    results = pl.pallas_call(
        functools.partial(spectra_kernel, count, last, devices, message, len(sizes), taps, in_local),
        out_shape=blocks + ([] if last else [power]),
        grid_spec=grid_spec,
        compiler_params=pltpu.CompilerParams(vmem_limit_bytes=60 * MIB),
        cost_estimate=pl.CostEstimate(
            flops=3 * 2 * rows * HALF * 2 * BAND, bytes_accessed=30 * MIB, transcendentals=0
        ),
        name="spectra",
    )(
        row_of,
        fir_taps,
        fir_taps,
        samples,
        samples,
        table,
        table,
        table,
        *([before] if last else []),
    )
    sent = [r.reshape(*size, LANES) for r, size in zip(results, sizes)]
    return sent + list(results[len(sizes) :])


def exchange_lanes(values, in_local):
    count = len(values)
    lane = lax.broadcasted_iota(jnp.int32, values[0].shape, 1) // in_local
    values = list(values)
    distance = count // 2
    while distance:
        upper = (lane & distance) != 0
        shift = distance * in_local
        for a in range(count):
            if a & distance:
                continue
            x, y = values[a], values[a + distance]
            values[a] = jnp.where(upper, pltpu.roll(y, shift, 1), x)
            values[a + distance] = jnp.where(upper, y, pltpu.roll(x, LANES - shift, 1))
        distance //= 2
    return values


def correlate_kernel(widths, low, count, distant, in_local, factor_ref, used_ref, index_ref, *refs):
    near_a, near_b, *far_b = refs[: 2 + distant]
    out, left_0, right_0, left_1, right_1, second, staged, sems = refs[-8:]
    step, last = pl.program_id(0), count // 2 - 1
    per_tile = LANES // in_local
    blocks = near_a.shape[0] // per_tile
    nin = near_a.shape[0] * in_local
    factor = factor_ref[0]
    upper = lax.broadcasted_iota(jnp.int32, (8, LANES), 0) >= 4

    def prepare(slot, left, right, block):
        used = used_ref[2 * step + slot] != 0
        straight, turned = [], []
        for group, (ref, width) in enumerate(zip((near_a, second), widths)):
            tiles = []
            for start in range(slot * width, (slot + 1) * width, 8):
                mixed = []
                for source in range(block * per_tile, (block + 1) * per_tile):
                    at = index_ref[source] if group else source
                    mixed.append(jnp.where(used, ref[at, start : start + 8], 0.0))
                tiles.append(exchange_lanes(mixed, in_local))
            for q in range(per_tile):
                column = [t[q] for t in tiles]
                straight += column
                if len(column) == 1:
                    swapped = pltpu.roll(column[0], 4, 0)
                    turned.append(jnp.where(upper, swapped, -swapped))
                else:
                    half = len(column) // 2
                    turned += [-t for t in column[half:]] + column[:half]
        pad = [jnp.zeros((LANES - 8 * len(straight), LANES), jnp.float32)]
        columns = jnp.concatenate(straight + pad, axis=0)
        for part, value in enumerate((columns, jnp.concatenate(turned + pad, axis=0))):
            right[0, part * blocks + block], right[1, part * blocks + block] = split(value)
        at = slice(block * LANES, (block + 1) * LANES)
        left[0, at, :], left[1, at, :] = split(columns.T)

    def multiply(index, left, right, part):
        wide = [
            jnp.concatenate([right[k, part * blocks + b] for b in range(blocks)], axis=1)
            for k in range(2)
        ]
        total = jnp.dot(
            jnp.concatenate([left[0], left[1], left[0]], axis=1),
            jnp.concatenate([wide[0], wide[0], wide[1]], axis=0),
            preferred_element_type=jnp.float32,
        )
        staged[lax.rem(index + STAGES, STAGES), part] = (total * factor).astype(jnp.bfloat16)

    def copies(index):
        buffer = lax.rem(index, STAGES)
        return [
            pltpu.make_async_copy(
                staged.at[buffer, part, pl.ds(half * nin // 2, nin // 2)],
                out.at[low + index, part, pl.ds(half * nin // 2, nin // 2)],
                sems.at[buffer, 2 * part + half],
            )
            for part in range(2)
            for half in range(2)
        ]

    def start(index):
        for copy in copies(index):
            copy.start()

    def wait(index):
        for copy in copies(index):
            copy.wait()

    odd, even = 2 * step - 1, 2 * step
    second[: near_b.shape[0]] = near_b[...]
    for k, ref in enumerate(far_b):
        second[near_b.shape[0] + k] = ref[0]

    @pl.when(odd >= STAGES)
    def _():
        wait(odd - STAGES)

    for part in range(2):
        multiply(odd, left_1, right_1, part)
        for block in range(part * blocks // 2, (part + 1) * blocks // 2):
            prepare(0, left_0, right_0, block)

    @pl.when(step >= 1)
    def _():
        start(odd)

    @pl.when(even >= STAGES)
    def _():
        wait(even - STAGES)

    for part in range(2):
        multiply(even, left_0, right_0, part)
        for block in range(part * blocks // 2, (part + 1) * blocks // 2):
            prepare(1, left_1, right_1, block)

    start(even)

    @pl.when(step == last)
    def _():
        if count > STAGES:
            wait(jnp.int32(count - 1 - STAGES))
        for part in range(2):
            multiply(even + 1, left_1, right_1, part)
        start(even + 1)
        for index in range(count - min(STAGES, count), count):
            wait(jnp.int32(index))


def correlate_call(
    first, rest, begin, widths, low, high, capacity, used, factor, index, before, in_local
):
    sources = first.shape[0]
    nin = sources * in_local
    count = high - low

    def spec(block, width, start):
        return pl.BlockSpec(
            (block.shape[0], 2 * width, LANES), lambda s: (0, s + (low - start) // 2, 0)
        )

    in_specs = [pl.BlockSpec(memory_space=pltpu.SMEM)] * 3 + [spec(first, widths[0], 0)]
    in_specs += [spec(block, widths[1], begin) for block in rest]
    arrays = [first] + rest
    aliases = {}
    if before is not None:
        in_specs.append(pl.BlockSpec(memory_space=pl.ANY))
        aliases = {3 + len(arrays): 0}
        arrays.append(before)
    return pl.pallas_call(
        functools.partial(correlate_kernel, widths, low, count, len(rest) - 1, in_local),
        out_shape=jax.ShapeDtypeStruct((capacity, 2, nin, nin), jnp.bfloat16),
        grid=(count // 2,),
        in_specs=in_specs,
        out_specs=pl.BlockSpec(memory_space=pl.ANY),
        input_output_aliases=aliases,
        scratch_shapes=[
            pltpu.VMEM((2, nin, LANES), jnp.bfloat16),
            pltpu.VMEM((2, 2 * nin // LANES, LANES, LANES), jnp.bfloat16),
        ]
        * 2
        + [
            pltpu.VMEM((sources, 2 * widths[1], LANES), jnp.float32),
            pltpu.VMEM((STAGES, 2, nin, nin), jnp.bfloat16),
            pltpu.SemaphoreType.DMA((STAGES, 4)),
        ],
        compiler_params=pltpu.CompilerParams(vmem_limit_bytes=60 * MIB),
        cost_estimate=pl.CostEstimate(
            flops=count * 8 * nin * nin * 256,
            bytes_accessed=count * (4 * nin * nin + 8 * nin * SPEC),
            transcendentals=0,
        ),
        name="correlate",
    )(factor, used[low:high], index, *arrays)


def exchange(block):
    return lax.all_to_all(block, "feed", split_axis=0, concat_axis=0, tiled=True)


def exchange_halves(near, far, flight):
    devices = 2 * near.shape[0]
    half = near.shape[0]
    groups = [list(range(half)), list(range(half, devices))]
    arrived = []
    for k, block in enumerate(far):
        if k >= flight:
            block, arrived[k - flight] = lax.optimization_barrier((block, arrived[k - flight]))
        arrived.append(lax.ppermute(block, "feed", [(i, i ^ (half + k)) for i in range(devices)]))
    near, arrived[0] = lax.optimization_barrier((near, arrived[0]))
    close = lax.all_to_all(
        near, "feed", split_axis=0, concat_axis=0, axis_index_groups=groups, tiled=True
    )
    return close, arrived


def channel_tables(owners, dropped_channels):
    channels = jnp.arange(BAND, dtype=jnp.int32)[:, None]
    names = jnp.concatenate([owners, dropped_channels])[None, :]
    entry = jnp.arange(names.shape[1], dtype=jnp.int32)[None, :]
    earlier = (entry < channels) & (names == owners[:, None])
    flagged = (entry >= BAND) & (names == channels)
    total = jnp.sum(jnp.where(flagged, BAND, earlier.astype(jnp.int32)), axis=1)
    return total % BAND, total >= BAND


def local_blocks(samples, fir_taps, owner_map, dropped_channels):
    devices = lax.axis_size("feed")
    capacity = BAND // devices + BAND // (2 * devices)
    in_local = samples.shape[0]
    owners = owner_map[:, 0]
    ranks, dead = channel_tables(owners, dropped_channels)
    call = functools.partial(
        spectra_call,
        table=jnp.asarray(folded_table()),
        fir_taps=fir_taps,
        samples=jnp.transpose(samples, (1, 0, 2)),
    )
    half = devices // 2
    middle = capacity - 4
    me = lax.axis_index("feed")
    widths = [2 * n * in_local // LANES for n in (FIRST, SPEC - FIRST)]

    def place(device):
        return jnp.where(device // half == me // half, device % half, half + (device ^ me) % half)

    rows = widths[0] // 8
    block_a, power = call(
        0,
        FIRST,
        [(devices, capacity * widths[0])],
        jnp.where(dead, -1, (owners * capacity + ranks) * rows),
        None,
    )
    received_a = exchange(block_a)
    rows = widths[1] // 8
    head, tail = middle * rows + 1, (capacity - middle) * rows
    row_of = jnp.where(
        ranks < middle,
        place(owners) * head + ranks * rows,
        devices * head + owners * tail + (ranks - middle) * rows,
    )
    near, *far, block_c = call(
        FIRST,
        SPEC - FIRST,
        [(half, 8 * head)] + [(1, 8 * head)] * half + [(devices, 8 * tail)],
        jnp.where(dead, -1, row_of),
        power,
    )
    near, received_a = lax.optimization_barrier((near, received_a))
    close, arrived = exchange_halves(near, far, 3)
    late = half - 3
    block_c, close, arrived[late] = lax.optimization_barrier((block_c, close, arrived[late]))
    received_c = exchange(block_c)
    received_b = [close] + arrived

    kept = jnp.sum(jnp.logical_not(dead).astype(jnp.float32))
    mine = (owners == lax.axis_index("feed")) & jnp.logical_not(dead)
    slots = jnp.arange(capacity, dtype=jnp.int32)
    used = jnp.any((ranks[None, :] == slots[:, None]) & mine[None, :], axis=1).astype(jnp.int32)
    powers = jnp.concatenate([block[:, -8:] for block in received_b])
    mean_power = jnp.sum(powers) / (NIN * SPEC * kept)
    factor = jnp.reshape(1.0 / (SPEC * mean_power), (1,))
    everyone = jnp.arange(devices, dtype=jnp.int32)
    run = functools.partial(
        correlate_call,
        widths=widths,
        capacity=capacity,
        used=used,
        factor=factor,
        in_local=in_local,
    )
    vis = run(
        received_a,
        received_b,
        begin=0,
        low=0,
        high=middle,
        index=place(everyone).astype(jnp.int32),
        before=None,
    )
    return run(
        received_a, [received_c], begin=middle, low=middle, high=capacity, index=everyone, before=vis
    )


def solution(mesh):
    in_local = NIN // mesh.shape["feed"]
    blocks = in_local * 4 == LANES
    return jax.shard_map(
        local_blocks if blocks else local_plain,
        mesh=mesh,
        in_specs=(P("feed", "grp", None), P(), P(), P("grp")),
        out_specs=P(("grp", "feed"), None, None, None),
        check_vma=False,
    )
```

```python
import functools
import math

import jax
import jax.numpy as jnp
import ml_dtypes
import numpy as np
from jax import lax
from jax.experimental import pallas as pl
from jax.experimental.pallas import tpu as pltpu
from jax.sharding import PartitionSpec as P

NIN = 512
NFFT = 8192
HALF = NFFT // 2
BAND = 256
BAND_START = 1536
SPEC = 48
FIRST = 16
KB = 256
LANES = 128
STAGES = 4
MIB = 1 << 20


def dft_table(length, first, width):
    row_ids = lax.broadcasted_iota(jnp.int32, (length, width), 0)
    chan_ids = first + lax.broadcasted_iota(jnp.int32, (length, width), 1)
    phase_int = row_ids * chan_ids % length
    angles = phase_int.astype(jnp.float32) * (2.0 * math.pi / length)
    return jnp.concatenate([jnp.cos(angles), -jnp.sin(angles)], axis=1)


def folded_table():
    n = np.arange(HALF, dtype=np.int64)
    tables = []
    for parity in range(2):
        chans = BAND_START + 2 * np.arange(BAND // 2, dtype=np.int64) + parity
        angles = (n[:, None] * chans[None, :] % NFFT) * (2.0 * math.pi / NFFT)
        full = np.stack([np.cos(angles), -np.sin(angles)]) / math.sqrt(NFFT)
        high = full.astype(np.float32).astype(ml_dtypes.bfloat16)
        low = (full - high.astype(np.float64)).astype(np.float32).astype(ml_dtypes.bfloat16)
        tables.append(np.stack([high, low]))
    return np.stack(tables)


def slot_tables(owner_map, dropped_channels, capacity, slot_total):
    owners = owner_map[:, 0]
    channels = jnp.arange(owners.shape[0], dtype=jnp.int32)
    same_owner = (owners[:, None] == owners[None, :]) & (channels[None, :] < channels[:, None])
    rank_in = jnp.sum(same_owner.astype(jnp.int32), axis=1)
    slot_of = owners * capacity + rank_in
    flagged = jnp.any(dropped_channels[:, None] == channels[None, :], axis=0)
    channel_live = jnp.logical_not(flagged)
    targets = jnp.arange(slot_total, dtype=jnp.int32)
    slot_hit = (slot_of[:, None] == targets[None, :]) & channel_live[:, None]
    chan_of = jnp.sum(slot_hit.astype(jnp.int32) * channels[:, None], axis=0)
    slot_used = jnp.any(slot_hit, axis=0)
    return (chan_of, slot_used, channel_live)


def window(block, fir_taps):
    taps = fir_taps.shape[0]
    spec_count = block.shape[1] - taps + 1
    summed = jnp.zeros((block.shape[0], spec_count, block.shape[2]), jnp.float32)
    for tap_index in range(taps):
        summed = summed + fir_taps[tap_index][None, None, :] * block[
            :, tap_index : tap_index + spec_count, :
        ].astype(jnp.float32)
    return summed


def pair_products(left, right):
    return jnp.einsum(
        "qis,qjs->qij",
        left,
        right,
        precision=lax.Precision.HIGHEST,
        preferred_element_type=jnp.float32,
    )


def correlate(received):
    columns = received[0]
    real_rows = columns[:, :, :SPEC]
    imag_rows = columns[:, :, SPEC:]
    rotated = jnp.concatenate([imag_rows, -real_rows], axis=2)
    real_vis = pair_products(columns, columns)
    imag_vis = pair_products(rotated, columns)
    return jnp.stack([real_vis, imag_vis], axis=1)


def local_plain(samples, fir_taps, owner_map, dropped_channels):
    devices = lax.axis_size("feed")
    capacity = BAND // devices + BAND // (2 * devices)
    slot_total = devices * capacity
    in_local = samples.shape[0]
    dft_scale = 1.0 / math.sqrt(NFFT)
    chan_of, slot_used, channel_live = slot_tables(
        owner_map, dropped_channels, capacity, slot_total
    )
    live_mask = channel_live.astype(jnp.float32)
    kept = jnp.sum(live_mask)
    windowed = window(samples, fir_taps).reshape(in_local * SPEC, NFFT)
    table = dft_table(NFFT, BAND_START, BAND)
    spectra = (
        jnp.dot(
            windowed, table, precision=lax.Precision.HIGHEST, preferred_element_type=jnp.float32
        )
        * dft_scale
    )
    spectra = spectra.reshape(in_local, SPEC, 2, BAND)
    chosen = jnp.take(spectra, chan_of, axis=3) * slot_used.astype(jnp.float32)[None, None, None, :]
    outgoing = jnp.transpose(chosen, (3, 0, 2, 1)).reshape(devices, capacity, in_local, 2 * SPEC)
    raw_vis = correlate(lax.all_to_all(outgoing, "feed", split_axis=0, concat_axis=2, tiled=True))
    local_power = jnp.sum(jnp.trace(raw_vis[:, 0], axis1=1, axis2=2))
    power = lax.psum(local_power, "feed")
    mean_power = power / (NIN * SPEC * kept)
    factor = 1.0 / (SPEC * mean_power)
    return (raw_vis * factor).astype(jnp.bfloat16)


def weighted(coefs, values):
    terms = [c * v for c, v in zip(coefs, values)]
    while len(terms) > 1:
        terms = [sum(terms[k + 1 : k + 2], terms[k]) for k in range(0, len(terms), 2)]
    return terms[0]


def split(value):
    high = value.astype(jnp.bfloat16)
    return high, (value - high.astype(jnp.float32)).astype(jnp.bfloat16)


def spectra_kernel(count, last, devices, message, blocks, taps, in_local, *refs):
    row_ref, taps_a, taps_b, frames_a, frames_b, table_a, table_b, table_last = refs[:8]
    refs = refs[8:]
    if last:
        before, refs = refs[0], refs[1:]
    outs, refs = refs[:blocks], refs[blocks:]
    if not last:
        power_out, refs = refs[0], refs[1:]
    even_0, odd_0, even_1, odd_1, acc, flat, staged, sems = refs
    step = pl.program_id(0)
    rows = count * in_local

    def window_piece(block, tile, begin, even, odd):
        lanes = slice(block * KB + tile * LANES, block * KB + (tile + 1) * LANES)
        coef_a = [jnp.broadcast_to(taps_a[t : t + 1, lanes], (16, LANES)) for t in range(taps)]
        coef_b = [jnp.broadcast_to(taps_b[t : t + 1, lanes], (16, LANES)) for t in range(taps)]
        for first in range(0, in_local, 16):

            def load(ref, f):
                return ref[f, first : first + 16, lanes].astype(jnp.float32)

            held_a = [load(frames_a, begin + f) for f in range(taps - 1)]
            held_b = [load(frames_b, begin + f) for f in range(taps - 1)]
            for s in range(begin, begin + 8):
                held_a.append(load(frames_a, s + taps - 1))
                held_b.append(load(frames_b, s + taps - 1))
                near = weighted(coef_a, held_a)
                far = weighted(coef_b, held_b)
                at = slice(s * in_local + first, s * in_local + first + 16)
                for ref, value in ((even, near + far), (odd, near - far)):
                    ref[0, tile, at, :], ref[1, tile, at, :] = split(value)
                held_a, held_b = held_a[1:], held_b[1:]

    def matmul_piece(table, parity, start, ref):
        cols = slice(parity * BAND, (parity + 1) * BAND)
        at = slice(start, start + 512)
        tall = [
            jnp.concatenate([table[parity, part, 0], table[parity, part, 1]], axis=1)
            for part in range(2)
        ]
        right = jnp.concatenate([tall[0], tall[0], tall[1]], axis=0)
        wide = [ref[part, tile, at, :] for part in (0, 1, 0) for tile in range(KB // LANES)]
        left = jnp.concatenate(wide, axis=1)
        acc[at, cols] += jnp.dot(left, right, preferred_element_type=jnp.float32)

    def matmul_pieces(table, even, odd):
        return [
            functools.partial(matmul_piece, table, parity, start, ref)
            for parity, ref in enumerate((even, odd))
            for start in range(0, rows, 512)
        ]

    def window_pieces(block, even, odd):
        return [
            functools.partial(window_piece, block, tile, begin, even, odd)
            for tile in range(KB // LANES)
            for begin in range(0, count, 8)
        ]

    def alternate(left, right):
        share = len(right) // len(left)
        for k, piece in enumerate(left):
            piece()
            for other in right[k * share : (k + 1) * share]:
                other()

    @pl.when(step == 0)
    def _():
        even_1[...] = jnp.zeros_like(even_1)
        odd_1[...] = jnp.zeros_like(odd_1)
        acc[...] = jnp.zeros_like(acc)

    alternate(matmul_pieces(table_b, even_1, odd_1), window_pieces(0, even_0, odd_0))
    alternate(matmul_pieces(table_a, even_0, odd_0), window_pieces(1, even_1, odd_1))

    @pl.when(step == pl.num_programs(0) - 1)
    def _():
        for piece in matmul_pieces(table_last, even_1, odd_1):
            piece()
        width = rows // LANES
        for parity in range(2):
            for part in range(2):
                cols = slice(parity * BAND + part * LANES, parity * BAND + (part + 1) * LANES)
                for g in range(width):
                    turned = acc[g * LANES : (g + 1) * LANES, cols].T
                    row = (parity * 2 + part) * width + g
                    flat[pl.ds(row, LANES, stride=4 * width), :] = turned
        size = 2 * width

        def place(c, total):
            value = flat[pl.ds(pl.multiple_of(c * size, size), size), :]
            row = row_ref[c]

            @pl.when(row >= 0)
            def _():
                staged[pl.ds(pl.multiple_of(row * 8, 8), size), :] = value

            square = value[:8] * value[:8]
            for start in range(8, size, 8):
                square += value[start : start + 8] * value[start : start + 8]
            return total + (row >= 0).astype(jnp.float32) * square

        total = lax.fori_loop(0, BAND, place, jnp.zeros((8, LANES), jnp.float32), unroll=8)
        if last:
            total = total + before[...]
            for d in range(devices):
                staged[(d + 1) * message - 8 : (d + 1) * message, :] = total
        else:
            power_out[...] = total
        copies, row = [], 0
        for k, out in enumerate(outs):
            count_rows = out.shape[0]
            copies.append(
                pltpu.make_async_copy(staged.at[pl.ds(row, count_rows)], out, sems.at[k])
            )
            row += count_rows
        for copy in copies:
            copy.start()
        for copy in copies:
            copy.wait()


def spectra_call(first, count, sizes, row_of, before, table, fir_taps, samples):
    _, in_local, _ = samples.shape
    taps = fir_taps.shape[0]
    step_size = 2 * KB
    steps = HALF // step_size
    last = before is not None
    rows = count * in_local
    width = 2 * rows // LANES
    total_rows = sum(n * r for n, r in sizes)
    message = sizes[0][1]
    devices = sum(n for n, r in sizes if r == message)

    def frames_spec(offset):
        return pl.BlockSpec(
            (pl.Element(count + taps - 1), pl.Element(in_local), pl.Element(step_size)),
            lambda j, *_: (first, 0, pl.multiple_of((j + offset) * step_size, step_size)),
        )

    def taps_spec(offset):
        return pl.BlockSpec((taps, step_size), lambda j, *_: (0, j + offset))

    def table_spec(index):
        return pl.BlockSpec((2, 2, 2, KB, LANES), lambda j, *_: (0, 0, 0, index(j), 0))

    blocks = [jax.ShapeDtypeStruct((n * r, LANES), jnp.float32) for n, r in sizes]
    power = jax.ShapeDtypeStruct((8, LANES), jnp.float32)
    whole = [pl.BlockSpec(memory_space=pl.ANY)] * len(sizes)
    single = [pl.BlockSpec(power.shape, lambda j, *_: (0, 0))]
    grid_spec = pltpu.PrefetchScalarGridSpec(
        num_scalar_prefetch=1,
        grid=(steps,),
        in_specs=[
            taps_spec(0),
            taps_spec(steps),
            frames_spec(0),
            frames_spec(steps),
            table_spec(lambda j: 2 * j),
            table_spec(lambda j: jnp.maximum(2 * j - 1, 0)),
            table_spec(lambda j: 2 * steps - 1),
        ]
        + (single if last else []),
        out_specs=whole + ([] if last else single),
        scratch_shapes=[pltpu.VMEM((2, KB // LANES, rows, LANES), jnp.bfloat16)] * 4
        + [
            pltpu.VMEM((rows, 2 * BAND), jnp.float32),
            pltpu.VMEM((BAND * width, LANES), jnp.float32),
            pltpu.VMEM((total_rows, LANES), jnp.float32),
            pltpu.SemaphoreType.DMA((len(sizes),)),
        ],
    )
    results = pl.pallas_call(
        functools.partial(spectra_kernel, count, last, devices, message, len(sizes), taps, in_local),
        out_shape=blocks + ([] if last else [power]),
        grid_spec=grid_spec,
        compiler_params=pltpu.CompilerParams(vmem_limit_bytes=60 * MIB),
        cost_estimate=pl.CostEstimate(
            flops=3 * 2 * rows * HALF * 2 * BAND, bytes_accessed=30 * MIB, transcendentals=0
        ),
        name="spectra",
    )(
        row_of,
        fir_taps,
        fir_taps,
        samples,
        samples,
        table,
        table,
        table,
        *([before] if last else []),
    )
    sent = [r.reshape(*size, LANES) for r, size in zip(results, sizes)]
    return sent + list(results[len(sizes) :])


def exchange_lanes(values, in_local):
    count = len(values)
    lane = lax.broadcasted_iota(jnp.int32, values[0].shape, 1) // in_local
    values = list(values)
    distance = count // 2
    while distance:
        upper = (lane & distance) != 0
        shift = distance * in_local
        for a in range(count):
            if a & distance:
                continue
            x, y = values[a], values[a + distance]
            values[a] = jnp.where(upper, pltpu.roll(y, shift, 1), x)
            values[a + distance] = jnp.where(upper, y, pltpu.roll(x, LANES - shift, 1))
        distance //= 2
    return values


def correlate_kernel(widths, low, count, distant, in_local, factor_ref, used_ref, index_ref, *refs):
    near_a, near_b, *far_b = refs[: 2 + distant]
    out, left_0, right_0, left_1, right_1, second, staged, sems = refs[-8:]
    step, last = pl.program_id(0), count // 2 - 1
    per_tile = LANES // in_local
    blocks = near_a.shape[0] // per_tile
    nin = near_a.shape[0] * in_local
    factor = factor_ref[0]
    upper = lax.broadcasted_iota(jnp.int32, (8, LANES), 0) >= 4

    def prepare(slot, left, right, block):
        used = used_ref[2 * step + slot] != 0
        straight, turned = [], []
        for group, (ref, width) in enumerate(zip((near_a, second), widths)):
            tiles = []
            for start in range(slot * width, (slot + 1) * width, 8):
                mixed = []
                for source in range(block * per_tile, (block + 1) * per_tile):
                    at = index_ref[source] if group else source
                    mixed.append(jnp.where(used, ref[at, start : start + 8], 0.0))
                tiles.append(exchange_lanes(mixed, in_local))
            for q in range(per_tile):
                column = [t[q] for t in tiles]
                straight += column
                if len(column) == 1:
                    swapped = pltpu.roll(column[0], 4, 0)
                    turned.append(jnp.where(upper, swapped, -swapped))
                else:
                    half = len(column) // 2
                    turned += [-t for t in column[half:]] + column[:half]
        pad = [jnp.zeros((LANES - 8 * len(straight), LANES), jnp.float32)]
        columns = jnp.concatenate(straight + pad, axis=0)
        for part, value in enumerate((columns, jnp.concatenate(turned + pad, axis=0))):
            right[0, part * blocks + block], right[1, part * blocks + block] = split(value)
        at = slice(block * LANES, (block + 1) * LANES)
        left[0, at, :], left[1, at, :] = split(columns.T)

    def multiply(index, left, right, part):
        wide = [
            jnp.concatenate([right[k, part * blocks + b] for b in range(blocks)], axis=1)
            for k in range(2)
        ]
        total = jnp.dot(
            jnp.concatenate([left[0], left[1], left[0]], axis=1),
            jnp.concatenate([wide[0], wide[0], wide[1]], axis=0),
            preferred_element_type=jnp.float32,
        )
        staged[lax.rem(index + STAGES, STAGES), part] = (total * factor).astype(jnp.bfloat16)

    def copies(index):
        buffer = lax.rem(index, STAGES)
        return [
            pltpu.make_async_copy(
                staged.at[buffer, part, pl.ds(half * nin // 2, nin // 2)],
                out.at[low + index, part, pl.ds(half * nin // 2, nin // 2)],
                sems.at[buffer, 2 * part + half],
            )
            for part in range(2)
            for half in range(2)
        ]

    def start(index):
        for copy in copies(index):
            copy.start()

    def wait(index):
        for copy in copies(index):
            copy.wait()

    odd, even = 2 * step - 1, 2 * step
    second[: near_b.shape[0]] = near_b[...]
    for k, ref in enumerate(far_b):
        second[near_b.shape[0] + k] = ref[0]

    @pl.when(odd >= STAGES)
    def _():
        wait(odd - STAGES)

    for part in range(2):
        multiply(odd, left_1, right_1, part)
        for block in range(part * blocks // 2, (part + 1) * blocks // 2):
            prepare(0, left_0, right_0, block)

    @pl.when(step >= 1)
    def _():
        start(odd)

    @pl.when(even >= STAGES)
    def _():
        wait(even - STAGES)

    for part in range(2):
        multiply(even, left_0, right_0, part)
        for block in range(part * blocks // 2, (part + 1) * blocks // 2):
            prepare(1, left_1, right_1, block)

    start(even)

    @pl.when(step == last)
    def _():
        if count > STAGES:
            wait(jnp.int32(count - 1 - STAGES))
        for part in range(2):
            multiply(even + 1, left_1, right_1, part)
        start(even + 1)
        for index in range(count - min(STAGES, count), count):
            wait(jnp.int32(index))


def correlate_call(
    first, rest, begin, widths, low, high, capacity, used, factor, index, before, in_local
):
    sources = first.shape[0]
    nin = sources * in_local
    count = high - low

    def spec(block, width, start):
        return pl.BlockSpec(
            (block.shape[0], 2 * width, LANES), lambda s: (0, s + (low - start) // 2, 0)
        )

    in_specs = [pl.BlockSpec(memory_space=pltpu.SMEM)] * 3 + [spec(first, widths[0], 0)]
    in_specs += [spec(block, widths[1], begin) for block in rest]
    arrays = [first] + rest
    aliases = {}
    if before is not None:
        in_specs.append(pl.BlockSpec(memory_space=pl.ANY))
        aliases = {3 + len(arrays): 0}
        arrays.append(before)
    return pl.pallas_call(
        functools.partial(correlate_kernel, widths, low, count, len(rest) - 1, in_local),
        out_shape=jax.ShapeDtypeStruct((capacity, 2, nin, nin), jnp.bfloat16),
        grid=(count // 2,),
        in_specs=in_specs,
        out_specs=pl.BlockSpec(memory_space=pl.ANY),
        input_output_aliases=aliases,
        scratch_shapes=[
            pltpu.VMEM((2, nin, LANES), jnp.bfloat16),
            pltpu.VMEM((2, 2 * nin // LANES, LANES, LANES), jnp.bfloat16),
        ]
        * 2
        + [
            pltpu.VMEM((sources, 2 * widths[1], LANES), jnp.float32),
            pltpu.VMEM((STAGES, 2, nin, nin), jnp.bfloat16),
            pltpu.SemaphoreType.DMA((STAGES, 4)),
        ],
        compiler_params=pltpu.CompilerParams(vmem_limit_bytes=60 * MIB),
        cost_estimate=pl.CostEstimate(
            flops=count * 8 * nin * nin * 256,
            bytes_accessed=count * (4 * nin * nin + 8 * nin * SPEC),
            transcendentals=0,
        ),
        name="correlate",
    )(factor, used[low:high], index, *arrays)


def exchange(block):
    return lax.all_to_all(block, "feed", split_axis=0, concat_axis=0, tiled=True)


def exchange_halves(near, far, flight):
    devices = 2 * near.shape[0]
    half = near.shape[0]
    groups = [list(range(half)), list(range(half, devices))]
    arrived = []
    for k, block in enumerate(far):
        if k >= flight:
            block, arrived[k - flight] = lax.optimization_barrier((block, arrived[k - flight]))
        arrived.append(lax.ppermute(block, "feed", [(i, i ^ (half + k)) for i in range(devices)]))
    close = lax.all_to_all(
        near, "feed", split_axis=0, concat_axis=0, axis_index_groups=groups, tiled=True
    )
    return close, arrived


def channel_tables(owners, dropped_channels):
    channels = jnp.arange(BAND, dtype=jnp.int32)[:, None]
    names = jnp.concatenate([owners, dropped_channels])[None, :]
    entry = jnp.arange(names.shape[1], dtype=jnp.int32)[None, :]
    earlier = (entry < channels) & (names == owners[:, None])
    flagged = (entry >= BAND) & (names == channels)
    total = jnp.sum(jnp.where(flagged, BAND, earlier.astype(jnp.int32)), axis=1)
    return total % BAND, total >= BAND


def local_blocks(samples, fir_taps, owner_map, dropped_channels):
    devices = lax.axis_size("feed")
    capacity = BAND // devices + BAND // (2 * devices)
    in_local = samples.shape[0]
    owners = owner_map[:, 0]
    ranks, dead = channel_tables(owners, dropped_channels)
    call = functools.partial(
        spectra_call,
        table=jnp.asarray(folded_table()),
        fir_taps=fir_taps,
        samples=jnp.transpose(samples, (1, 0, 2)),
    )
    half = devices // 2
    middle = capacity * 2 // 3
    me = lax.axis_index("feed")
    widths = [2 * n * in_local // LANES for n in (FIRST, SPEC - FIRST)]

    def place(device):
        return jnp.where(device // half == me // half, device % half, half + (device ^ me) % half)

    rows = widths[0] // 8
    block_a, power = call(
        0,
        FIRST,
        [(devices, capacity * widths[0])],
        jnp.where(dead, -1, (owners * capacity + ranks) * rows),
        None,
    )
    received_a = exchange(block_a)
    rows = widths[1] // 8
    head, tail = middle * rows, (capacity - middle) * rows + 1
    row_of = jnp.where(
        ranks < middle,
        devices * tail + place(owners) * head + ranks * rows,
        owners * tail + (ranks - middle) * rows,
    )
    block_c, near, *far = call(
        FIRST,
        SPEC - FIRST,
        [(devices, 8 * tail), (half, 8 * head)] + [(1, 8 * head)] * half,
        jnp.where(dead, -1, row_of),
        power,
    )
    block_c, received_a = lax.optimization_barrier((block_c, received_a))
    received_c = exchange(block_c)
    near, received_c = lax.optimization_barrier((near, received_c))
    close, arrived = exchange_halves(near, far, 3)
    received_b = [close] + arrived

    kept = jnp.sum(jnp.logical_not(dead).astype(jnp.float32))
    mine = (owners == lax.axis_index("feed")) & jnp.logical_not(dead)
    slots = jnp.arange(capacity, dtype=jnp.int32)
    used = jnp.any((ranks[None, :] == slots[:, None]) & mine[None, :], axis=1).astype(jnp.int32)
    mean_power = jnp.sum(received_c[:, -8:]) / (NIN * SPEC * kept)
    factor = jnp.reshape(1.0 / (SPEC * mean_power), (1,))
    everyone = jnp.arange(devices, dtype=jnp.int32)
    run = functools.partial(
        correlate_call,
        widths=widths,
        capacity=capacity,
        used=used,
        factor=factor,
        in_local=in_local,
    )
    vis = run(
        received_a, [received_c], begin=middle, low=middle, high=capacity, index=everyone, before=None
    )
    return run(
        received_a,
        received_b,
        begin=0,
        low=0,
        high=middle,
        index=place(everyone).astype(jnp.int32),
        before=vis,
    )


def solution(mesh):
    in_local = NIN // mesh.shape["feed"]
    blocks = in_local * 4 == LANES
    return jax.shard_map(
        local_blocks if blocks else local_plain,
        mesh=mesh,
        in_specs=(P("feed", "grp", None), P(), P(), P("grp")),
        out_specs=P(("grp", "feed"), None, None, None),
        check_vma=False,
    )
```

```python
import functools
import math

import jax
import jax.numpy as jnp
import ml_dtypes
import numpy as np
from jax import lax
from jax.experimental import pallas as pl
from jax.experimental.pallas import tpu as pltpu
from jax.sharding import PartitionSpec as P

NIN = 512
NFFT = 8192
HALF = NFFT // 2
BAND = 256
BAND_START = 1536
SPEC = 48
FIRST = 16
KB = 256
LANES = 128
STAGES = 4
MIB = 1 << 20


def dft_table(length, first, width):
    row_ids = lax.broadcasted_iota(jnp.int32, (length, width), 0)
    chan_ids = first + lax.broadcasted_iota(jnp.int32, (length, width), 1)
    phase_int = row_ids * chan_ids % length
    angles = phase_int.astype(jnp.float32) * (2.0 * math.pi / length)
    return jnp.concatenate([jnp.cos(angles), -jnp.sin(angles)], axis=1)


def folded_table():
    n = np.arange(HALF, dtype=np.int64)
    tables = []
    for parity in range(2):
        chans = BAND_START + 2 * np.arange(BAND // 2, dtype=np.int64) + parity
        angles = (n[:, None] * chans[None, :] % NFFT) * (2.0 * math.pi / NFFT)
        full = np.stack([np.cos(angles), -np.sin(angles)]) / math.sqrt(NFFT)
        high = full.astype(np.float32).astype(ml_dtypes.bfloat16)
        low = (full - high.astype(np.float64)).astype(np.float32).astype(ml_dtypes.bfloat16)
        tables.append(np.stack([high, low]))
    return np.stack(tables)


def slot_tables(owner_map, dropped_channels, capacity, slot_total):
    owners = owner_map[:, 0]
    channels = jnp.arange(owners.shape[0], dtype=jnp.int32)
    same_owner = (owners[:, None] == owners[None, :]) & (channels[None, :] < channels[:, None])
    rank_in = jnp.sum(same_owner.astype(jnp.int32), axis=1)
    slot_of = owners * capacity + rank_in
    flagged = jnp.any(dropped_channels[:, None] == channels[None, :], axis=0)
    channel_live = jnp.logical_not(flagged)
    targets = jnp.arange(slot_total, dtype=jnp.int32)
    slot_hit = (slot_of[:, None] == targets[None, :]) & channel_live[:, None]
    chan_of = jnp.sum(slot_hit.astype(jnp.int32) * channels[:, None], axis=0)
    slot_used = jnp.any(slot_hit, axis=0)
    return (chan_of, slot_used, channel_live)


def window(block, fir_taps):
    taps = fir_taps.shape[0]
    spec_count = block.shape[1] - taps + 1
    summed = jnp.zeros((block.shape[0], spec_count, block.shape[2]), jnp.float32)
    for tap_index in range(taps):
        summed = summed + fir_taps[tap_index][None, None, :] * block[
            :, tap_index : tap_index + spec_count, :
        ].astype(jnp.float32)
    return summed


def pair_products(left, right):
    return jnp.einsum(
        "qis,qjs->qij",
        left,
        right,
        precision=lax.Precision.HIGHEST,
        preferred_element_type=jnp.float32,
    )


def correlate(received):
    columns = received[0]
    real_rows = columns[:, :, :SPEC]
    imag_rows = columns[:, :, SPEC:]
    rotated = jnp.concatenate([imag_rows, -real_rows], axis=2)
    real_vis = pair_products(columns, columns)
    imag_vis = pair_products(rotated, columns)
    return jnp.stack([real_vis, imag_vis], axis=1)


def local_plain(samples, fir_taps, owner_map, dropped_channels):
    devices = lax.axis_size("feed")
    capacity = BAND // devices + BAND // (2 * devices)
    slot_total = devices * capacity
    in_local = samples.shape[0]
    dft_scale = 1.0 / math.sqrt(NFFT)
    chan_of, slot_used, channel_live = slot_tables(
        owner_map, dropped_channels, capacity, slot_total
    )
    live_mask = channel_live.astype(jnp.float32)
    kept = jnp.sum(live_mask)
    windowed = window(samples, fir_taps).reshape(in_local * SPEC, NFFT)
    table = dft_table(NFFT, BAND_START, BAND)
    spectra = (
        jnp.dot(
            windowed, table, precision=lax.Precision.HIGHEST, preferred_element_type=jnp.float32
        )
        * dft_scale
    )
    spectra = spectra.reshape(in_local, SPEC, 2, BAND)
    chosen = jnp.take(spectra, chan_of, axis=3) * slot_used.astype(jnp.float32)[None, None, None, :]
    outgoing = jnp.transpose(chosen, (3, 0, 2, 1)).reshape(devices, capacity, in_local, 2 * SPEC)
    raw_vis = correlate(lax.all_to_all(outgoing, "feed", split_axis=0, concat_axis=2, tiled=True))
    local_power = jnp.sum(jnp.trace(raw_vis[:, 0], axis1=1, axis2=2))
    power = lax.psum(local_power, "feed")
    mean_power = power / (NIN * SPEC * kept)
    factor = 1.0 / (SPEC * mean_power)
    return (raw_vis * factor).astype(jnp.bfloat16)


def weighted(coefs, values):
    terms = [c * v for c, v in zip(coefs, values)]
    while len(terms) > 1:
        terms = [sum(terms[k + 1 : k + 2], terms[k]) for k in range(0, len(terms), 2)]
    return terms[0]


def split(value):
    high = value.astype(jnp.bfloat16)
    return high, (value - high.astype(jnp.float32)).astype(jnp.bfloat16)


def spectra_kernel(count, last, devices, message, blocks, taps, in_local, *refs):
    row_ref, taps_a, taps_b, frames_a, frames_b, table_a, table_b, table_last = refs[:8]
    refs = refs[8:]
    if last:
        before, refs = refs[0], refs[1:]
    outs, refs = refs[:blocks], refs[blocks:]
    if not last:
        power_out, refs = refs[0], refs[1:]
    even_0, odd_0, even_1, odd_1, acc, flat, staged, sems = refs
    step = pl.program_id(0)
    rows = count * in_local

    def window_piece(block, tile, begin, even, odd):
        lanes = slice(block * KB + tile * LANES, block * KB + (tile + 1) * LANES)
        coef_a = [jnp.broadcast_to(taps_a[t : t + 1, lanes], (16, LANES)) for t in range(taps)]
        coef_b = [jnp.broadcast_to(taps_b[t : t + 1, lanes], (16, LANES)) for t in range(taps)]
        for first in range(0, in_local, 16):

            def load(ref, f):
                return ref[f, first : first + 16, lanes].astype(jnp.float32)

            held_a = [load(frames_a, begin + f) for f in range(taps - 1)]
            held_b = [load(frames_b, begin + f) for f in range(taps - 1)]
            for s in range(begin, begin + 8):
                held_a.append(load(frames_a, s + taps - 1))
                held_b.append(load(frames_b, s + taps - 1))
                near = weighted(coef_a, held_a)
                far = weighted(coef_b, held_b)
                at = slice(s * in_local + first, s * in_local + first + 16)
                for ref, value in ((even, near + far), (odd, near - far)):
                    ref[0, tile, at, :], ref[1, tile, at, :] = split(value)
                held_a, held_b = held_a[1:], held_b[1:]

    def matmul_piece(table, parity, start, ref):
        cols = slice(parity * BAND, (parity + 1) * BAND)
        at = slice(start, start + 512)
        tall = [
            jnp.concatenate([table[parity, part, 0], table[parity, part, 1]], axis=1)
            for part in range(2)
        ]
        right = jnp.concatenate([tall[0], tall[0], tall[1]], axis=0)
        wide = [ref[part, tile, at, :] for part in (0, 1, 0) for tile in range(KB // LANES)]
        left = jnp.concatenate(wide, axis=1)
        acc[at, cols] += jnp.dot(left, right, preferred_element_type=jnp.float32)

    def matmul_pieces(table, even, odd):
        return [
            functools.partial(matmul_piece, table, parity, start, ref)
            for parity, ref in enumerate((even, odd))
            for start in range(0, rows, 512)
        ]

    def window_pieces(block, even, odd):
        return [
            functools.partial(window_piece, block, tile, begin, even, odd)
            for tile in range(KB // LANES)
            for begin in range(0, count, 8)
        ]

    def alternate(left, right):
        share = len(right) // len(left)
        for k, piece in enumerate(left):
            piece()
            for other in right[k * share : (k + 1) * share]:
                other()

    @pl.when(step == 0)
    def _():
        even_1[...] = jnp.zeros_like(even_1)
        odd_1[...] = jnp.zeros_like(odd_1)
        acc[...] = jnp.zeros_like(acc)

    alternate(matmul_pieces(table_b, even_1, odd_1), window_pieces(0, even_0, odd_0))
    alternate(matmul_pieces(table_a, even_0, odd_0), window_pieces(1, even_1, odd_1))

    @pl.when(step == pl.num_programs(0) - 1)
    def _():
        for piece in matmul_pieces(table_last, even_1, odd_1):
            piece()
        width = rows // LANES
        for parity in range(2):
            for part in range(2):
                cols = slice(parity * BAND + part * LANES, parity * BAND + (part + 1) * LANES)
                for g in range(width):
                    turned = acc[g * LANES : (g + 1) * LANES, cols].T
                    row = (parity * 2 + part) * width + g
                    flat[pl.ds(row, LANES, stride=4 * width), :] = turned
        size = 2 * width

        def place(c, total):
            value = flat[pl.ds(pl.multiple_of(c * size, size), size), :]
            row = row_ref[c]

            @pl.when(row >= 0)
            def _():
                staged[pl.ds(pl.multiple_of(row * 8, 8), size), :] = value

            square = value[:8] * value[:8]
            for start in range(8, size, 8):
                square += value[start : start + 8] * value[start : start + 8]
            return total + (row >= 0).astype(jnp.float32) * square

        total = lax.fori_loop(0, BAND, place, jnp.zeros((8, LANES), jnp.float32), unroll=8)
        if last:
            total = total + before[...]
            for d in range(devices):
                staged[(d + 1) * message - 8 : (d + 1) * message, :] = total
        else:
            power_out[...] = total
        copies, row = [], 0
        for k, out in enumerate(outs):
            count_rows = out.shape[0]
            copies.append(
                pltpu.make_async_copy(staged.at[pl.ds(row, count_rows)], out, sems.at[k])
            )
            row += count_rows
        for copy in copies:
            copy.start()
        for copy in copies:
            copy.wait()


def spectra_call(first, count, sizes, row_of, before, table, fir_taps, samples):
    _, in_local, _ = samples.shape
    taps = fir_taps.shape[0]
    step_size = 2 * KB
    steps = HALF // step_size
    last = before is not None
    rows = count * in_local
    width = 2 * rows // LANES
    total_rows = sum(n * r for n, r in sizes)
    message = sizes[0][1]
    devices = sum(n for n, r in sizes if r == message)

    def frames_spec(offset):
        return pl.BlockSpec(
            (pl.Element(count + taps - 1), pl.Element(in_local), pl.Element(step_size)),
            lambda j, *_: (first, 0, pl.multiple_of((j + offset) * step_size, step_size)),
        )

    def taps_spec(offset):
        return pl.BlockSpec((taps, step_size), lambda j, *_: (0, j + offset))

    def table_spec(index):
        return pl.BlockSpec((2, 2, 2, KB, LANES), lambda j, *_: (0, 0, 0, index(j), 0))

    blocks = [jax.ShapeDtypeStruct((n * r, LANES), jnp.float32) for n, r in sizes]
    power = jax.ShapeDtypeStruct((8, LANES), jnp.float32)
    whole = [pl.BlockSpec(memory_space=pl.ANY)] * len(sizes)
    single = [pl.BlockSpec(power.shape, lambda j, *_: (0, 0))]
    grid_spec = pltpu.PrefetchScalarGridSpec(
        num_scalar_prefetch=1,
        grid=(steps,),
        in_specs=[
            taps_spec(0),
            taps_spec(steps),
            frames_spec(0),
            frames_spec(steps),
            table_spec(lambda j: 2 * j),
            table_spec(lambda j: jnp.maximum(2 * j - 1, 0)),
            table_spec(lambda j: 2 * steps - 1),
        ]
        + (single if last else []),
        out_specs=whole + ([] if last else single),
        scratch_shapes=[pltpu.VMEM((2, KB // LANES, rows, LANES), jnp.bfloat16)] * 4
        + [
            pltpu.VMEM((rows, 2 * BAND), jnp.float32),
            pltpu.VMEM((BAND * width, LANES), jnp.float32),
            pltpu.VMEM((total_rows, LANES), jnp.float32),
            pltpu.SemaphoreType.DMA((len(sizes),)),
        ],
    )
    results = pl.pallas_call(
        functools.partial(spectra_kernel, count, last, devices, message, len(sizes), taps, in_local),
        out_shape=blocks + ([] if last else [power]),
        grid_spec=grid_spec,
        compiler_params=pltpu.CompilerParams(vmem_limit_bytes=60 * MIB),
        cost_estimate=pl.CostEstimate(
            flops=3 * 2 * rows * HALF * 2 * BAND, bytes_accessed=30 * MIB, transcendentals=0
        ),
        name="spectra",
    )(
        row_of,
        fir_taps,
        fir_taps,
        samples,
        samples,
        table,
        table,
        table,
        *([before] if last else []),
    )
    sent = [r.reshape(*size, LANES) for r, size in zip(results, sizes)]
    return sent + list(results[len(sizes) :])


def exchange_lanes(values, in_local):
    count = len(values)
    lane = lax.broadcasted_iota(jnp.int32, values[0].shape, 1) // in_local
    values = list(values)
    distance = count // 2
    while distance:
        upper = (lane & distance) != 0
        shift = distance * in_local
        for a in range(count):
            if a & distance:
                continue
            x, y = values[a], values[a + distance]
            values[a] = jnp.where(upper, pltpu.roll(y, shift, 1), x)
            values[a + distance] = jnp.where(upper, y, pltpu.roll(x, LANES - shift, 1))
        distance //= 2
    return values


def correlate_kernel(widths, low, count, distant, in_local, factor_ref, used_ref, index_ref, *refs):
    near_a, near_b, *far_b = refs[: 2 + distant]
    out, left_0, right_0, left_1, right_1, second, staged, sems = refs[-8:]
    step, last = pl.program_id(0), count // 2 - 1
    per_tile = LANES // in_local
    blocks = near_a.shape[0] // per_tile
    nin = near_a.shape[0] * in_local
    factor = factor_ref[0]
    upper = lax.broadcasted_iota(jnp.int32, (8, LANES), 0) >= 4

    def prepare(slot, left, right, block):
        used = used_ref[2 * step + slot] != 0
        straight, turned = [], []
        for group, (ref, width) in enumerate(zip((near_a, second), widths)):
            tiles = []
            for start in range(slot * width, (slot + 1) * width, 8):
                mixed = []
                for source in range(block * per_tile, (block + 1) * per_tile):
                    at = index_ref[source] if group else source
                    mixed.append(jnp.where(used, ref[at, start : start + 8], 0.0))
                tiles.append(exchange_lanes(mixed, in_local))
            for q in range(per_tile):
                column = [t[q] for t in tiles]
                straight += column
                if len(column) == 1:
                    swapped = pltpu.roll(column[0], 4, 0)
                    turned.append(jnp.where(upper, swapped, -swapped))
                else:
                    half = len(column) // 2
                    turned += [-t for t in column[half:]] + column[:half]
        pad = [jnp.zeros((LANES - 8 * len(straight), LANES), jnp.float32)]
        columns = jnp.concatenate(straight + pad, axis=0)
        for part, value in enumerate((columns, jnp.concatenate(turned + pad, axis=0))):
            right[0, part * blocks + block], right[1, part * blocks + block] = split(value)
        at = slice(block * LANES, (block + 1) * LANES)
        left[0, at, :], left[1, at, :] = split(columns.T)

    def multiply(index, left, right, part):
        wide = [
            jnp.concatenate([right[k, part * blocks + b] for b in range(blocks)], axis=1)
            for k in range(2)
        ]
        total = jnp.dot(
            jnp.concatenate([left[0], left[1], left[0]], axis=1),
            jnp.concatenate([wide[0], wide[0], wide[1]], axis=0),
            preferred_element_type=jnp.float32,
        )
        staged[lax.rem(index + STAGES, STAGES), part] = (total * factor).astype(jnp.bfloat16)

    def copies(index):
        buffer = lax.rem(index, STAGES)
        return [
            pltpu.make_async_copy(
                staged.at[buffer, part, pl.ds(half * nin // 2, nin // 2)],
                out.at[low + index, part, pl.ds(half * nin // 2, nin // 2)],
                sems.at[buffer, 2 * part + half],
            )
            for part in range(2)
            for half in range(2)
        ]

    def start(index):
        for copy in copies(index):
            copy.start()

    def wait(index):
        for copy in copies(index):
            copy.wait()

    odd, even = 2 * step - 1, 2 * step
    second[: near_b.shape[0]] = near_b[...]
    for k, ref in enumerate(far_b):
        second[near_b.shape[0] + k] = ref[0]

    @pl.when(odd >= STAGES)
    def _():
        wait(odd - STAGES)

    for part in range(2):
        multiply(odd, left_1, right_1, part)
        for block in range(part * blocks // 2, (part + 1) * blocks // 2):
            prepare(0, left_0, right_0, block)

    @pl.when(step >= 1)
    def _():
        start(odd)

    @pl.when(even >= STAGES)
    def _():
        wait(even - STAGES)

    for part in range(2):
        multiply(even, left_0, right_0, part)
        for block in range(part * blocks // 2, (part + 1) * blocks // 2):
            prepare(1, left_1, right_1, block)

    start(even)

    @pl.when(step == last)
    def _():
        if count > STAGES:
            wait(jnp.int32(count - 1 - STAGES))
        for part in range(2):
            multiply(even + 1, left_1, right_1, part)
        start(even + 1)
        for index in range(count - min(STAGES, count), count):
            wait(jnp.int32(index))


def correlate_call(
    first, rest, begin, widths, low, high, capacity, used, factor, index, before, in_local
):
    sources = first.shape[0]
    nin = sources * in_local
    count = high - low

    def spec(block, width, start):
        return pl.BlockSpec(
            (block.shape[0], 2 * width, LANES), lambda s: (0, s + (low - start) // 2, 0)
        )

    in_specs = [pl.BlockSpec(memory_space=pltpu.SMEM)] * 3 + [spec(first, widths[0], 0)]
    in_specs += [spec(block, widths[1], begin) for block in rest]
    arrays = [first] + rest
    aliases = {}
    if before is not None:
        in_specs.append(pl.BlockSpec(memory_space=pl.ANY))
        aliases = {3 + len(arrays): 0}
        arrays.append(before)
    return pl.pallas_call(
        functools.partial(correlate_kernel, widths, low, count, len(rest) - 1, in_local),
        out_shape=jax.ShapeDtypeStruct((capacity, 2, nin, nin), jnp.bfloat16),
        grid=(count // 2,),
        in_specs=in_specs,
        out_specs=pl.BlockSpec(memory_space=pl.ANY),
        input_output_aliases=aliases,
        scratch_shapes=[
            pltpu.VMEM((2, nin, LANES), jnp.bfloat16),
            pltpu.VMEM((2, 2 * nin // LANES, LANES, LANES), jnp.bfloat16),
        ]
        * 2
        + [
            pltpu.VMEM((sources, 2 * widths[1], LANES), jnp.float32),
            pltpu.VMEM((STAGES, 2, nin, nin), jnp.bfloat16),
            pltpu.SemaphoreType.DMA((STAGES, 4)),
        ],
        compiler_params=pltpu.CompilerParams(vmem_limit_bytes=60 * MIB),
        cost_estimate=pl.CostEstimate(
            flops=count * 8 * nin * nin * 256,
            bytes_accessed=count * (4 * nin * nin + 8 * nin * SPEC),
            transcendentals=0,
        ),
        name="correlate",
    )(factor, used[low:high], index, *arrays)


def exchange(block):
    return lax.all_to_all(block, "feed", split_axis=0, concat_axis=0, tiled=True)


def exchange_pairs(far, flight):
    devices = len(far) + 1
    half = devices // 2
    order = []
    for k in range(half):
        order += [half + k] + ([k] if k else [])
    arrived = [None] * len(far)
    for k, d in enumerate(order):
        block = far[d - 1]
        if k >= flight:
            e = order[k - flight] - 1
            block, arrived[e] = lax.optimization_barrier((block, arrived[e]))
        arrived[d - 1] = lax.ppermute(block, "feed", [(i, i ^ d) for i in range(devices)])
    return arrived


def channel_tables(owners, dropped_channels):
    channels = jnp.arange(BAND, dtype=jnp.int32)[:, None]
    names = jnp.concatenate([owners, dropped_channels])[None, :]
    entry = jnp.arange(names.shape[1], dtype=jnp.int32)[None, :]
    earlier = (entry < channels) & (names == owners[:, None])
    flagged = (entry >= BAND) & (names == channels)
    total = jnp.sum(jnp.where(flagged, BAND, earlier.astype(jnp.int32)), axis=1)
    return total % BAND, total >= BAND


def local_blocks(samples, fir_taps, owner_map, dropped_channels):
    devices = lax.axis_size("feed")
    capacity = BAND // devices + BAND // (2 * devices)
    in_local = samples.shape[0]
    owners = owner_map[:, 0]
    ranks, dead = channel_tables(owners, dropped_channels)
    call = functools.partial(
        spectra_call,
        table=jnp.asarray(folded_table()),
        fir_taps=fir_taps,
        samples=jnp.transpose(samples, (1, 0, 2)),
    )
    middle = capacity * 2 // 3
    me = lax.axis_index("feed")
    widths = [2 * n * in_local // LANES for n in (FIRST, SPEC - FIRST)]

    rows = widths[0] // 8
    block_a, power = call(
        0,
        FIRST,
        [(devices, capacity * widths[0])],
        jnp.where(dead, -1, (owners * capacity + ranks) * rows),
        None,
    )
    received_a = exchange(block_a)
    rows = widths[1] // 8
    head, tail = middle * rows, (capacity - middle) * rows + 1
    row_of = jnp.where(
        ranks < middle,
        devices * tail + (owners ^ me) * head + ranks * rows,
        owners * tail + (ranks - middle) * rows,
    )
    block_c, own, *far = call(
        FIRST,
        SPEC - FIRST,
        [(devices, 8 * tail)] + [(1, 8 * head)] * devices,
        jnp.where(dead, -1, row_of),
        power,
    )
    block_c, received_a = lax.optimization_barrier((block_c, received_a))
    received_c = exchange(block_c)
    received_b = [own] + exchange_pairs(far, 4)

    kept = jnp.sum(jnp.logical_not(dead).astype(jnp.float32))
    mine = (owners == lax.axis_index("feed")) & jnp.logical_not(dead)
    slots = jnp.arange(capacity, dtype=jnp.int32)
    used = jnp.any((ranks[None, :] == slots[:, None]) & mine[None, :], axis=1).astype(jnp.int32)
    mean_power = jnp.sum(received_c[:, -8:]) / (NIN * SPEC * kept)
    factor = jnp.reshape(1.0 / (SPEC * mean_power), (1,))
    everyone = jnp.arange(devices, dtype=jnp.int32)
    run = functools.partial(
        correlate_call,
        widths=widths,
        capacity=capacity,
        used=used,
        factor=factor,
        in_local=in_local,
    )
    vis = run(
        received_a, [received_c], begin=middle, low=middle, high=capacity, index=everyone, before=None
    )
    return run(
        received_a,
        received_b,
        begin=0,
        low=0,
        high=middle,
        index=everyone ^ me,
        before=vis,
    )


def solution(mesh):
    in_local = NIN // mesh.shape["feed"]
    blocks = in_local * 4 == LANES
    return jax.shard_map(
        local_blocks if blocks else local_plain,
        mesh=mesh,
        in_specs=(P("feed", "grp", None), P(), P(), P("grp")),
        out_specs=P(("grp", "feed"), None, None, None),
        check_vma=False,
    )
```

```python
import functools
import math

import jax
import jax.numpy as jnp
import ml_dtypes
import numpy as np
from jax import lax
from jax.experimental import pallas as pl
from jax.experimental.pallas import tpu as pltpu
from jax.sharding import PartitionSpec as P

NIN = 512
NFFT = 8192
HALF = NFFT // 2
BAND = 256
BAND_START = 1536
SPEC = 48
FIRST = 16
KB = 256
LANES = 128
STAGES = 4
MIB = 1 << 20


def dft_table(length, first, width):
    row_ids = lax.broadcasted_iota(jnp.int32, (length, width), 0)
    chan_ids = first + lax.broadcasted_iota(jnp.int32, (length, width), 1)
    phase_int = row_ids * chan_ids % length
    angles = phase_int.astype(jnp.float32) * (2.0 * math.pi / length)
    return jnp.concatenate([jnp.cos(angles), -jnp.sin(angles)], axis=1)


def folded_table():
    n = np.arange(HALF, dtype=np.int64)
    tables = []
    for parity in range(2):
        chans = BAND_START + 2 * np.arange(BAND // 2, dtype=np.int64) + parity
        angles = (n[:, None] * chans[None, :] % NFFT) * (2.0 * math.pi / NFFT)
        full = np.stack([np.cos(angles), -np.sin(angles)]) / math.sqrt(NFFT)
        high = full.astype(np.float32).astype(ml_dtypes.bfloat16)
        low = (full - high.astype(np.float64)).astype(np.float32).astype(ml_dtypes.bfloat16)
        tables.append(np.stack([high, low]))
    return np.stack(tables)


def slot_tables(owner_map, dropped_channels, capacity, slot_total):
    owners = owner_map[:, 0]
    channels = jnp.arange(owners.shape[0], dtype=jnp.int32)
    same_owner = (owners[:, None] == owners[None, :]) & (channels[None, :] < channels[:, None])
    rank_in = jnp.sum(same_owner.astype(jnp.int32), axis=1)
    slot_of = owners * capacity + rank_in
    flagged = jnp.any(dropped_channels[:, None] == channels[None, :], axis=0)
    channel_live = jnp.logical_not(flagged)
    targets = jnp.arange(slot_total, dtype=jnp.int32)
    slot_hit = (slot_of[:, None] == targets[None, :]) & channel_live[:, None]
    chan_of = jnp.sum(slot_hit.astype(jnp.int32) * channels[:, None], axis=0)
    slot_used = jnp.any(slot_hit, axis=0)
    return (chan_of, slot_used, channel_live)


def window(block, fir_taps):
    taps = fir_taps.shape[0]
    spec_count = block.shape[1] - taps + 1
    summed = jnp.zeros((block.shape[0], spec_count, block.shape[2]), jnp.float32)
    for tap_index in range(taps):
        summed = summed + fir_taps[tap_index][None, None, :] * block[
            :, tap_index : tap_index + spec_count, :
        ].astype(jnp.float32)
    return summed


def pair_products(left, right):
    return jnp.einsum(
        "qis,qjs->qij",
        left,
        right,
        precision=lax.Precision.HIGHEST,
        preferred_element_type=jnp.float32,
    )


def correlate(received):
    columns = received[0]
    real_rows = columns[:, :, :SPEC]
    imag_rows = columns[:, :, SPEC:]
    rotated = jnp.concatenate([imag_rows, -real_rows], axis=2)
    real_vis = pair_products(columns, columns)
    imag_vis = pair_products(rotated, columns)
    return jnp.stack([real_vis, imag_vis], axis=1)


def local_plain(samples, fir_taps, owner_map, dropped_channels):
    devices = lax.axis_size("feed")
    capacity = BAND // devices + BAND // (2 * devices)
    slot_total = devices * capacity
    in_local = samples.shape[0]
    dft_scale = 1.0 / math.sqrt(NFFT)
    chan_of, slot_used, channel_live = slot_tables(
        owner_map, dropped_channels, capacity, slot_total
    )
    live_mask = channel_live.astype(jnp.float32)
    kept = jnp.sum(live_mask)
    windowed = window(samples, fir_taps).reshape(in_local * SPEC, NFFT)
    table = dft_table(NFFT, BAND_START, BAND)
    spectra = (
        jnp.dot(
            windowed, table, precision=lax.Precision.HIGHEST, preferred_element_type=jnp.float32
        )
        * dft_scale
    )
    spectra = spectra.reshape(in_local, SPEC, 2, BAND)
    chosen = jnp.take(spectra, chan_of, axis=3) * slot_used.astype(jnp.float32)[None, None, None, :]
    outgoing = jnp.transpose(chosen, (3, 0, 2, 1)).reshape(devices, capacity, in_local, 2 * SPEC)
    raw_vis = correlate(lax.all_to_all(outgoing, "feed", split_axis=0, concat_axis=2, tiled=True))
    local_power = jnp.sum(jnp.trace(raw_vis[:, 0], axis1=1, axis2=2))
    power = lax.psum(local_power, "feed")
    mean_power = power / (NIN * SPEC * kept)
    factor = 1.0 / (SPEC * mean_power)
    return (raw_vis * factor).astype(jnp.bfloat16)


def weighted(coefs, values):
    terms = [c * v for c, v in zip(coefs, values)]
    while len(terms) > 1:
        terms = [sum(terms[k + 1 : k + 2], terms[k]) for k in range(0, len(terms), 2)]
    return terms[0]


def split(value):
    high = value.astype(jnp.bfloat16)
    return high, (value - high.astype(jnp.float32)).astype(jnp.bfloat16)


def spectra_kernel(count, last, devices, message, blocks, taps, in_local, *refs):
    row_ref, taps_a, taps_b, frames_a, frames_b, table_a, table_b, table_last = refs[:8]
    refs = refs[8:]
    if last:
        before, refs = refs[0], refs[1:]
    outs, refs = refs[:blocks], refs[blocks:]
    if not last:
        power_out, refs = refs[0], refs[1:]
    even_0, odd_0, even_1, odd_1, acc, flat, staged, sems = refs
    step = pl.program_id(0)
    rows = count * in_local

    def window_piece(block, tile, begin, even, odd):
        lanes = slice(block * KB + tile * LANES, block * KB + (tile + 1) * LANES)
        coef_a = [jnp.broadcast_to(taps_a[t : t + 1, lanes], (16, LANES)) for t in range(taps)]
        coef_b = [jnp.broadcast_to(taps_b[t : t + 1, lanes], (16, LANES)) for t in range(taps)]
        for first in range(0, in_local, 16):

            def load(ref, f):
                return ref[f, first : first + 16, lanes].astype(jnp.float32)

            held_a = [load(frames_a, begin + f) for f in range(taps - 1)]
            held_b = [load(frames_b, begin + f) for f in range(taps - 1)]
            for s in range(begin, begin + 8):
                held_a.append(load(frames_a, s + taps - 1))
                held_b.append(load(frames_b, s + taps - 1))
                near = weighted(coef_a, held_a)
                far = weighted(coef_b, held_b)
                at = slice(s * in_local + first, s * in_local + first + 16)
                for ref, value in ((even, near + far), (odd, near - far)):
                    ref[0, tile, at, :], ref[1, tile, at, :] = split(value)
                held_a, held_b = held_a[1:], held_b[1:]

    def matmul_piece(table, parity, start, ref):
        cols = slice(parity * BAND, (parity + 1) * BAND)
        at = slice(start, start + 512)
        tall = [
            jnp.concatenate([table[parity, part, 0], table[parity, part, 1]], axis=1)
            for part in range(2)
        ]
        right = jnp.concatenate([tall[0], tall[0], tall[1]], axis=0)
        wide = [ref[part, tile, at, :] for part in (0, 1, 0) for tile in range(KB // LANES)]
        left = jnp.concatenate(wide, axis=1)
        acc[at, cols] += jnp.dot(left, right, preferred_element_type=jnp.float32)

    def matmul_pieces(table, even, odd):
        return [
            functools.partial(matmul_piece, table, parity, start, ref)
            for parity, ref in enumerate((even, odd))
            for start in range(0, rows, 512)
        ]

    def window_pieces(block, even, odd):
        return [
            functools.partial(window_piece, block, tile, begin, even, odd)
            for tile in range(KB // LANES)
            for begin in range(0, count, 8)
        ]

    def alternate(left, right):
        share = len(right) // len(left)
        for k, piece in enumerate(left):
            piece()
            for other in right[k * share : (k + 1) * share]:
                other()

    @pl.when(step == 0)
    def _():
        even_1[...] = jnp.zeros_like(even_1)
        odd_1[...] = jnp.zeros_like(odd_1)
        acc[...] = jnp.zeros_like(acc)

    alternate(matmul_pieces(table_b, even_1, odd_1), window_pieces(0, even_0, odd_0))
    alternate(matmul_pieces(table_a, even_0, odd_0), window_pieces(1, even_1, odd_1))

    @pl.when(step == pl.num_programs(0) - 1)
    def _():
        for piece in matmul_pieces(table_last, even_1, odd_1):
            piece()
        width = rows // LANES
        for parity in range(2):
            for part in range(2):
                cols = slice(parity * BAND + part * LANES, parity * BAND + (part + 1) * LANES)
                for g in range(width):
                    turned = acc[g * LANES : (g + 1) * LANES, cols].T
                    row = (parity * 2 + part) * width + g
                    flat[pl.ds(row, LANES, stride=4 * width), :] = turned
        size = 2 * width

        def place(c, total):
            value = flat[pl.ds(pl.multiple_of(c * size, size), size), :]
            row = row_ref[c]

            @pl.when(row >= 0)
            def _():
                staged[pl.ds(pl.multiple_of(row * 8, 8), size), :] = value

            square = value[:8] * value[:8]
            for start in range(8, size, 8):
                square += value[start : start + 8] * value[start : start + 8]
            return total + (row >= 0).astype(jnp.float32) * square

        total = lax.fori_loop(0, BAND, place, jnp.zeros((8, LANES), jnp.float32), unroll=8)
        if last:
            total = total + before[...]
            for d in range(devices):
                staged[(d + 1) * message - 8 : (d + 1) * message, :] = total
        else:
            power_out[...] = total
        copies, row = [], 0
        for k, out in enumerate(outs):
            count_rows = out.shape[0]
            copies.append(
                pltpu.make_async_copy(staged.at[pl.ds(row, count_rows)], out, sems.at[k])
            )
            row += count_rows
        for copy in copies:
            copy.start()
        for copy in copies:
            copy.wait()


def spectra_call(first, count, sizes, row_of, before, table, fir_taps, samples):
    _, in_local, _ = samples.shape
    taps = fir_taps.shape[0]
    step_size = 2 * KB
    steps = HALF // step_size
    last = before is not None
    rows = count * in_local
    width = 2 * rows // LANES
    total_rows = sum(n * r for n, r in sizes)
    message = sizes[0][1]
    devices = sum(n for n, r in sizes if r == message)

    def frames_spec(offset):
        return pl.BlockSpec(
            (pl.Element(count + taps - 1), pl.Element(in_local), pl.Element(step_size)),
            lambda j, *_: (first, 0, pl.multiple_of((j + offset) * step_size, step_size)),
        )

    def taps_spec(offset):
        return pl.BlockSpec((taps, step_size), lambda j, *_: (0, j + offset))

    def table_spec(index):
        return pl.BlockSpec((2, 2, 2, KB, LANES), lambda j, *_: (0, 0, 0, index(j), 0))

    blocks = [jax.ShapeDtypeStruct((n * r, LANES), jnp.float32) for n, r in sizes]
    power = jax.ShapeDtypeStruct((8, LANES), jnp.float32)
    whole = [pl.BlockSpec(memory_space=pl.ANY)] * len(sizes)
    single = [pl.BlockSpec(power.shape, lambda j, *_: (0, 0))]
    grid_spec = pltpu.PrefetchScalarGridSpec(
        num_scalar_prefetch=1,
        grid=(steps,),
        in_specs=[
            taps_spec(0),
            taps_spec(steps),
            frames_spec(0),
            frames_spec(steps),
            table_spec(lambda j: 2 * j),
            table_spec(lambda j: jnp.maximum(2 * j - 1, 0)),
            table_spec(lambda j: 2 * steps - 1),
        ]
        + (single if last else []),
        out_specs=whole + ([] if last else single),
        scratch_shapes=[pltpu.VMEM((2, KB // LANES, rows, LANES), jnp.bfloat16)] * 4
        + [
            pltpu.VMEM((rows, 2 * BAND), jnp.float32),
            pltpu.VMEM((BAND * width, LANES), jnp.float32),
            pltpu.VMEM((total_rows, LANES), jnp.float32),
            pltpu.SemaphoreType.DMA((len(sizes),)),
        ],
    )
    results = pl.pallas_call(
        functools.partial(spectra_kernel, count, last, devices, message, len(sizes), taps, in_local),
        out_shape=blocks + ([] if last else [power]),
        grid_spec=grid_spec,
        compiler_params=pltpu.CompilerParams(vmem_limit_bytes=60 * MIB),
        cost_estimate=pl.CostEstimate(
            flops=3 * 2 * rows * HALF * 2 * BAND, bytes_accessed=30 * MIB, transcendentals=0
        ),
        name="spectra",
    )(
        row_of,
        fir_taps,
        fir_taps,
        samples,
        samples,
        table,
        table,
        table,
        *([before] if last else []),
    )
    sent = [r.reshape(*size, LANES) for r, size in zip(results, sizes)]
    return sent + list(results[len(sizes) :])


def exchange_lanes(values, in_local):
    count = len(values)
    lane = lax.broadcasted_iota(jnp.int32, values[0].shape, 1) // in_local
    values = list(values)
    distance = count // 2
    while distance:
        upper = (lane & distance) != 0
        shift = distance * in_local
        for a in range(count):
            if a & distance:
                continue
            x, y = values[a], values[a + distance]
            values[a] = jnp.where(upper, pltpu.roll(y, shift, 1), x)
            values[a + distance] = jnp.where(upper, y, pltpu.roll(x, LANES - shift, 1))
        distance //= 2
    return values


def correlate_kernel(widths, low, count, distant, in_local, factor_ref, used_ref, index_ref, *refs):
    near_a, near_b, *far_b = refs[: 2 + distant]
    out, left_0, right_0, left_1, right_1, second, staged, sems = refs[-8:]
    step, last = pl.program_id(0), count // 2 - 1
    per_tile = LANES // in_local
    blocks = near_a.shape[0] // per_tile
    nin = near_a.shape[0] * in_local
    factor = factor_ref[0]
    upper = lax.broadcasted_iota(jnp.int32, (8, LANES), 0) >= 4

    def prepare(slot, left, right, block):
        used = used_ref[2 * step + slot] != 0
        straight, turned = [], []
        for group, (ref, width) in enumerate(zip((near_a, second), widths)):
            tiles = []
            for start in range(slot * width, (slot + 1) * width, 8):
                mixed = []
                for source in range(block * per_tile, (block + 1) * per_tile):
                    at = index_ref[source] if group else source
                    mixed.append(jnp.where(used, ref[at, start : start + 8], 0.0))
                tiles.append(exchange_lanes(mixed, in_local))
            for q in range(per_tile):
                column = [t[q] for t in tiles]
                straight += column
                if len(column) == 1:
                    swapped = pltpu.roll(column[0], 4, 0)
                    turned.append(jnp.where(upper, swapped, -swapped))
                else:
                    half = len(column) // 2
                    turned += [-t for t in column[half:]] + column[:half]
        pad = [jnp.zeros((LANES - 8 * len(straight), LANES), jnp.float32)]
        columns = jnp.concatenate(straight + pad, axis=0)
        for part, value in enumerate((columns, jnp.concatenate(turned + pad, axis=0))):
            right[0, part * blocks + block], right[1, part * blocks + block] = split(value)
        at = slice(block * LANES, (block + 1) * LANES)
        left[0, at, :], left[1, at, :] = split(columns.T)

    def multiply(index, left, right, part):
        wide = [
            jnp.concatenate([right[k, part * blocks + b] for b in range(blocks)], axis=1)
            for k in range(2)
        ]
        total = jnp.dot(
            jnp.concatenate([left[0], left[1], left[0]], axis=1),
            jnp.concatenate([wide[0], wide[0], wide[1]], axis=0),
            preferred_element_type=jnp.float32,
        )
        staged[lax.rem(index + STAGES, STAGES), part] = (total * factor).astype(jnp.bfloat16)

    def copies(index):
        buffer = lax.rem(index, STAGES)
        return [
            pltpu.make_async_copy(
                staged.at[buffer, part, pl.ds(half * nin // 2, nin // 2)],
                out.at[low + index, part, pl.ds(half * nin // 2, nin // 2)],
                sems.at[buffer, 2 * part + half],
            )
            for part in range(2)
            for half in range(2)
        ]

    def start(index):
        for copy in copies(index):
            copy.start()

    def wait(index):
        for copy in copies(index):
            copy.wait()

    odd, even = 2 * step - 1, 2 * step
    second[: near_b.shape[0]] = near_b[...]
    for k, ref in enumerate(far_b):
        second[near_b.shape[0] + k] = ref[0]

    @pl.when(odd >= STAGES)
    def _():
        wait(odd - STAGES)

    for part in range(2):
        multiply(odd, left_1, right_1, part)
        for block in range(part * blocks // 2, (part + 1) * blocks // 2):
            prepare(0, left_0, right_0, block)

    @pl.when(step >= 1)
    def _():
        start(odd)

    @pl.when(even >= STAGES)
    def _():
        wait(even - STAGES)

    for part in range(2):
        multiply(even, left_0, right_0, part)
        for block in range(part * blocks // 2, (part + 1) * blocks // 2):
            prepare(1, left_1, right_1, block)

    start(even)

    @pl.when(step == last)
    def _():
        if count > STAGES:
            wait(jnp.int32(count - 1 - STAGES))
        for part in range(2):
            multiply(even + 1, left_1, right_1, part)
        start(even + 1)
        for index in range(count - min(STAGES, count), count):
            wait(jnp.int32(index))


def correlate_call(
    first, rest, begin, widths, low, high, capacity, used, factor, index, before, in_local
):
    sources = first.shape[0]
    nin = sources * in_local
    count = high - low

    def spec(block, width, start):
        return pl.BlockSpec(
            (block.shape[0], 2 * width, LANES), lambda s: (0, s + (low - start) // 2, 0)
        )

    in_specs = [pl.BlockSpec(memory_space=pltpu.SMEM)] * 3 + [spec(first, widths[0], 0)]
    in_specs += [spec(block, widths[1], begin) for block in rest]
    arrays = [first] + rest
    aliases = {}
    if before is not None:
        in_specs.append(pl.BlockSpec(memory_space=pl.ANY))
        aliases = {3 + len(arrays): 0}
        arrays.append(before)
    return pl.pallas_call(
        functools.partial(correlate_kernel, widths, low, count, len(rest) - 1, in_local),
        out_shape=jax.ShapeDtypeStruct((capacity, 2, nin, nin), jnp.bfloat16),
        grid=(count // 2,),
        in_specs=in_specs,
        out_specs=pl.BlockSpec(memory_space=pl.ANY),
        input_output_aliases=aliases,
        scratch_shapes=[
            pltpu.VMEM((2, nin, LANES), jnp.bfloat16),
            pltpu.VMEM((2, 2 * nin // LANES, LANES, LANES), jnp.bfloat16),
        ]
        * 2
        + [
            pltpu.VMEM((sources, 2 * widths[1], LANES), jnp.float32),
            pltpu.VMEM((STAGES, 2, nin, nin), jnp.bfloat16),
            pltpu.SemaphoreType.DMA((STAGES, 4)),
        ],
        compiler_params=pltpu.CompilerParams(vmem_limit_bytes=60 * MIB),
        cost_estimate=pl.CostEstimate(
            flops=count * 8 * nin * nin * 256,
            bytes_accessed=count * (4 * nin * nin + 8 * nin * SPEC),
            transcendentals=0,
        ),
        name="correlate",
    )(factor, used[low:high], index, *arrays)


def exchange(block):
    return lax.all_to_all(block, "feed", split_axis=0, concat_axis=0, tiled=True)


def exchange_pairs(far, flight, ahead):
    devices = len(far) + 1
    half = devices // 2
    order = []
    for k in range(half):
        order += [half + k] + ([k] if k else [])
    arrived = [None] * len(far)
    for k, d in enumerate(order):
        block = far[d - 1]
        if k >= flight:
            e = order[k - flight] - 1
            block, arrived[e] = lax.optimization_barrier((block, arrived[e]))
        if d == order[-1]:
            block, ahead = lax.optimization_barrier((block, ahead))
        arrived[d - 1] = lax.ppermute(block, "feed", [(i, i ^ d) for i in range(devices)])
    return arrived, ahead


def channel_tables(owners, dropped_channels):
    channels = jnp.arange(BAND, dtype=jnp.int32)[:, None]
    names = jnp.concatenate([owners, dropped_channels])[None, :]
    entry = jnp.arange(names.shape[1], dtype=jnp.int32)[None, :]
    earlier = (entry < channels) & (names == owners[:, None])
    flagged = (entry >= BAND) & (names == channels)
    total = jnp.sum(jnp.where(flagged, BAND, earlier.astype(jnp.int32)), axis=1)
    return total % BAND, total >= BAND


def local_blocks(samples, fir_taps, owner_map, dropped_channels):
    devices = lax.axis_size("feed")
    capacity = BAND // devices + BAND // (2 * devices)
    in_local = samples.shape[0]
    owners = owner_map[:, 0]
    ranks, dead = channel_tables(owners, dropped_channels)
    call = functools.partial(
        spectra_call,
        table=jnp.asarray(folded_table()),
        fir_taps=fir_taps,
        samples=jnp.transpose(samples, (1, 0, 2)),
    )
    middle = capacity * 2 // 3
    me = lax.axis_index("feed")
    widths = [2 * n * in_local // LANES for n in (FIRST, SPEC - FIRST)]

    rows = widths[0] // 8
    block_a, power = call(
        0,
        FIRST,
        [(devices, capacity * widths[0])],
        jnp.where(dead, -1, (owners * capacity + ranks) * rows),
        None,
    )
    received_a = exchange(block_a)
    rows = widths[1] // 8
    head, tail = middle * rows, (capacity - middle) * rows + 1
    row_of = jnp.where(
        ranks < middle,
        devices * tail + (owners ^ me) * head + ranks * rows,
        owners * tail + (ranks - middle) * rows,
    )
    block_c, own, *far = call(
        FIRST,
        SPEC - FIRST,
        [(devices, 8 * tail)] + [(1, 8 * head)] * devices,
        jnp.where(dead, -1, row_of),
        power,
    )
    block_c, received_a = lax.optimization_barrier((block_c, received_a))
    received_c = exchange(block_c)
    kept = jnp.sum(jnp.logical_not(dead).astype(jnp.float32))
    mine = (owners == lax.axis_index("feed")) & jnp.logical_not(dead)
    slots = jnp.arange(capacity, dtype=jnp.int32)
    used = jnp.any((ranks[None, :] == slots[:, None]) & mine[None, :], axis=1).astype(jnp.int32)
    mean_power = jnp.sum(received_c[:, -8:]) / (NIN * SPEC * kept)
    factor = jnp.reshape(1.0 / (SPEC * mean_power), (1,))
    everyone = jnp.arange(devices, dtype=jnp.int32)
    run = functools.partial(
        correlate_call,
        widths=widths,
        capacity=capacity,
        used=used,
        factor=factor,
        in_local=in_local,
    )
    vis = run(
        received_a, [received_c], begin=middle, low=middle, high=capacity, index=everyone, before=None
    )
    arrived, vis = exchange_pairs(far, 4, vis)
    return run(
        received_a,
        [own] + arrived,
        begin=0,
        low=0,
        high=middle,
        index=everyone ^ me,
        before=vis,
    )


def solution(mesh):
    in_local = NIN // mesh.shape["feed"]
    blocks = in_local * 4 == LANES
    return jax.shard_map(
        local_blocks if blocks else local_plain,
        mesh=mesh,
        in_specs=(P("feed", "grp", None), P(), P(), P("grp")),
        out_specs=P(("grp", "feed"), None, None, None),
        check_vma=False,
    )
```
